32 devices in a mesh: section: 4 (over y, x), dp: 8 (over z, core).
Axes of the slice: x: 2, y: 2, z: 4, core: 2. Of those that a mesh axis runs over, the one named last changes fastest.
Arguments:
- latent_in: bfloat16 [4096, 512], P('dp'), may hold values from 0 to 0.25
- actions: bfloat16 [4, 4096, 64], P('section', 'dp'), may hold values from -1 to 1
- task_ids: int32 [4096], P('dp'), may hold values from 0 to 79
- valid: int32 [4096], P('dp'), may hold values from 0 to 1, as said below
- action_mask: int32 [80, 64], replicated, may hold values from 0 to 1, as said below
- bins: int32 [4, 4096], P('section', 'dp'), may hold values from 0 to 99
- fraction: float32 [4, 4096], P('section', 'dp'), may hold values from 0 to 1
- latent_cot: bfloat16 [4, 4096, 512], P('section', 'dp'), may hold values from -24 to 24
- w_in: bfloat16 [4, 6, 672, 1024], P('section'), may hold values from -0.25 to 0.25
- b_in: bfloat16 [4, 6, 1024], P('section'), may hold values from -1.5 to 1.5
- g_in: bfloat16 [4, 6, 1024], P('section'), may hold values from 0.5 to 1.5
- beta_in: bfloat16 [4, 6, 1024], P('section'), may hold values from -1.5 to 1.5
- w_mid: bfloat16 [4, 6, 1024, 1024], P('section'), may hold values from -0.1875 to 0.1875
- b_mid: bfloat16 [4, 6, 1024], P('section'), may hold values from -1.5 to 1.5
- g_mid: bfloat16 [4, 6, 1024], P('section'), may hold values from 0.5 to 1.5
- beta_mid: bfloat16 [4, 6, 1024], P('section'), may hold values from -1.5 to 1.5
- w_dyn_out: bfloat16 [4, 1024, 512], P('section'), may hold values from -0.75 to 0.75
- b_dyn_out: bfloat16 [4, 512], P('section'), may hold values from -2.5 to 2.5
- g_dyn_out: bfloat16 [4, 512], P('section'), may hold values from 0.5 to 1.5
- beta_dyn_out: bfloat16 [4, 512], P('section'), may hold values from -2.5 to 2.5
- w_q_out: bfloat16 [4, 5, 1024, 101], P('section'), may hold values from -0.375 to 0.375
- b_q_out: bfloat16 [4, 5, 101], P('section'), may hold values from -2.5 to 2.5
- table: bfloat16 [80, 96], replicated, may hold values from -5 to 5
Outputs:
- latents_out: bfloat16 [4, 4096, 512], P('section', 'dp')
- grad_latents: float32 [4, 4096, 512], P('section', 'dp')
- grad_w_in: float32 [4, 6, 672, 1024], P('section', None, None, 'dp')
- grad_b_in: float32 [4, 6, 1024], P('section', None, 'dp')
- grad_g_in: float32 [4, 6, 1024], P('section', None, 'dp')
- grad_beta_in: float32 [4, 6, 1024], P('section', None, 'dp')
- grad_w_mid: float32 [4, 6, 1024, 1024], P('section', None, None, 'dp')
- grad_b_mid: float32 [4, 6, 1024], P('section', None, 'dp')
- grad_g_mid: float32 [4, 6, 1024], P('section', None, 'dp')
- grad_beta_mid: float32 [4, 6, 1024], P('section', None, 'dp')
- grad_w_dyn_out: float32 [4, 1024, 512], P('section', 'dp')
- grad_b_dyn_out: float32 [4, 512], P('section')
- grad_g_dyn_out: float32 [4, 512], P('section')
- grad_beta_dyn_out: float32 [4, 512], P('section')
- grad_w_q_out: float32 [4, 5, 1024, 101], P('section', None, 'dp')
- grad_b_q_out: float32 [4, 5, 101], P('section')
- grad_table: float32 [80, 96], replicated
- rms_stats: float32 [4, 2], P('section')
The draws below stay inside these ranges and needn't reach their ends.
Inputs may be any that keep to these rules, and one draw needn't show every extreme that they name: `valid`: every aligned block of 512 rows holds a 1. `action_mask`: row t is 1 on its first k_t entries and 0 after them, k_t from 16 to 61, both reached.
All inputs are finite; a program needn't handle non-finite values.
Results may differ from the reference program's by a relative error of at most 0.012.
Values may be sent and summed in bfloat16 or wider, within the bound.
A program may use at most 576 MiB of HBM per device.

```python
import math
import jax
import jax.numpy as jnp
import numpy as np
from jax import lax

LAT = 512
ACT = 64
EMB = 96
HID = 1024
HEADS = 5
BINS = 101
GROUP = 8
TASKS = 80
ROWS = 512
LAYERS = 4
TOKENS = 4096


def draw_valid(key, part):
    key = jax.random.fold_in(key, 11)
    places = jnp.arange(TOKENS, dtype=jnp.int32)
    rolls = jax.random.randint(key, (TOKENS,), 0, 1000)
    limit = 300 + 600 * places // TOKENS
    chosen = (rolls < limit) | (places % ROWS == 0)
    return chosen.astype(jnp.int32)


def draw_action_mask(key, part):
    key = jax.random.fold_in(key, 23)
    lowest = ACT // 4
    highest = ACT - 3
    reach = jax.random.randint(key, (TASKS,), lowest, highest + 1)
    task_lanes = jnp.arange(TASKS, dtype=jnp.int32)
    reach = jnp.where(task_lanes == 0, highest, jnp.where(task_lanes == 1, lowest, reach))
    act_lanes = jnp.arange(ACT, dtype=jnp.int32)[None, :]
    return (act_lanes < reach[:, None]).astype(jnp.int32)


def draw_latent_cot(key, part):
    key = jax.random.fold_in(key, 31)
    entry_key = jax.random.fold_in(key, 0)
    places = jnp.arange(TOKENS, dtype=jnp.float32) / TOKENS
    trend = jnp.exp(jnp.log(4.0) * places)[None, :, None]
    entries = jnp.clip(jax.random.normal(entry_key, (LAYERS, TOKENS, LAT), jnp.float32), -6.0, 6.0)
    return (entries * trend).astype(jnp.bfloat16)


def with_ends(array, own_key, least, top_value):
    longest = array.shape.index(max(array.shape))
    spots = []
    for shift in (0, 1):
        where = [jax.random.randint(jax.random.fold_in(own_key, axis), (), 0, length) for axis, length in enumerate(array.shape)]
        where[longest] = (where[longest] + shift) % array.shape[longest]
        spots.append(tuple(where))
    return array.at[spots[0]].set(least).at[spots[1]].set(top_value)


def shard_levels(rng, extent, cuts, smallest, top_value):
    gain = 1.0
    for position, shards_of in cuts:
        heights = jax.random.uniform(jax.random.fold_in(jax.random.fold_in(rng, 6), position), (shards_of,), jnp.float32, smallest / len(cuts), top_value / len(cuts))
        gain = gain * jnp.repeat(jnp.exp(heights), extent[position] // shards_of).reshape((-1,) + (1,) * (len(extent) - 1 - position))
    return gain


def rank_bounds(count, lean):
    weights = [(1 << 20) // math.isqrt(standing ** lean) + 1 for standing in range(1, count + 1)]
    width = 1 + sum(weights) // (1 << 30)
    return np.cumsum(np.array([max(1, weight // width) for weight in weights]))


def ranked(own_key, dims, number_of, skew):
    listing = rank_bounds(number_of, skew)
    pick = jax.random.randint(jax.random.fold_in(own_key, 1), dims, 0, int(listing[number_of - 1]))
    grade = jnp.searchsorted(jnp.asarray(listing, jnp.int32), pick, side="right")
    return jax.random.permutation(jax.random.fold_in(own_key, 2), number_of)[grade].astype(jnp.int32)


def bell_draw(stream_key, dims, width, bound, cuts=(), kind=jnp.bfloat16):
    loudness = shard_levels(stream_key, dims, cuts, -0.22, 0.18) if cuts else 1.0
    values = jax.random.normal(stream_key, dims, jnp.float32) * width * loudness
    return jnp.minimum(jnp.maximum(values, -bound), bound).astype(kind)


def setup_inputs(seed: int = 0) -> dict:
    key_list = jax.random.split(jax.random.key(seed), 24)
    return {
        "latent_in": jnp.clip(0.25 * jax.random.uniform(key_list[0], (TOKENS, LAT), jnp.float32) ** shard_levels(key_list[0], (TOKENS, LAT), ((0, 8),), -0.2, 0.2), 0.0, 0.25).astype(jnp.bfloat16),
        "actions": jnp.clip(jax.random.uniform(key_list[1], (LAYERS, TOKENS, ACT), jnp.float32, -1.0, 1.0) * shard_levels(key_list[1], (LAYERS, TOKENS, ACT), ((0, 4), (1, 8)), -0.4, 0.0), -1.0, 1.0).astype(jnp.bfloat16),
        "task_ids": with_ends(ranked(key_list[2], (TOKENS,), TASKS, 2), jax.random.fold_in(key_list[2], 3), 0, TASKS - 1).astype(jnp.int32),
        "valid": draw_valid(jax.random.fold_in(key_list[23], 71), 0),
        "action_mask": draw_action_mask(jax.random.fold_in(key_list[23], 71), 0),
        "bins": with_ends(jax.random.randint(key_list[5], (LAYERS, TOKENS), 0, BINS - 1), jax.random.fold_in(key_list[5], 1), 0, (BINS - 1) - 1).astype(jnp.int32),
        "fraction": jnp.clip(1.0 * jax.random.uniform(key_list[6], (LAYERS, TOKENS), jnp.float32) ** shard_levels(key_list[6], (LAYERS, TOKENS), ((0, 4), (1, 8)), -0.2, 0.2), 0.0, 1.0),
        "latent_cot": draw_latent_cot(jax.random.fold_in(key_list[23], 71), 0),
        "w_in": bell_draw(key_list[8], (LAYERS, HEADS + 1, LAT + ACT + EMB, HID), (LAT + ACT + EMB) ** -0.5, 0.25, ((0, 4),)),
        "b_in": bell_draw(key_list[9], (LAYERS, HEADS + 1, HID), 0.3, 1.5, ((0, 4),)),
        "g_in": jnp.clip(1.0 + 0.1 * jax.random.normal(key_list[10], (LAYERS, HEADS + 1, HID), jnp.float32), 0.5, 1.5).astype(jnp.bfloat16),
        "beta_in": bell_draw(key_list[11], (LAYERS, HEADS + 1, HID), 0.3, 1.5, ((0, 4),)),
        "w_mid": bell_draw(key_list[12], (LAYERS, HEADS + 1, HID, HID), HID ** -0.5, 0.1875, ((0, 4),)),
        "b_mid": bell_draw(key_list[13], (LAYERS, HEADS + 1, HID), 0.3, 1.5, ((0, 4),)),
        "g_mid": jnp.clip(1.0 + 0.1 * jax.random.normal(key_list[14], (LAYERS, HEADS + 1, HID), jnp.float32), 0.5, 1.5).astype(jnp.bfloat16),
        "beta_mid": bell_draw(key_list[15], (LAYERS, HEADS + 1, HID), 0.3, 1.5, ((0, 4),)),
        "w_dyn_out": bell_draw(key_list[16], (LAYERS, HID, LAT), 64 ** -0.5, 0.75, ((0, 4),)),
        "b_dyn_out": bell_draw(key_list[17], (LAYERS, LAT), 0.5, 2.5, ((0, 4),)),
        "g_dyn_out": jnp.clip(1.0 + 0.1 * jax.random.normal(key_list[18], (LAYERS, LAT), jnp.float32), 0.5, 1.5).astype(jnp.bfloat16),
        "beta_dyn_out": bell_draw(key_list[19], (LAYERS, LAT), 0.5, 2.5, ((0, 4),)),
        "w_q_out": bell_draw(key_list[20], (LAYERS, HEADS, HID, BINS), 256 ** -0.5, 0.375, ((0, 4),)),
        "b_q_out": bell_draw(key_list[21], (LAYERS, HEADS, BINS), 0.5, 2.5, ((0, 4),)),
        "table": bell_draw(key_list[22], (TASKS, EMB), 1.0, 5.0),
    }


EPS = 1e-05
HIGH_PRECISION = lax.Precision.HIGHEST

@jax.custom_vjp
def low(v):
    return lax.optimization_barrier(v.astype(jnp.bfloat16)).astype(jnp.float32)

@jax.custom_vjp
def low_back(v):
    return v

def low_keep(v):
    return (low(v), None)

def low_pass(kept, grad):
    return (grad,)

def back_keep(v):
    return (v, None)

def back_low(kept, grad):
    return (low(grad),)
low.defvjp(low_keep, low_pass)
low_back.defvjp(back_keep, back_low)

def mish(values):
    return values * jnp.tanh(jax.nn.softplus(values))

def normed(values, gain_vec, shift_vec):
    center = values - lax.optimization_barrier(jnp.mean(values, -1, keepdims=True))
    spread = lax.optimization_barrier(jnp.mean(center * center, -1, keepdims=True))
    return mish(center * lax.rsqrt(spread + EPS) * gain_vec[:, None, :] + shift_vec[:, None, :])

def simplex_norm(values, gain_vec, shift_vec):
    center = values - lax.optimization_barrier(jnp.mean(values, -1, keepdims=True))
    spread = lax.optimization_barrier(jnp.mean(center * center, -1, keepdims=True))
    scaled = center * lax.rsqrt(spread + EPS) * gain_vec + shift_vec
    row_total = values.shape[0]
    return jax.nn.softmax(scaled.reshape(row_total, -1, GROUP), -1).reshape(row_total, -1)

def section_forward(params, latent, side, valid_rows, bin_rows, frac_rows):
    w_in, b_in, g_in, beta_in, w_mid, b_mid, g_mid, beta_mid, w_dyn, b_dyn, g_dyn, beta_dyn, critic_weight, critic_bias = params
    inputs = low(jnp.concatenate([latent, side], 1))
    first_pre = low_back(jnp.einsum('ri,hij->hrj', inputs, w_in, precision=HIGH_PRECISION) + b_in[:, None, :])
    first_act = low(normed(first_pre, g_in, beta_in))
    second_pre = low_back(jnp.einsum('hri,hij->hrj', first_act, w_mid, precision=HIGH_PRECISION) + b_mid[:, None, :])
    second_activation = low(normed(second_pre, g_mid, beta_mid))
    dyn_pre = low_back(jnp.dot(second_activation[0], w_dyn, precision=HIGH_PRECISION) + b_dyn)
    new_latent = simplex_norm(dyn_pre, g_dyn, beta_dyn)
    critic_logits = low_back(jnp.einsum('tcy,tyo->tco', second_activation[1:], critic_weight, precision=HIGH_PRECISION) + critic_bias[:, None, :])
    log_prob = jax.nn.log_softmax(critic_logits, -1)
    bin_lanes = jnp.arange(BINS, dtype=jnp.int32)[None, :]
    target = (1.0 - frac_rows)[:, None] * (bin_lanes == bin_rows[:, None]).astype(jnp.float32)
    target = target + frac_rows[:, None] * (bin_lanes == bin_rows[:, None] + 1).astype(jnp.float32)
    cross_loss = -jnp.sum(valid_rows[None, :, None] * target[None] * log_prob)
    return (new_latent, second_activation[0], cross_loss)

def reference(latent_in, actions, task_ids, valid, action_mask, bins, fraction, latent_cot, w_in, b_in, g_in, beta_in, w_mid, b_mid, g_mid, beta_mid, w_dyn_out, b_dyn_out, g_dyn_out, beta_dyn_out, w_q_out, b_q_out, table):
    weights = tuple((source.astype(jnp.float32) for source in (w_in, b_in, g_in, beta_in, w_mid, b_mid, g_mid, beta_mid, w_dyn_out, b_dyn_out, g_dyn_out, beta_dyn_out, w_q_out, b_q_out)))
    table_full = table.astype(jnp.float32)
    latent_full = latent_in.astype(jnp.float32)
    acts_full = actions.astype(jnp.float32)
    cot_full = latent_cot.astype(jnp.float32)
    valid_full = valid.astype(jnp.float32)
    mask_full = action_mask.astype(jnp.float32)
    block_count = TOKENS // ROWS

    def per_block(running, block_index):
        first_row = block_index * ROWS
        task_rows = lax.dynamic_slice_in_dim(task_ids, first_row, ROWS, 0)
        lat_rows = lax.dynamic_slice_in_dim(latent_full, first_row, ROWS, 0)
        act_rows = lax.dynamic_slice_in_dim(acts_full, first_row, ROWS, 1)
        cot_rows = lax.dynamic_slice_in_dim(cot_full, first_row, ROWS, 1)
        valid_rows = lax.dynamic_slice_in_dim(valid_full, first_row, ROWS, 0)
        bin_rows = lax.dynamic_slice_in_dim(bins, first_row, ROWS, 1)
        frac_rows = lax.dynamic_slice_in_dim(fraction, first_row, ROWS, 1)
        mask_rows = jnp.take(mask_full, task_rows, axis=0)

        def loss_fn(params, table_param, shifts):
            embedded = jnp.take(table_param, task_rows, axis=0)
            latent = lat_rows + shifts[0]
            loss_total = jnp.zeros((), jnp.float32)
            latent_rows = []
            stat_rows = []
            for layer_index in range(LAYERS):
                side = jnp.concatenate([act_rows[layer_index] * mask_rows, embedded], 1)
                own = tuple((param[layer_index] for param in params))
                new_latent, hidden, cross_loss = section_forward(own, latent, side, valid_rows, bin_rows[layer_index], frac_rows[layer_index])
                sent_latent = low(new_latent)
                loss_total = loss_total + cross_loss + jnp.sum(sent_latent * cot_rows[layer_index])
                latent_rows.append(sent_latent)
                stat_rows.append(jnp.stack([jnp.sum(valid_rows), jnp.sum(valid_rows * lax.optimization_barrier(jnp.sum(sent_latent * sent_latent, 1)))]))
                if layer_index + 1 < LAYERS:
                    latent = low_back(sent_latent) + shifts[layer_index + 1]
            return (loss_total, (jnp.stack(latent_rows), jnp.stack(stat_rows)))
        loss_total, pullback, (latent_rows, stat_rows) = jax.vjp(loss_fn, weights, table_full, jnp.zeros((LAYERS, ROWS, LAT), jnp.float32), has_aux=True)
        grad_weights, grad_tab, grad_shift = pullback(jnp.ones((), jnp.float32))
        grad_stat = lax.optimization_barrier(jnp.sum(valid_rows[None, :] * lax.optimization_barrier(jnp.sum(grad_shift * grad_shift, 2)), 1))
        stat_rows = jnp.concatenate([stat_rows, grad_stat[:, None]], 1)
        running = jax.tree.map(jnp.add, running, (grad_weights, grad_tab))
        return (running, (latent_rows, grad_shift, stat_rows))
    start_carry = jax.tree.map(jnp.zeros_like, (weights, table_full))
    (grad_weights, grad_tab), (latent_rows, grad_shift, stat_rows) = lax.scan(per_block, start_carry, jnp.arange(block_count, dtype=jnp.int32))
    latents_out = jnp.transpose(latent_rows, (1, 0, 2, 3)).reshape(LAYERS, TOKENS, LAT).astype(jnp.bfloat16)
    grad_latents = jnp.transpose(grad_shift, (1, 0, 2, 3)).reshape(LAYERS, TOKENS, LAT)
    totals = lax.optimization_barrier(jnp.sum(stat_rows, 0))
    rms_stats = jnp.stack([jnp.sqrt(totals[:, 1] / totals[:, 0]), jnp.sqrt(totals[:, 2] / (totals[:, 0] * LAT))], 1)
    return (latents_out, grad_latents, grad_weights[0], grad_weights[1], grad_weights[2], grad_weights[3], grad_weights[4], grad_weights[5], grad_weights[6], grad_weights[7], grad_weights[8], grad_weights[9], grad_weights[10], grad_weights[11], grad_weights[12], grad_weights[13], grad_tab, rms_stats)
```

```python
import functools

import jax
import jax.numpy as jnp
from jax import lax
from jax.experimental import pallas as pl
from jax.experimental.pallas import tpu as pltpu
from jax.sharding import PartitionSpec as P

GROUP = 8
EPS = 1e-05
F32 = jnp.float32
B16 = jnp.bfloat16
MESH = pl.DeviceIdType.MESH

LANES = 128
CHIPS = 4
PEERS = 2 * CHIPS
CHUNK = 128
QROWS = 256
SUB = 128
VECS = 16

NN = (((1,), (0,)), ((), ()))
NT = (((1,), (1,)), ((), ()))
TN = (((0,), (0,)), ((), ()))


def dot(a, b, dims=NN):
    return lax.dot_general(a, b, dims, preferred_element_type=F32)


def split_dot(a, b, dims=NN):
    high = a.astype(B16)
    low = (a - high.astype(F32)).astype(B16)
    return dot(high, b, dims) + dot(low, b, dims)


def split_dot_right(a, b, dims):
    high = b.astype(B16)
    low = (b - high.astype(F32)).astype(B16)
    return dot(a, high, dims) + dot(a, low, dims)


def norm_mish(x, gain, shift):
    center = x - jnp.mean(x, -1, keepdims=True)
    spread = jnp.mean(center * center, -1, keepdims=True)
    scale = lax.rsqrt(spread + EPS)
    n = center * scale
    u = n * gain + shift
    w = jnp.exp(jnp.minimum(u, 30.0))
    top = w * (w + 2.0)
    over = pltpu.reciprocal(top + 2.0, approx=True)
    act = u * (top * over)
    slope = (top + 4.0 * (u * (top - w)) * over) * over
    return act, n, slope, scale


def tiles(size, step=256):
    return [(lo, min(lo + step, size)) for lo in range(0, size, step)]


def eight_rows(x):
    return x.reshape(x.shape[0] // 8, 8, x.shape[1]).sum(0)


def each_sub(count, body):
    if count <= SUB:
        body(0, count)
        return

    def step(j, carry):
        body(pl.multiple_of(j * SUB, SUB), SUB)
        return carry

    lax.fori_loop(0, count // SUB, step, 0)


def layer_forward(pre, count, bias, gain, shift, act_ref, act_at, n_ref, slope_ref, scale_ref, lane, at):
    def body(j, sub):
        act, n, slope, scale = norm_mish(pre[pl.ds(j, sub), :] + bias, gain, shift)
        act_ref[pl.ds(act_at + j, sub), :] = act.astype(B16)
        here = pl.ds(at + j, sub)
        n_ref[here, :] = n.astype(n_ref.dtype)
        slope_ref[here, :] = slope.astype(slope_ref.dtype)
        scale_ref[here, lane : lane + 1] = scale

    each_sub(count, body)


def layer_backward(pre, count, gain, n_ref, slope_ref, scale_ref, lane, at, out_ref, out_at, sums, first):
    def body(j, sub):
        here = pl.ds(at + j, sub)
        n = n_ref[here, :].astype(F32)
        du = pre[pl.ds(j, sub), :] * slope_ref[here, :].astype(F32)
        by_n = du * n
        dn = du * gain
        mean_dn = jnp.mean(dn, -1, keepdims=True)
        mean_by_n = jnp.mean(by_n * gain, -1, keepdims=True)
        out = (dn - mean_dn - n * mean_by_n) * scale_ref[here, lane : lane + 1]
        out_ref[pl.ds(out_at + j, sub), :] = out.astype(B16)
        sums[first : first + 8, :] += eight_rows(out)
        sums[first + 8 : first + 16, :] += eight_rows(by_n)
        sums[first + 16 : first + 24, :] += eight_rows(du)

    each_sub(count, body)


def step_kernel(dims, *refs):
    rows, lat, act_width, in_width, hid, heads, bins, tasks, emb, steps = dims
    side_width = in_width - lat
    block = in_width + hid + LANES + VECS
    block0 = in_width + hid + lat + VECS
    at_mid = in_width
    at_out = in_width + hid
    (
        lat_in, acts, meta, amask, table, cot_in, w_in, w_mid, w_dyn, w_q,
        b_in, g_in, s_in, b_mid, g_mid, s_mid, b_dyn, g_dyn, s_dyn, b_q,
        lat_out, grad_out, recv_q, recv_0, small_out,
        x, m, hot, wi, wm, wq, wq_raw, wi0, wm0, wd, vec, bq, diag,
        ig, act1, act2, spg, fpg, qg, n1, d1, n2, d2, q_scales, pre,
        act1_0, act2_0, spg_0, fpg_0, n1_0, d1_0, n2_0, d2_0, scales,
        dyn_n, new_lat, lat_low, cot, dyn_grad, arrived, back, pair_grad, pair_send,
        gb, half_q, half_0, sums, q_sums, dyn_sums, stat, small, small_recv, table_recv,
        w_sem, in_sem, out_sem, lat_s, lat_r, px_s, px_r, side_s, side_r, pg_s, pg_r, gr_s, gr_r,
        half_s, half_r, own_s, rb_s, rb_r, sm_s, sm_r, tb_s, tb_r,
    ) = refs
    section = lax.axis_index("section")
    d = lax.axis_index("dp")
    place = lax.rem(d, PEERS)
    base = d - place
    chip = place // 2
    core = lax.rem(place, 2)
    edge = (chip == 0) | (chip == CHIPS - 1)
    last = steps - 1
    mate = base + chip * 2 + (1 - core)
    pair = base + (chip + 1 - 2 * lax.rem(chip, 2)) * 2 + core
    following = jnp.minimum(section + 1, last)
    before = jnp.maximum(section - 1, 0)
    chunks = rows // CHUNK
    head_of = [jnp.int32(3), jnp.where(edge, 1, 4), jnp.where(edge, 2, 5)]

    def remote(src, dst, send, recv, to):
        return pltpu.make_async_remote_copy(
            src_ref=src, dst_ref=dst, send_sem=send, recv_sem=recv, device_id=to, device_id_type=MESH
        )

    def chunk_at(i):
        return pl.multiple_of(i * CHUNK, CHUNK)

    loads = [
        pltpu.make_async_copy(w_in.at[0], wi0, w_sem.at[0]),
        pltpu.make_async_copy(w_mid.at[0], wm0, w_sem.at[1]),
        pltpu.make_async_copy(w_dyn, wd, w_sem.at[2]),
    ]
    for job in range(3):
        h = head_of[job]
        slot = job % 2
        loads += [
            pltpu.make_async_copy(w_in.at[h], wi.at[slot], w_sem.at[3 + 3 * job]),
            pltpu.make_async_copy(w_mid.at[h], wm.at[slot], w_sem.at[4 + 3 * job]),
            pltpu.make_async_copy(w_q.at[h - 1], wq_raw.at[slot], w_sem.at[5 + 3 * job]),
        ]
    load_cot = pltpu.make_async_copy(cot_in, cot, w_sem.at[12])
    load_meta = pltpu.make_async_copy(meta, m.at[0:rows], w_sem.at[13])
    load_meta.start()

    def load_lat(i):
        here = pl.ds(chunk_at(i), CHUNK)
        return pltpu.make_async_copy(lat_in.at[here], x.at[here, 0:lat], in_sem.at[i])

    for copy in loads[:1]:
        copy.start()

    @pl.when(section == 0)
    def _():
        for i in range(chunks):
            load_lat(i).start()

    for copy in loads[1:9]:
        copy.start()
    load_cot.start()

    barrier = pltpu.get_barrier_semaphore()
    for other in range(1, PEERS):
        to = base + lax.rem(place + other, PEERS)
        pl.semaphore_signal(barrier, inc=1, device_id=(section, to), device_id_type=MESH)
    for other in range(1, steps):
        to = lax.rem(section + other, steps)
        pl.semaphore_signal(barrier, inc=1, device_id=(to, d), device_id_type=MESH)

    load_meta.wait()
    one_hot = (m[0:rows, 0:1] == lax.broadcasted_iota(jnp.int32, (rows, tasks), 1).astype(F32)).astype(B16)
    hot[0:rows, :] = one_hot
    mask = dot(one_hot, amask[...].astype(F32).astype(B16))
    side = jnp.concatenate(
        [(acts[...].astype(F32) * mask).astype(B16), dot(one_hot, table[...]).astype(B16)], 1
    )
    x[0:rows, lat:in_width] = side
    for t, source in enumerate((b_in, g_in, s_in, b_mid, g_mid, s_mid)):
        vec[t, 0 : heads + 1, :] = source[...].astype(F32)
    bq[...] = jnp.full(bq.shape, -1e30, F32)
    bq[0:heads, 0:bins] = b_q[...].astype(F32)
    wq[...] = jnp.zeros(wq.shape, B16)
    shift = GROUP.bit_length() - 1
    diag[...] = (
        lax.shift_right_logical(lax.broadcasted_iota(jnp.int32, (lat, lat), 0), shift)
        == lax.shift_right_logical(lax.broadcasted_iota(jnp.int32, (lat, lat), 1), shift)
    ).astype(F32).astype(B16)
    sums[...] = jnp.zeros(sums.shape, F32)
    ig[rows : 2 * rows, :] = jnp.zeros((rows, in_width), F32)
    q_sums[...] = jnp.zeros(q_sums.shape, F32)
    dyn_sums[...] = jnp.zeros(dyn_sums.shape, F32)
    stat[...] = jnp.zeros(stat.shape, F32)
    small[...] = jnp.zeros(small.shape, F32)

    @pl.when(section == last)
    def _():
        arrived[...] = jnp.zeros(arrived.shape, B16)

    pl.semaphore_wait(barrier, PEERS - 1 + steps - 1)

    side_copy = remote(
        x.at[0:rows, lat : lat + 2 * LANES], x.at[rows : 2 * rows, lat : lat + 2 * LANES],
        side_s.at[0], side_r.at[0], (section, pair),
    )
    meta_copy = remote(
        m.at[0:rows], m.at[rows : 2 * rows], side_s.at[1], side_r.at[1], (section, pair)
    )
    side_copy.start()
    meta_copy.start()
    for copy in loads[:3]:
        copy.wait()

    def vec_of(t, h):
        return vec[t, pl.ds(h, 1), :]

    def lat_copy(i):
        here = pl.ds(chunk_at(i), CHUNK)
        return remote(
            lat_low.at[here], x.at[here, 0:lat], lat_s.at[i], lat_r.at[i], (following, d)
        )

    def pair_copy(i):
        here = chunk_at(i)
        return remote(
            x.at[pl.ds(here, CHUNK), 0:lat], x.at[pl.ds(rows + here, CHUNK), 0:lat],
            px_s.at[i], px_r.at[i], (section, pair),
        )

    def lat_store(i):
        here = pl.ds(chunk_at(i), CHUNK)
        return pltpu.make_async_copy(lat_low.at[here], lat_out.at[here], out_sem.at[i])

    def forward_chunk(i, carry):
        at = chunk_at(i)
        here = pl.ds(at, CHUNK)

        @pl.when(section > 0)
        def _():
            lat_copy(i).wait_recv()

        @pl.when(section == 0)
        def _():
            load_lat(i).wait()

        pair_copy(i).start()
        pre[0:CHUNK, :] = dot(x[here, 0:in_width], wi0[...])
        layer_forward(
            pre, CHUNK, vec[0, 0:1, :], vec[1, 0:1, :], vec[2, 0:1, :], act1_0, at, n1_0, d1_0, scales, 0, at
        )
        pre[0:CHUNK, :] = dot(act1_0[here, :], wm0[...])
        layer_forward(
            pre, CHUNK, vec[3, 0:1, :], vec[4, 0:1, :], vec[5, 0:1, :], act2_0, at, n2_0, d2_0, scales, 1, at
        )
        out = dot(act2_0[here, :], wd[...]) + b_dyn[...].astype(F32)
        center = out - jnp.mean(out, -1, keepdims=True)
        scale = lax.rsqrt(jnp.mean(center * center, -1, keepdims=True) + EPS)
        normal = center * scale
        dyn_n[here, :] = normal
        scales[here, 2:3] = scale
        power = jnp.exp(normal * g_dyn[...].astype(F32) + s_dyn[...].astype(F32))
        fresh = power * pltpu.reciprocal(split_dot(power, diag[...]), approx=True)
        new_lat[here, :] = fresh
        low = fresh.astype(B16)
        lat_low[here, :] = low

        @pl.when(section < last)
        def _():
            lat_copy(i).start()

        lat_store(i).start()
        wide = low.astype(F32)
        stat[0:8, :] += eight_rows(m[here, 1:2] * (wide * wide))
        return carry

    lax.fori_loop(0, chunks, forward_chunk, 0)

    def q_chunk(job, at):
        here = pl.ds(at, QROWS)
        h = head_of[job]
        pre[...] = dot(x[here, 0:in_width], wi[job % 2])
        layer_forward(
            pre, QROWS, vec_of(0, h), vec_of(1, h), vec_of(2, h), act1, at, n1, d1, q_scales, 0, 0
        )
        pre[...] = dot(act1[here, :], wm[job % 2])
        layer_forward(
            pre, QROWS, vec_of(3, h), vec_of(4, h), vec_of(5, h), act2, at, n2, d2, q_scales, 1, 0
        )
        logits = dot(act2[here, :], wq[job % 2]) + bq[pl.ds(h - 1, 1), :]
        power = jnp.exp(logits - jnp.max(logits, -1, keepdims=True))
        chance = power / jnp.sum(power, -1, keepdims=True)
        lane = lax.broadcasted_iota(jnp.int32, (QROWS, LANES), 1).astype(F32)
        low_bin = m[here, 2:3]
        part = m[here, 3:4]
        target = jnp.where(lane == low_bin, 1.0 - part, 0.0) + jnp.where(lane == low_bin + 1.0, part, 0.0)
        grad = (m[here, 1:2] * (chance - target)).astype(B16)
        qg[here, :] = grad
        q_sums[8 * job : 8 * job + 8, :] += eight_rows(grad.astype(F32))
        pre[...] = dot(grad, wq[job % 2], NT)
        layer_backward(pre, QROWS, vec_of(4, h), n2, d2, q_scales, 1, 0, spg, at, sums.at[job], 24)
        pre[...] = dot(spg[here, :], wm[job % 2], NT)
        layer_backward(pre, QROWS, vec_of(1, h), n1, d1, q_scales, 0, 0, fpg, at, sums.at[job], 0)
        for lo, hi in tiles(in_width):
            back_in = dot(fpg[here, :], wi[job % 2, lo:hi, :], NT)
            if job == 0:
                ig[here, lo:hi] = back_in
            else:
                ig[here, lo:hi] += back_in

    def q_job(job):
        for copy in loads[3 + 3 * job : 6 + 3 * job]:
            copy.wait()
        wq[job % 2, :, 0:bins] = wq_raw[job % 2]

        def body(i, carry):
            q_chunk(job, pl.multiple_of(i * QROWS, QROWS))
            return carry

        lax.fori_loop(0, (rows if job == 0 else 2 * rows) // QROWS, body, 0)

    def half_copy(job, z):
        if job < 3:
            src, dst = gb.at[1 - core, z, 0:block], half_q.at[job, z]
        else:
            src, dst = gb.at[1 - core, z], half_0.at[z]
        return remote(src, dst, half_s.at[job, z], half_r.at[job, z], (section, mate))

    def owner_copy(job, z):
        if job < 3:
            src, dst = half_q.at[job, z], recv_q.at[job, chip]
        else:
            src, dst = half_0.at[z], recv_0.at[chip]
        return remote(src, dst, rb_s.at[job, z], rb_r.at[job, chip], (section, base + 2 * z + core))

    def arrival(job, z):
        if job < 3:
            src, dst = half_q.at[job, chip], recv_q.at[job, z]
        else:
            src, dst = half_0.at[chip], recv_0.at[z]
        return remote(src, dst, rb_s.at[job, z], rb_r.at[job, z], (section, base + 2 * z + core))

    def keep_copy(job):
        if job < 3:
            src, dst = half_q.at[job, chip], recv_q.at[job, chip]
        else:
            src, dst = half_0.at[chip], recv_0.at[chip]
        return pltpu.make_async_copy(src, dst, own_s.at[job])

    def weight_grads(job):
        if job < 3:
            count = rows if job == 0 else 2 * rows
            a1, a2, sp, fp, out = act1, act2, spg, fpg, qg
        else:
            count = rows
            a1, a2, sp, fp, out = act1_0, act2_0, spg_0, fpg_0, dyn_grad
        size = block if job < 3 else block0

        def body(z, carry):
            cols = pl.ds(pl.multiple_of(z * 2 * LANES, 2 * LANES), 2 * LANES)
            for left, right, first, size_of in ((x, fp, 0, in_width), (a1, sp, at_mid, hid)):
                for lo, hi in tiles(size_of):
                    grad = dot(left[0:count, lo:hi], right[0:count, cols], TN)
                    for p in range(2):
                        gb[p, z, first + lo : first + hi, :] = grad[:, p * LANES : (p + 1) * LANES].astype(B16)
            g_out = dot(a2[0:count, cols], out[0:count, :], TN)
            for p in range(2):
                for t in range(g_out.shape[1] // LANES):
                    gb[p, z, at_out + t * LANES : at_out + (t + 1) * LANES, :] = g_out[
                        p * LANES : (p + 1) * LANES, t * LANES : (t + 1) * LANES
                    ].astype(B16)
            lines = [jnp.sum(sums[job, 8 * t : 8 * t + 8, cols], 0, keepdims=True) for t in range(6)]
            lines.append(jnp.zeros((VECS - 6, 2 * LANES), F32))
            vectors = jnp.concatenate(lines, 0).astype(B16)
            for p in range(2):
                gb[p, z, size - VECS : size, :] = vectors[:, p * LANES : (p + 1) * LANES]
            half_copy(job, z).start()
            return carry

        lax.fori_loop(0, CHIPS, body, 0)

        def finish(z, carry):
            half_copy(job, z).wait_recv()
            parts = 4
            step = size // parts // 16 * 16
            for part in range(parts):
                span = slice(part * step, size if part == parts - 1 else (part + 1) * step)
                if job < 3:
                    half_q[job, z, span, :] = (
                        half_q[job, z, span, :].astype(F32) + gb[core, z, span, :].astype(F32)
                    ).astype(B16)
                else:
                    half_0[z, span, :] = (
                        half_0[z, span, :].astype(F32) + gb[core, z, span, :].astype(F32)
                    ).astype(B16)

            @pl.when(z != chip)
            def _():
                owner_copy(job, z).start()

            return carry

        lax.fori_loop(0, CHIPS, finish, 0)
        keep_copy(job).start()

        def sent(z, carry):
            half_copy(job, z).wait_send()
            return carry

        lax.fori_loop(0, CHIPS, sent, 0)

    q_job(0)
    for copy in loads[9:]:
        copy.start()
    weight_grads(0)

    side_copy.wait_recv()
    meta_copy.wait_recv()
    hot[rows : 2 * rows, :] = (
        m[rows : 2 * rows, 0:1] == lax.broadcasted_iota(jnp.int32, (rows, tasks), 1).astype(F32)
    ).astype(B16)

    def pair_here(i, carry):
        pair_copy(i).wait_recv()
        return carry

    lax.fori_loop(0, chunks, pair_here, 0)
    q_job(1)
    weight_grads(1)
    q_job(2)

    def pg_copy(i):
        here = pl.ds(chunk_at(i), CHUNK)
        return remote(
            pair_send.at[here], pair_grad.at[here], pg_s.at[i], pg_r.at[i], (section, pair)
        )

    def send_pair(i, carry):
        at = chunk_at(i)
        pair_send[pl.ds(at, CHUNK), :] = ig[pl.ds(rows + at, CHUNK), 0:lat].astype(B16)
        pg_copy(i).start()
        return carry

    lax.fori_loop(0, chunks, send_pair, 0)

    load_cot.wait()

    def back_copy(i):
        here = pl.ds(chunk_at(i), CHUNK)
        return remote(back.at[here], arrived.at[here], gr_s.at[i], gr_r.at[i], (before, d))

    def grad_store(i):
        here = pl.ds(chunk_at(i), CHUNK)
        return pltpu.make_async_copy(new_lat.at[here], grad_out.at[here], out_sem.at[chunks + i])

    def backward_chunk(i, carry):
        at = chunk_at(i)
        here = pl.ds(at, CHUNK)

        @pl.when(section < last)
        def _():
            back_copy(i).wait_recv()

        out_grad = cot[here, :].astype(F32) + arrived[here, :].astype(F32)
        fresh = new_lat[here, :]
        normal = dyn_n[here, :]
        norm_grad = fresh * (out_grad - split_dot(out_grad * fresh, diag[...]))
        by_n = norm_grad * normal
        gain = g_dyn[...].astype(F32)
        dm = norm_grad * gain
        mean_dm = jnp.mean(dm, -1, keepdims=True)
        mean_by_n = jnp.mean(by_n * gain, -1, keepdims=True)
        low = ((dm - mean_dm - normal * mean_by_n) * scales[here, 2:3]).astype(B16)
        dyn_grad[here, :] = low
        dyn_sums[0:8, :] += eight_rows(low.astype(F32))
        dyn_sums[8:16, :] += eight_rows(by_n)
        dyn_sums[16:24, :] += eight_rows(norm_grad)
        pre[0:CHUNK, :] = dot(low, wd[...], NT)
        layer_backward(pre, CHUNK, vec[4, 0:1, :], n2_0, d2_0, scales, 1, at, spg_0, at, sums.at[3], 24)
        pre[0:CHUNK, :] = dot(spg_0[here, :], wm0[...], NT)
        layer_backward(pre, CHUNK, vec[1, 0:1, :], n1_0, d1_0, scales, 0, at, fpg_0, at, sums.at[3], 0)
        back_in = dot(fpg_0[here, :], wi0[...], NT)
        pg_copy(i).wait_recv()
        total = back_in[:, 0:lat] + ig[here, 0:lat] + pair_grad[here, :].astype(F32)
        back[here, :] = total.astype(B16)

        @pl.when(section > 0)
        def _():
            back_copy(i).start()

        new_lat[here, :] = total
        grad_store(i).start()
        stat[8:16, :] += eight_rows(m[here, 1:2] * (total * total))
        ig[here, lat:in_width] += back_in[:, lat:in_width]
        return carry

    def late(turn, carry):
        @pl.when((turn == 0) == (section == last))
        def _():
            lax.fori_loop(0, chunks, backward_chunk, 0)

        @pl.when((turn == 0) == (section < last))
        def _():
            weight_grads(2)

        return carry

    lax.fori_loop(0, 2, late, 0)
    weight_grads(3)

    small[0:tasks, 0:emb] = split_dot_right(hot[...], ig[:, lat:in_width], TN)[:, side_width - emb :]
    for t in range(3):
        line = jnp.sum(dyn_sums[8 * t : 8 * t + 8, :], 0, keepdims=True)
        for part in range(lat // LANES):
            row = tasks + t * (lat // LANES) + part
            small[row : row + 1, :] = line[:, part * LANES : (part + 1) * LANES]
    q_lines = [jnp.sum(q_sums[8 * job : 8 * job + 8, :], 0, keepdims=True) for job in range(3)]
    for h in range(heads):
        line = sum(jnp.where(head_of[job] == h + 1, q_lines[job], 0.0) for job in range(3))
        row = tasks + 3 * (lat // LANES) + h
        small[row : row + 1, :] = line
    row = tasks + 3 * (lat // LANES) + heads
    lane = lax.broadcasted_iota(jnp.int32, (1, LANES), 1)
    count = jnp.sum(m[0:rows, 1:2], 0, keepdims=True)
    lat_square = jnp.sum(jnp.sum(stat[0:8, :], 0, keepdims=True), 1, keepdims=True)
    grad_square = jnp.sum(jnp.sum(stat[8:16, :], 0, keepdims=True), 1, keepdims=True)
    small[row : row + 1, :] = jnp.where(
        lane == 0, count, jnp.where(lane == 1, lat_square, jnp.where(lane == 2, grad_square, 0.0))
    )
    small_recv[place] = small[...]

    def small_copy(other):
        to = base + lax.rem(place + other, PEERS)
        return remote(small, small_recv.at[place], sm_s.at[other], sm_r.at[place], (section, to))

    def small_arrival(other):
        source = lax.rem(place + other, PEERS)
        return remote(small, small_recv.at[source], sm_s.at[other], sm_r.at[source], (section, base + source))

    for other in range(1, PEERS):
        small_copy(other).start()
    for other in range(1, PEERS):
        small_arrival(other).wait_recv()
    total = small_recv[0]
    for source in range(1, PEERS):
        total = total + small_recv[source]
    for other in range(1, PEERS):
        small_copy(other).wait_send()
    small[...] = total
    table_recv[section] = small[0:tasks, :]

    def table_copy(other):
        to = lax.rem(section + other, steps)
        return remote(
            small.at[0:tasks], table_recv.at[section], tb_s.at[other], tb_r.at[section], (to, d)
        )

    def table_arrival(other):
        source = lax.rem(section + other, steps)
        return remote(small.at[0:tasks], table_recv.at[source], tb_s.at[other], tb_r.at[source], (source, d))

    for other in range(1, steps):
        table_copy(other).start()

    def own_done(job):
        def body(other, carry):
            z = lax.rem(chip + other, CHIPS)
            arrival(job, z).wait_recv()
            owner_copy(job, z).wait_send()
            return carry

        lax.fori_loop(1, CHIPS, body, 0)
        keep_copy(job).wait()

    side_copy.wait_send()
    meta_copy.wait_send()

    def sends(i, carry):
        pair_copy(i).wait_send()
        pg_copy(i).wait_send()
        lat_store(i).wait()
        grad_store(i).wait()

        @pl.when(section < last)
        def _():
            lat_copy(i).wait_send()

        @pl.when(section > 0)
        def _():
            back_copy(i).wait_send()

        return carry

    lax.fori_loop(0, chunks, sends, 0)
    for job in range(4):
        own_done(job)
    for other in range(1, steps):
        table_arrival(other).wait_recv()
    for other in range(1, steps):
        table_copy(other).wait_send()
    whole = table_recv[0]
    for source in range(1, steps):
        whole = whole + table_recv[source]
    small[0:tasks, :] = whole
    done = pltpu.make_async_copy(small, small_out, out_sem.at[2 * chunks])
    done.start()
    done.wait()


def on_device(
    latent_in, actions, task_ids, valid, action_mask, bins, fraction, latent_cot,
    w_in, b_in, g_in, beta_in, w_mid, b_mid, g_mid, beta_mid,
    w_dyn_out, b_dyn_out, g_dyn_out, beta_dyn_out, w_q_out, b_q_out, table,
):
    steps = lax.axis_size("section")
    spread = lax.axis_size("dp")
    groups = spread // PEERS
    rows, lat = latent_in.shape
    act_width = actions.shape[2]
    in_width, hid = w_in.shape[2:]
    heads = w_q_out.shape[1]
    bin_count = w_q_out.shape[-1]
    tasks, emb = table.shape
    block = in_width + hid + LANES + VECS
    block0 = in_width + hid + lat + VECS
    chunks = rows // CHUNK
    small_rows = tasks + 24
    meta = jnp.stack(
        [task_ids.astype(F32), valid.astype(F32), bins[0].astype(F32), fraction[0]], 1
    )
    meta = jnp.pad(meta, ((0, 0), (0, LANES - 4)))
    dims = (rows, lat, act_width, in_width, hid, heads, bin_count, tasks, emb, steps)
    anywhere = pl.BlockSpec(memory_space=pl.ANY)
    vmem = pl.BlockSpec(memory_space=pltpu.VMEM)
    dma = pltpu.SemaphoreType.DMA
    both = 2 * rows
    wide = pltpu.VMEM((rows, hid), B16)
    thin = pltpu.VMEM((rows, LANES), F32)
    low = pltpu.VMEM((rows, lat), B16)
    full = pltpu.VMEM((rows, lat), F32)
    part_low = pltpu.VMEM((QROWS, hid), B16)
    part_thin = pltpu.VMEM((QROWS, LANES), F32)
    q_wide = pltpu.VMEM((both, hid), B16)
    lat_out, grad_out, recv_q, recv_0, small = pl.pallas_call(
        functools.partial(step_kernel, dims),
        out_shape=[
            jax.ShapeDtypeStruct((rows, lat), B16),
            jax.ShapeDtypeStruct((rows, lat), F32),
            jax.ShapeDtypeStruct((3, CHIPS, block, LANES), B16),
            jax.ShapeDtypeStruct((CHIPS, block0, LANES), B16),
            jax.ShapeDtypeStruct((small_rows, LANES), F32),
        ],
        in_specs=[
            anywhere, vmem, anywhere, vmem, vmem, anywhere, anywhere, anywhere, anywhere, anywhere,
            vmem, vmem, vmem, vmem, vmem, vmem, vmem, vmem, vmem, vmem,
        ],
        out_specs=[anywhere] * 5,
        scratch_shapes=[
            pltpu.VMEM((both, 6 * LANES), B16),
            pltpu.VMEM((both, LANES), F32),
            pltpu.VMEM((both, tasks), B16),
            pltpu.VMEM((2, in_width, hid), B16),
            pltpu.VMEM((2, hid, hid), B16),
            pltpu.VMEM((2, hid, LANES), B16),
            pltpu.VMEM((2, hid, bin_count), B16),
            pltpu.VMEM((in_width, hid), B16),
            pltpu.VMEM((hid, hid), B16),
            pltpu.VMEM((hid, lat), B16),
            pltpu.VMEM((6, 8, hid), F32),
            pltpu.VMEM((8, LANES), F32),
            pltpu.VMEM((lat, lat), B16),
            pltpu.VMEM((both, in_width), F32),
            q_wide, q_wide, q_wide, q_wide,
            pltpu.VMEM((both, LANES), B16),
            part_low, part_low, part_low, part_low, part_thin, pltpu.VMEM((QROWS, hid), F32),
            wide, wide, wide, wide,
            wide, wide, wide, wide, thin,
            full, full, low, low, low, low, low, low, low,
            pltpu.VMEM((2, CHIPS, block0, LANES), B16),
            pltpu.VMEM((3, CHIPS, block, LANES), B16),
            pltpu.VMEM((CHIPS, block0, LANES), B16),
            pltpu.VMEM((4, 48, hid), F32),
            pltpu.VMEM((24, LANES), F32),
            pltpu.VMEM((24, lat), F32),
            pltpu.VMEM((16, lat), F32),
            pltpu.VMEM((small_rows, LANES), F32),
            pltpu.VMEM((PEERS, small_rows, LANES), F32),
            pltpu.VMEM((steps, tasks, LANES), F32),
            dma((14,)), dma((chunks,)), dma((2 * chunks + 1,)),
            dma((chunks,)), dma((chunks,)), dma((chunks,)), dma((chunks,)),
            dma((2,)), dma((2,)), dma((chunks,)), dma((chunks,)), dma((chunks,)), dma((chunks,)),
            dma((4, CHIPS)), dma((4, CHIPS)), dma((4,)), dma((4, CHIPS)), dma((4, CHIPS)),
            dma((PEERS,)), dma((PEERS,)), dma((steps,)), dma((steps,)),
        ],
        compiler_params=pltpu.CompilerParams(
            collective_id=0, has_side_effects=True, vmem_limit_bytes=63 * 2**20
        ),
        name="step",
    )(
        latent_in, actions[0], meta, action_mask, table, latent_cot[0],
        w_in[0], w_mid[0], w_dyn_out[0], w_q_out[0],
        b_in[0], g_in[0], beta_in[0], b_mid[0], g_mid[0], beta_mid[0],
        b_dyn_out, g_dyn_out, beta_dyn_out, b_q_out[0],
    )
    q_parts = recv_q.astype(F32)
    shared = q_parts[0].sum(0)
    outer = q_parts[1:, 0] + q_parts[1:, 3]
    inner = q_parts[1:, 1] + q_parts[1:, 2]
    q_sum = jnp.stack([outer[0], outer[1], shared, inner[0], inner[1]])
    dyn_sum = recv_0.astype(F32).sum(0)

    across = [[q * PEERS + r for q in range(groups)] for r in range(PEERS)]

    def owned(piece, dim):
        if groups == 1:
            return piece
        piece = lax.psum_scatter(piece, "dp", scatter_dimension=dim, axis_index_groups=across, tiled=True)
        moves = [(q * PEERS + r, r * groups + q) for q in range(groups) for r in range(PEERS)]
        return lax.ppermute(piece, "dp", moves)

    part_in = owned(jnp.concatenate([dyn_sum[None, :in_width], q_sum[:, :in_width]], 0), 2)
    part_mid = owned(
        jnp.concatenate([dyn_sum[None, in_width : in_width + hid], q_sum[:, in_width : in_width + hid]], 0), 2
    )
    part_dyn = dyn_sum[in_width + hid : in_width + hid + lat].reshape(lat // LANES, LANES, LANES)
    part_dyn = owned(part_dyn.transpose(1, 0, 2).reshape(LANES, lat), 0)
    part_q = owned(q_sum[:, in_width + hid : in_width + hid + LANES, :bin_count], 1)
    vecs = owned(jnp.concatenate([dyn_sum[None, block0 - VECS :], q_sum[:, block - VECS :]], 0), 2)
    if groups > 1:
        small = lax.psum(small, "dp", axis_index_groups=across)
    at_q = tasks + 3 * (lat // LANES)
    grad_table = small[:tasks, :emb]
    dyn_vecs = small[tasks:at_q].reshape(3, lat)
    q_bias = small[at_q : at_q + heads, :bin_count]
    stat = small[at_q + heads, :3]
    rms = jnp.sqrt(jnp.stack([stat[1] / stat[0], stat[2] / (stat[0] * lat)]))[None]
    return (
        lat_out[None],
        grad_out[None],
        part_in[None],
        vecs[None, :, 0],
        vecs[None, :, 1],
        vecs[None, :, 2],
        part_mid[None],
        vecs[None, :, 3],
        vecs[None, :, 4],
        vecs[None, :, 5],
        part_dyn[None],
        dyn_vecs[0:1],
        dyn_vecs[1:2],
        dyn_vecs[2:3],
        part_q[None],
        q_bias[None],
        grad_table,
        rms,
    )


def solution(mesh):
    placed = (
        P("dp", None),
        P("section", "dp", None),
        P("dp"),
        P("dp"),
        P(),
        P("section", "dp"),
        P("section", "dp"),
        P("section", "dp", None),
        P("section", None, None, None),
        P("section", None, None),
        P("section", None, None),
        P("section", None, None),
        P("section", None, None, None),
        P("section", None, None),
        P("section", None, None),
        P("section", None, None),
        P("section", None, None),
        P("section", None),
        P("section", None),
        P("section", None),
        P("section", None, None, None),
        P("section", None, None),
        P(),
    )
    return jax.shard_map(
        on_device,
        mesh=mesh,
        in_specs=placed,
        out_specs=(
            P("section", "dp", None),
            P("section", "dp", None),
            P("section", None, None, "dp"),
            P("section", None, "dp"),
            P("section", None, "dp"),
            P("section", None, "dp"),
            P("section", None, None, "dp"),
            P("section", None, "dp"),
            P("section", None, "dp"),
            P("section", None, "dp"),
            P("section", "dp", None),
            P("section", None),
            P("section", None),
            P("section", None),
            P("section", None, "dp", None),
            P("section", None, None),
            P(),
            P("section", None),
        ),
        check_vma=False,
    )
```

```python
import functools

import jax
import jax.numpy as jnp
from jax import lax
from jax.experimental import pallas as pl
from jax.experimental.pallas import tpu as pltpu
from jax.sharding import PartitionSpec as P

GROUP = 8
EPS = 1e-05
F32 = jnp.float32
B16 = jnp.bfloat16
MESH = pl.DeviceIdType.MESH

LANES = 128
CHIPS = 4
PEERS = 2 * CHIPS
CHUNK = 128
QROWS = 256
SUB = 256
VECS = 16

NN = (((1,), (0,)), ((), ()))
NT = (((1,), (1,)), ((), ()))
TN = (((0,), (0,)), ((), ()))


def dot(a, b, dims=NN):
    return lax.dot_general(a, b, dims, preferred_element_type=F32)


def split_dot(a, b, dims=NN):
    high = a.astype(B16)
    low = (a - high.astype(F32)).astype(B16)
    return dot(high, b, dims) + dot(low, b, dims)


def split_dot_right(a, b, dims):
    high = b.astype(B16)
    low = (b - high.astype(F32)).astype(B16)
    return dot(a, high, dims) + dot(a, low, dims)


def norm_mish(x, gain, shift):
    center = x - jnp.mean(x, -1, keepdims=True)
    spread = jnp.mean(center * center, -1, keepdims=True)
    scale = lax.rsqrt(spread + EPS)
    n = center * scale
    u = n * gain + shift
    w = jnp.exp(jnp.minimum(u, 30.0))
    top = w * (w + 2.0)
    over = pltpu.reciprocal(top + 2.0, approx=True)
    act = u * (top * over)
    slope = (top + 4.0 * (u * (top - w)) * over) * over
    return act, n, slope, scale


def tiles(size, step=256):
    return [(lo, min(lo + step, size)) for lo in range(0, size, step)]


def eight_rows(x):
    return x.reshape(x.shape[0] // 8, 8, x.shape[1]).sum(0)


def each_sub(count, body):
    if count <= SUB:
        body(0, count)
        return

    def step(j, carry):
        body(pl.multiple_of(j * SUB, SUB), SUB)
        return carry

    lax.fori_loop(0, count // SUB, step, 0)


def layer_forward(pre, count, bias, gain, shift, act_ref, act_at, n_ref, slope_ref, scale_ref, lane, at):
    def body(j, sub):
        act, n, slope, scale = norm_mish(pre[pl.ds(j, sub), :] + bias, gain, shift)
        act_ref[pl.ds(act_at + j, sub), :] = act.astype(B16)
        here = pl.ds(at + j, sub)
        n_ref[here, :] = n.astype(n_ref.dtype)
        slope_ref[here, :] = slope.astype(slope_ref.dtype)
        scale_ref[here, lane : lane + 1] = scale

    each_sub(count, body)


def layer_backward(pre, count, gain, n_ref, slope_ref, scale_ref, lane, at, out_ref, out_at, sums, first):
    def body(j, sub):
        here = pl.ds(at + j, sub)
        n = n_ref[here, :].astype(F32)
        du = pre[pl.ds(j, sub), :] * slope_ref[here, :].astype(F32)
        by_n = du * n
        dn = du * gain
        mean_dn = jnp.mean(dn, -1, keepdims=True)
        mean_by_n = jnp.mean(by_n * gain, -1, keepdims=True)
        out = (dn - mean_dn - n * mean_by_n) * scale_ref[here, lane : lane + 1]
        out_ref[pl.ds(out_at + j, sub), :] = out.astype(B16)
        sums[first : first + 8, :] += eight_rows(out)
        sums[first + 8 : first + 16, :] += eight_rows(by_n)
        sums[first + 16 : first + 24, :] += eight_rows(du)

    each_sub(count, body)


def step_kernel(dims, *refs):
    rows, lat, act_width, in_width, hid, heads, bins, tasks, emb, steps = dims
    side_width = in_width - lat
    block = in_width + hid + LANES + VECS
    block0 = in_width + hid + lat + VECS
    at_mid = in_width
    at_out = in_width + hid
    both = 2 * rows
    (
        lat_in, acts, task, valid, bin_at, part_of, amask, table, cot_in, w_in, w_mid, w_dyn, w_q,
        b_in, g_in, s_in, b_mid, g_mid, s_mid, b_dyn, g_dyn, s_dyn, b_q,
        lat_out, grad_out, recv_q, recv_0, small_out,
        x, m, wi, wm, wq, wq_raw, wi0, wm0, wd, vec, bq, diag,
        ig, act1, act2, spg, fpg, qg, n1, d1, n2, d2, q_scales, pre,
        act1_0, act2_0, spg_0, fpg_0, n1_0, d1_0, n2_0, d2_0, scales,
        dyn_n, new_lat, lat_low, cot, arrived, pair_grad, pair_send,
        gb, half_q, half_0, sums, q_sums, dyn_sums, stat, small, small_recv, table_recv,
        w_sem, in_sem, out_sem, lat_s, lat_r, px_s, px_r, side_s, side_r, pg_s, pg_r, gr_s, gr_r,
        half_s, half_r, own_s, rb_s, rb_r, sm_s, sm_r, tb_s, tb_r, up_s, up_r, dn_s, dn_r, up_ok, dn_ok,
    ) = refs
    section = lax.axis_index("section")
    d = lax.axis_index("dp")
    place = lax.rem(d, PEERS)
    base = d - place
    chip = place // 2
    core = lax.rem(place, 2)
    edge = (chip == 0) | (chip == CHIPS - 1)
    lower = chip < CHIPS // 2
    side_of = chip // 2
    last = steps - 1
    mate = base + chip * 2 + (1 - core)
    pair = base + (chip + 1 - 2 * lax.rem(chip, 2)) * 2 + core
    following = jnp.minimum(section + 1, last)
    before = jnp.maximum(section - 1, 0)
    chunks = rows // CHUNK
    jobs = jnp.where(edge, 2, 3)
    first_head = jnp.where(edge, 1, 3)

    def remote(src, dst, send, recv, to):
        return pltpu.make_async_remote_copy(
            src_ref=src, dst_ref=dst, send_sem=send, recv_sem=recv, device_id=to, device_id_type=MESH
        )

    def chunk_at(i):
        return pl.multiple_of(i * CHUNK, CHUNK)

    loads = [
        pltpu.make_async_copy(w_in.at[0], wi0, w_sem.at[0]),
        pltpu.make_async_copy(w_mid.at[0], wm0, w_sem.at[1]),
        pltpu.make_async_copy(w_dyn, wd, w_sem.at[2]),
    ]

    def job_loads(job):
        slot = lax.rem(job, 2)
        h = first_head + job
        return [
            pltpu.make_async_copy(w_in.at[h], wi.at[slot], w_sem.at[3 + 3 * slot]),
            pltpu.make_async_copy(w_mid.at[h], wm.at[slot], w_sem.at[4 + 3 * slot]),
            pltpu.make_async_copy(w_q.at[h - 1], wq_raw.at[slot], w_sem.at[5 + 3 * slot]),
        ]

    load_cot = pltpu.make_async_copy(cot_in, cot, w_sem.at[9])

    def load_lat(i):
        here = pl.ds(chunk_at(i), CHUNK)
        return pltpu.make_async_copy(lat_in.at[here], x.at[here, 0:lat], in_sem.at[i])

    loads[0].start()

    @pl.when(section == 0)
    def _():
        for i in range(chunks):
            load_lat(i).start()

    for copy in loads[1:] + job_loads(jnp.int32(0)) + job_loads(jnp.int32(1)):
        copy.start()
    load_cot.start()

    barrier = pltpu.get_barrier_semaphore()
    for other in range(1, PEERS):
        to = base + lax.rem(place + other, PEERS)
        pl.semaphore_signal(barrier, inc=1, device_id=(section, to), device_id_type=MESH)
    for other in range(1, steps):
        to = lax.rem(section + other, steps)
        pl.semaphore_signal(barrier, inc=1, device_id=(to, d), device_id_type=MESH)

    lines = [task[...].astype(F32), valid[...].astype(F32), bin_at[...].astype(F32), part_of[...]]
    lines.append(jnp.zeros((4, rows), F32))
    m[0:rows, 0:8] = jnp.concatenate(lines, 0).T

    def one_hot(lo, count):
        task_lane = lax.broadcasted_iota(jnp.int32, (count, tasks), 1).astype(F32)
        return (m[lo : lo + count, 0:1] == task_lane).astype(F32).astype(B16)

    hot = one_hot(0, rows)
    mask = dot(amask[...].astype(F32).astype(B16), hot, NT)
    acting = (acts[...].astype(F32) * mask).T
    side = jnp.concatenate([acting.astype(B16), dot(hot, table[...]).astype(B16)], 1)
    x[0:rows, lat:in_width] = side
    for t, source in enumerate((b_in, g_in, s_in, b_mid, g_mid, s_mid)):
        vec[t, 0 : heads + 1, :] = source[...].astype(F32)
    bq[...] = jnp.full(bq.shape, -1e30, F32)
    bq[0:heads, 0:bins] = b_q[...].astype(F32)
    wq[...] = jnp.zeros(wq.shape, B16)
    shift = GROUP.bit_length() - 1
    diag[...] = (
        lax.shift_right_logical(lax.broadcasted_iota(jnp.int32, (lat, lat), 0), shift)
        == lax.shift_right_logical(lax.broadcasted_iota(jnp.int32, (lat, lat), 1), shift)
    ).astype(F32).astype(B16)
    sums[...] = jnp.zeros(sums.shape, F32)
    ig[...] = jnp.zeros(ig.shape, F32)
    q_sums[...] = jnp.zeros(q_sums.shape, F32)
    dyn_sums[...] = jnp.zeros(dyn_sums.shape, F32)
    stat[...] = jnp.zeros(stat.shape, F32)
    small[...] = jnp.zeros(small.shape, F32)

    @pl.when(section == last)
    def _():
        arrived[...] = jnp.zeros(arrived.shape, B16)

    pl.semaphore_wait(barrier, PEERS - 1 + steps - 1)

    side_copy = remote(
        x.at[0:rows, lat : lat + 2 * LANES], x.at[rows:both, lat : lat + 2 * LANES],
        side_s.at[0], side_r.at[0], (section, pair),
    )
    meta_copy = remote(m.at[0:rows], m.at[rows:both], side_s.at[1], side_r.at[1], (section, pair))
    side_copy.start()
    meta_copy.start()
    for copy in loads:
        copy.wait()

    def vec_of(t, h):
        return vec[t, pl.ds(h, 1), :]

    def lat_copy(i):
        here = pl.ds(chunk_at(i), CHUNK)
        return remote(
            lat_low.at[here], x.at[here, 0:lat], lat_s.at[i], lat_r.at[i], (following, d)
        )

    def pair_copy(i):
        here = chunk_at(i)
        return remote(
            x.at[pl.ds(here, CHUNK), 0:lat], x.at[pl.ds(rows + here, CHUNK), 0:lat],
            px_s.at[i], px_r.at[i], (section, pair),
        )

    def lat_store(i):
        here = pl.ds(chunk_at(i), CHUNK)
        return pltpu.make_async_copy(lat_low.at[here], lat_out.at[here], out_sem.at[i])

    def forward_chunk(i, carry):
        at = chunk_at(i)
        here = pl.ds(at, CHUNK)

        @pl.when(section > 0)
        def _():
            lat_copy(i).wait_recv()

        @pl.when(section == 0)
        def _():
            load_lat(i).wait()

        pair_copy(i).start()
        pre[0:CHUNK, :] = dot(x[here, 0:in_width], wi0[...])
        layer_forward(
            pre, CHUNK, vec[0, 0:1, :], vec[1, 0:1, :], vec[2, 0:1, :], act1_0, at, n1_0, d1_0, scales, 0, at
        )
        pre[0:CHUNK, :] = dot(act1_0[here, :], wm0[...])
        layer_forward(
            pre, CHUNK, vec[3, 0:1, :], vec[4, 0:1, :], vec[5, 0:1, :], act2_0, at, n2_0, d2_0, scales, 1, at
        )
        out = dot(act2_0[here, :], wd[...]) + b_dyn[...].astype(F32)
        center = out - jnp.mean(out, -1, keepdims=True)
        scale = lax.rsqrt(jnp.mean(center * center, -1, keepdims=True) + EPS)
        normal = center * scale
        dyn_n[here, :] = normal.astype(B16)
        scales[here, 2:3] = scale
        power = jnp.exp(normal * g_dyn[...].astype(F32) + s_dyn[...].astype(F32))
        fresh = power * pltpu.reciprocal(split_dot(power, diag[...]), approx=True)
        new_lat[here, :] = fresh
        low = fresh.astype(B16)
        lat_low[here, :] = low

        @pl.when(section < last)
        def _():
            lat_copy(i).start()

        lat_store(i).start()
        wide = low.astype(F32)
        stat[0:8, :] += eight_rows(m[here, 1:2] * (wide * wide))
        return carry

    lax.fori_loop(0, chunks, forward_chunk, 0)

    def pg_copy(i):
        here = pl.ds(chunk_at(i), CHUNK)
        return remote(
            pair_send.at[here], pair_grad.at[here], pg_s.at[i], pg_r.at[i], (section, pair)
        )

    def q_chunk(job, at):
        here = pl.ds(at, QROWS)
        h = first_head + job
        slot = lax.rem(job, 2)
        pre[...] = dot(x[here, 0:in_width], wi[slot])
        layer_forward(
            pre, QROWS, vec_of(0, h), vec_of(1, h), vec_of(2, h), act1, at, n1, d1, q_scales, 0, 0
        )
        pre[...] = dot(act1[here, :], wm[slot])
        layer_forward(
            pre, QROWS, vec_of(3, h), vec_of(4, h), vec_of(5, h), act2, at, n2, d2, q_scales, 1, 0
        )
        logits = dot(act2[here, :], wq[slot], NT) + bq[pl.ds(h - 1, 1), :]
        power = jnp.exp(logits - jnp.max(logits, -1, keepdims=True))
        chance = power / jnp.sum(power, -1, keepdims=True)
        lane = lax.broadcasted_iota(jnp.int32, (QROWS, LANES), 1).astype(F32)
        low_bin = m[here, 2:3]
        part = m[here, 3:4]
        target = jnp.where(lane == low_bin, 1.0 - part, 0.0) + jnp.where(lane == low_bin + 1.0, part, 0.0)
        grad = (m[here, 1:2] * (chance - target)).astype(B16)
        qg[here, :] = grad
        q_sums[job] += eight_rows(grad.astype(F32))
        pre[...] = dot(grad, wq[slot])
        layer_backward(pre, QROWS, vec_of(4, h), n2, d2, q_scales, 1, 0, spg, at, sums.at[0], 24)
        pre[...] = dot(spg[here, :], wm[slot], NT)
        layer_backward(pre, QROWS, vec_of(1, h), n1, d1, q_scales, 0, 0, fpg, at, sums.at[0], 0)
        for lo, hi in tiles(in_width):
            ig[here, lo:hi] += dot(fpg[here, :], wi[slot, lo:hi, :], NT)

    q_chunks = both // QROWS
    own_chunks = rows // QROWS

    def q_job(job):
        for copy in job_loads(job):
            copy.wait()
        slot = lax.rem(job, 2)
        wq[slot, 0:bins, :] = wq_raw[slot]
        sums[0] = jnp.zeros(sums.shape[1:], F32)

        def body(i, carry):
            which = lax.rem(i + jnp.where(job == 0, 0, own_chunks), q_chunks)
            at = pl.multiple_of(which * QROWS, QROWS)

            @pl.when((job == 0) & (which == own_chunks))
            def _():
                side_copy.wait_recv()
                meta_copy.wait_recv()

                def pair_here(j, carry):
                    pair_copy(j).wait_recv()
                    return carry

                lax.fori_loop(0, chunks, pair_here, 0)

            q_chunk(job, at)

            @pl.when((job == jobs - 1) & (which >= own_chunks))
            def _():
                for k in range(QROWS // CHUNK):
                    j = (which - own_chunks) * (QROWS // CHUNK) + k
                    to = chunk_at(j)
                    pair_send[pl.ds(to, CHUNK), :] = ig[pl.ds(rows + to, CHUNK), 0:lat].astype(B16)
                    pg_copy(j).start()

            return carry

        lax.fori_loop(0, q_chunks, body, 0)

        @pl.when(job + 2 < jobs)
        def _():
            for copy in job_loads(job + 2):
                copy.start()

    def half_copy(job, z, q):
        if q:
            src, dst = gb.at[1 - core, z, 0:block], half_q.at[job, z]
        else:
            src, dst = gb.at[1 - core, z], half_0.at[z]
        return remote(src, dst, half_s.at[job, z], half_r.at[job, z], (section, mate))

    def owner_copy(job, z):
        head = first_head + job - 1
        return remote(
            half_q.at[job, z], recv_q.at[head, side_of], rb_s.at[job, z], rb_r.at[head, side_of],
            (section, base + 2 * z + core),
        )

    def keep_copy(job):
        return pltpu.make_async_copy(
            half_q.at[job, chip], recv_q.at[first_head + job - 1, side_of], own_s.at[job]
        )

    def add_rows(dst, src, size):
        step = size // 4 // 16 * 16
        for part in range(4):
            span = slice(part * step, size if part == 3 else (part + 1) * step)
            dst[span, :] = (dst[span, :].astype(F32) + src[span, :].astype(F32)).astype(B16)

    def weight_grads(job, q):
        if q:
            count, a1, a2, sp, fp, own_sums = both, act1, act2, spg, fpg, 0
        else:
            count, a1, a2, sp, fp, own_sums = rows, act1_0, act2_0, spg_0, fpg_0, 1
        size = block if q else block0

        def order(i):
            return jnp.where(lower, CHIPS - 1 - i, i)

        def make(z):
            cols = pl.ds(pl.multiple_of(z * 2 * LANES, 2 * LANES), 2 * LANES)
            for left, right, first, size_of in ((x, fp, 0, in_width), (a1, sp, at_mid, hid)):
                for lo, hi in tiles(size_of):
                    grad = dot(left[0:count, lo:hi], right[0:count, cols], TN)
                    for p in range(2):
                        gb[p, z, first + lo : first + hi, :] = grad[:, p * LANES : (p + 1) * LANES].astype(B16)
            if q:
                g_out = dot(qg[0:count, :], a2[0:count, cols], TN)
                for p in range(2):
                    gb[p, z, at_out : at_out + LANES, :] = g_out[:, p * LANES : (p + 1) * LANES].astype(B16)
            else:
                g_out = dot(a2[0:count, cols], arrived[0:count, :], TN)
                for p in range(2):
                    for t in range(lat // LANES):
                        gb[p, z, at_out + t * LANES : at_out + (t + 1) * LANES, :] = g_out[
                            p * LANES : (p + 1) * LANES, t * LANES : (t + 1) * LANES
                        ].astype(B16)
            lines = [jnp.sum(sums[own_sums, 8 * t : 8 * t + 8, cols], 0, keepdims=True) for t in range(6)]
            lines.append(jnp.zeros((VECS - 6, 2 * LANES), F32))
            vectors = jnp.concatenate(lines, 0).astype(B16)
            for p in range(2):
                gb[p, z, size - VECS : size, :] = vectors[:, p * LANES : (p + 1) * LANES]
            half_copy(job, z, q).start()

        def finish(z):
            half_copy(job, z, q).wait_recv()
            if q:
                add_rows(half_q.at[job, z], gb.at[core, z], size)

                @pl.when(z != chip)
                def _():
                    owner_copy(job, z).start()

                @pl.when(z == chip)
                def _():
                    keep_copy(job).start()
            else:
                add_rows(half_0.at[z], gb.at[core, z], size)

        def body(i, carry):
            @pl.when(i < CHIPS)
            def _():
                make(order(i))

            @pl.when(i > 0)
            def _():
                finish(order(i - 1))

            return carry

        lax.fori_loop(0, CHIPS + 1, body, 0)

        def sent(z, carry):
            half_copy(job, z, q).wait_send()
            return carry

        lax.fori_loop(0, CHIPS, sent, 0)

    def job_body(job, carry):
        q_job(job)

        @pl.when(job < jobs - 1)
        def _():
            weight_grads(job, True)

        return carry

    lax.fori_loop(0, jobs, job_body, 0)

    def back_copy(i):
        here = pl.ds(chunk_at(i), CHUNK)
        return remote(lat_low.at[here], arrived.at[here], gr_s.at[i], gr_r.at[i], (before, d))

    def grad_store(i):
        here = pl.ds(chunk_at(i), CHUNK)
        return pltpu.make_async_copy(ig.at[here, 0:lat], grad_out.at[here], out_sem.at[chunks + i])

    def lat_sent(i, carry):
        lat_store(i).wait()

        @pl.when(section < last)
        def _():
            lat_copy(i).wait_send()

        return carry

    def backward_chunk(i, carry):
        at = chunk_at(i)
        here = pl.ds(at, CHUNK)

        @pl.when(section < last)
        def _():
            back_copy(i).wait_recv()

        out_grad = cot[here, :].astype(F32) + arrived[here, :].astype(F32)
        fresh = new_lat[here, :]
        normal = dyn_n[here, :].astype(F32)
        norm_grad = fresh * (out_grad - split_dot(out_grad * fresh, diag[...]))
        by_n = norm_grad * normal
        gain = g_dyn[...].astype(F32)
        dm = norm_grad * gain
        mean_dm = jnp.mean(dm, -1, keepdims=True)
        mean_by_n = jnp.mean(by_n * gain, -1, keepdims=True)
        low = ((dm - mean_dm - normal * mean_by_n) * scales[here, 2:3]).astype(B16)
        arrived[here, :] = low
        dyn_sums[0:8, :] += eight_rows(low.astype(F32))
        dyn_sums[8:16, :] += eight_rows(by_n)
        dyn_sums[16:24, :] += eight_rows(norm_grad)
        pre[0:CHUNK, :] = dot(low, wd[...], NT)
        layer_backward(pre, CHUNK, vec[4, 0:1, :], n2_0, d2_0, scales, 1, at, spg_0, at, sums.at[1], 24)
        pre[0:CHUNK, :] = dot(spg_0[here, :], wm0[...], NT)
        layer_backward(pre, CHUNK, vec[1, 0:1, :], n1_0, d1_0, scales, 0, at, fpg_0, at, sums.at[1], 0)
        back_in = dot(fpg_0[here, :], wi0[...], NT)
        pg_copy(i).wait_recv()
        total = back_in[:, 0:lat] + ig[here, 0:lat] + pair_grad[here, :].astype(F32)
        lat_low[here, :] = total.astype(B16)

        @pl.when(section > 0)
        def _():
            back_copy(i).start()

        ig[here, 0:lat] = total
        grad_store(i).start()
        stat[8:16, :] += eight_rows(m[here, 1:2] * (total * total))
        ig[here, lat:in_width] += back_in[:, lat:in_width]
        return carry

    def small_copy(other):
        to = base + lax.rem(place + other, PEERS)
        return remote(small, small_recv.at[place], sm_s.at[other], sm_r.at[place], (section, to))

    def small_arrival(other):
        source = lax.rem(place + other, PEERS)
        return remote(small, small_recv.at[source], sm_s.at[other], sm_r.at[source], (section, base + source))

    def send_small():
        table_part = jnp.zeros((tasks, side_width), F32)
        for lo in (0, rows):
            table_part += split_dot_right(one_hot(lo, rows), ig[lo : lo + rows, lat:in_width], TN)
        small[0:tasks, 0:emb] = table_part[:, side_width - emb :]
        for t in range(3):
            line = jnp.sum(dyn_sums[8 * t : 8 * t + 8, :], 0, keepdims=True)
            for part in range(lat // LANES):
                row = tasks + t * (lat // LANES) + part
                small[row : row + 1, :] = line[:, part * LANES : (part + 1) * LANES]
        q_lines = [jnp.sum(q_sums[job], 0, keepdims=True) for job in range(3)]
        for h in range(heads):
            line = jnp.zeros((1, LANES), F32)
            for job in range(3):
                line += jnp.where(first_head + job == h + 1, q_lines[job], 0.0)
            row = tasks + 3 * (lat // LANES) + h
            small[row : row + 1, :] = line
        row = tasks + 3 * (lat // LANES) + heads
        lane = lax.broadcasted_iota(jnp.int32, (1, LANES), 1)
        count = jnp.sum(m[0:rows, 1:2], 0, keepdims=True)
        lat_square = jnp.sum(jnp.sum(stat[0:8, :], 0, keepdims=True), 1, keepdims=True)
        grad_square = jnp.sum(jnp.sum(stat[8:16, :], 0, keepdims=True), 1, keepdims=True)
        small[row : row + 1, :] = jnp.where(
            lane == 0, count, jnp.where(lane == 1, lat_square, jnp.where(lane == 2, grad_square, 0.0))
        )
        small_recv[place] = small[...]
        for other in range(1, PEERS):
            small_copy(other).start()

    load_cot.wait()
    lax.fori_loop(0, chunks, lat_sent, 0)

    def late(turn, carry):
        @pl.when((turn == 0) == (section == last))
        def _():
            lax.fori_loop(0, chunks, backward_chunk, 0)
            send_small()

        @pl.when((turn == 0) == (section < last))
        def _():
            weight_grads(jobs - 1, True)

        return carry

    lax.fori_loop(0, 2, late, 0)
    weight_grads(jnp.int32(3), False)

    def at_chip(z):
        return (section, base + 2 * z + core)

    def up_copy(t):
        return remote(half_0.at[t], gb.at[0, t], up_s.at[t], up_r.at[t], at_chip(jnp.minimum(chip + 1, CHIPS - 1)))

    def down_copy(t):
        return remote(half_0.at[t], gb.at[1, t], dn_s.at[t], dn_r.at[t], at_chip(jnp.maximum(chip - 1, 0)))

    @pl.when(chip > 0)
    def _():
        pl.semaphore_signal(up_ok, inc=1, device_id=at_chip(jnp.maximum(chip - 1, 0)), device_id_type=MESH)

    @pl.when(chip < CHIPS - 1)
    def _():
        pl.semaphore_signal(
            dn_ok, inc=1, device_id=at_chip(jnp.minimum(chip + 1, CHIPS - 1)), device_id_type=MESH
        )

    def hops(turn, carry):
        @pl.when(((turn == 0) == lower) & (chip < CHIPS - 1))
        def _():
            pl.semaphore_wait(up_ok, 1)
            for t in range(CHIPS - 1, 0, -1):
                @pl.when(t > chip)
                def _():
                    @pl.when(chip > 0)
                    def _():
                        up_copy(t).wait_recv()
                        add_rows(half_0.at[t], gb.at[0, t], block0)

                    up_copy(t).start()

        @pl.when(((turn == 0) != lower) & (chip > 0))
        def _():
            pl.semaphore_wait(dn_ok, 1)
            for t in range(CHIPS - 1):
                @pl.when(t < chip)
                def _():
                    @pl.when(chip < CHIPS - 1)
                    def _():
                        down_copy(t).wait_recv()
                        add_rows(half_0.at[t], gb.at[1, t], block0)

                    down_copy(t).start()

        return carry

    lax.fori_loop(0, 2, hops, 0)

    for other in range(1, PEERS):
        small_arrival(other).wait_recv()
    total = small_recv[0]
    for source in range(1, PEERS):
        total = total + small_recv[source]
    for other in range(1, PEERS):
        small_copy(other).wait_send()
    small[...] = total
    table_recv[section] = small[0:tasks, :]

    def table_copy(other):
        to = lax.rem(section + other, steps)
        return remote(
            small.at[0:tasks], table_recv.at[section], tb_s.at[other], tb_r.at[section], (to, d)
        )

    def table_arrival(other):
        source = lax.rem(section + other, steps)
        return remote(small.at[0:tasks], table_recv.at[source], tb_s.at[other], tb_r.at[source], (source, d))

    for other in range(1, steps):
        table_copy(other).start()

    side_copy.wait_send()
    meta_copy.wait_send()

    def sends(i, carry):
        pair_copy(i).wait_send()
        pg_copy(i).wait_send()
        grad_store(i).wait()

        @pl.when(section > 0)
        def _():
            back_copy(i).wait_send()

        return carry

    lax.fori_loop(0, chunks, sends, 0)

    def job_done(job, carry):
        def body(other, carry):
            owner_copy(job, lax.rem(chip + other, CHIPS)).wait_send()
            return carry

        lax.fori_loop(1, CHIPS, body, 0)
        keep_copy(job).wait()
        return carry

    lax.fori_loop(0, jobs, job_done, 0)
    for head in range(heads):
        for half in range(2):
            source = (0, CHIPS - 1)[half] if head < 2 else (1, CHIPS - 2)[half]

            @pl.when(chip != source)
            def _():
                remote(
                    half_q.at[0, 0], recv_q.at[head, half], rb_s.at[0, 0], rb_r.at[head, half], at_chip(source)
                ).wait_recv()

    @pl.when(chip > 0)
    def _():
        up_copy(chip).wait_recv()
        add_rows(half_0.at[chip], gb.at[0, chip], block0)

    @pl.when(chip < CHIPS - 1)
    def _():
        down_copy(chip).wait_recv()
        add_rows(half_0.at[chip], gb.at[1, chip], block0)

    keep_0 = pltpu.make_async_copy(half_0.at[chip], recv_0, own_s.at[3])
    keep_0.start()
    for t in range(CHIPS):
        @pl.when(t > chip)
        def _():
            up_copy(t).wait_send()

        @pl.when(t < chip)
        def _():
            down_copy(t).wait_send()

    for other in range(1, steps):
        table_arrival(other).wait_recv()
    for other in range(1, steps):
        table_copy(other).wait_send()
    whole = table_recv[0]
    for source in range(1, steps):
        whole = whole + table_recv[source]
    small[0:tasks, :] = whole
    done = pltpu.make_async_copy(small, small_out, out_sem.at[2 * chunks])
    done.start()
    done.wait()
    keep_0.wait()


def finish_kernel(dims, *refs):
    lat, in_width, hid, heads, bins, tasks, emb = dims
    block = in_width + hid + LANES + VECS
    block0 = in_width + hid + lat + VECS
    at_out = in_width + hid
    recv_q, recv_0, small, lat_in, grad_in = refs[:5]
    lat_out, grad_out, w_in, w_mid, w_dyn, w_q, b_dyn, g_dyn, s_dyn, b_q, table, rms = refs[5:17]
    vecs = refs[17:23]
    sem = refs[23]
    copies = [
        pltpu.make_async_copy(lat_in, lat_out, sem.at[0]),
        pltpu.make_async_copy(grad_in, grad_out, sem.at[1]),
    ]
    for copy in copies:
        copy.start()

    def total(h, lo, hi):
        if h == 0:
            return recv_0[lo:hi, :].astype(F32)
        return recv_q[h - 1, 0, lo:hi, :].astype(F32) + recv_q[h - 1, 1, lo:hi, :].astype(F32)

    for h in range(heads + 1):
        w_in[h] = total(h, 0, in_width)
        w_mid[h] = total(h, in_width, at_out)
        size = block if h else block0
        lines = total(h, size - VECS, size)
        for t in range(6):
            vecs[t][h] = lines[t : t + 1, :]
        if h:
            w_q[h - 1] = total(h, at_out, at_out + LANES)[0:bins, :]
    for t in range(lat // LANES):
        w_dyn[:, t * LANES : (t + 1) * LANES] = total(0, at_out + t * LANES, at_out + (t + 1) * LANES)
    table[...] = small[0:tasks, 0:emb]
    for t, out in enumerate((b_dyn, g_dyn, s_dyn)):
        for part in range(lat // LANES):
            row = tasks + t * (lat // LANES) + part
            out[0:1, part * LANES : (part + 1) * LANES] = small[row : row + 1, :]
    at_q = tasks + 3 * (lat // LANES)
    for h in range(heads):
        b_q[h] = small[at_q + h : at_q + h + 1, 0:bins]
    stat = small[at_q + heads : at_q + heads + 1, :]
    count = stat[:, 0:1]
    squares = jnp.concatenate([stat[:, 1:2] / count, stat[:, 2:3] / (count * lat)], 1)
    rms[...] = jnp.sqrt(squares)
    for copy in copies:
        copy.wait()


def on_device(
    latent_in, actions, task_ids, valid, action_mask, bins, fraction, latent_cot,
    w_in, b_in, g_in, beta_in, w_mid, b_mid, g_mid, beta_mid,
    w_dyn_out, b_dyn_out, g_dyn_out, beta_dyn_out, w_q_out, b_q_out, table,
):
    steps = lax.axis_size("section")
    spread = lax.axis_size("dp")
    groups = spread // PEERS
    rows, lat = latent_in.shape
    act_width = actions.shape[2]
    in_width, hid = w_in.shape[2:]
    heads = w_q_out.shape[1]
    bin_count = w_q_out.shape[-1]
    tasks, emb = table.shape
    block = in_width + hid + LANES + VECS
    block0 = in_width + hid + lat + VECS
    chunks = rows // CHUNK
    small_rows = tasks + 24
    dims = (rows, lat, act_width, in_width, hid, heads, bin_count, tasks, emb, steps)
    anywhere = pl.BlockSpec(memory_space=pl.ANY)
    vmem = pl.BlockSpec(memory_space=pltpu.VMEM)
    dma = pltpu.SemaphoreType.DMA
    both = 2 * rows
    wide = pltpu.VMEM((rows, hid), B16)
    thin = pltpu.VMEM((rows, LANES), F32)
    low = pltpu.VMEM((rows, lat), B16)
    part_low = pltpu.VMEM((QROWS, hid), B16)
    q_wide = pltpu.VMEM((both, hid), B16)
    lat_out, grad_out, recv_q, recv_0, small = pl.pallas_call(
        functools.partial(step_kernel, dims),
        out_shape=[
            jax.ShapeDtypeStruct((rows, lat), B16),
            jax.ShapeDtypeStruct((rows, lat), F32),
            jax.ShapeDtypeStruct((heads, 2, block, LANES), B16),
            jax.ShapeDtypeStruct((block0, LANES), B16),
            jax.ShapeDtypeStruct((small_rows, LANES), F32),
        ],
        in_specs=[anywhere] + [vmem] * 7 + [anywhere] * 5 + [vmem] * 10,
        out_specs=[anywhere] * 5,
        scratch_shapes=[
            pltpu.VMEM((both, 6 * LANES), B16),
            pltpu.VMEM((both, LANES), F32),
            pltpu.VMEM((2, in_width, hid), B16),
            pltpu.VMEM((2, hid, hid), B16),
            pltpu.VMEM((2, LANES, hid), B16),
            pltpu.VMEM((2, bin_count, hid), B16),
            pltpu.VMEM((in_width, hid), B16),
            pltpu.VMEM((hid, hid), B16),
            pltpu.VMEM((hid, lat), B16),
            pltpu.VMEM((6, 8, hid), F32),
            pltpu.VMEM((8, LANES), F32),
            pltpu.VMEM((lat, lat), B16),
            pltpu.VMEM((both, in_width), F32),
            q_wide, q_wide, q_wide, q_wide,
            pltpu.VMEM((both, LANES), B16),
            part_low, part_low, part_low, part_low,
            pltpu.VMEM((QROWS, LANES), F32),
            pltpu.VMEM((QROWS, hid), F32),
            wide, wide, wide, wide, wide, wide, wide, wide, thin,
            low,
            pltpu.VMEM((rows, lat), F32),
            low, low, low, low, low,
            pltpu.VMEM((2, CHIPS, block0, LANES), B16),
            pltpu.VMEM((3, CHIPS, block, LANES), B16),
            pltpu.VMEM((CHIPS, block0, LANES), B16),
            pltpu.VMEM((2, 48, hid), F32),
            pltpu.VMEM((3, 8, LANES), F32),
            pltpu.VMEM((24, lat), F32),
            pltpu.VMEM((16, lat), F32),
            pltpu.VMEM((small_rows, LANES), F32),
            pltpu.VMEM((PEERS, small_rows, LANES), F32),
            pltpu.VMEM((steps, tasks, LANES), F32),
            dma((10,)), dma((chunks,)), dma((2 * chunks + 1,)),
            dma((chunks,)), dma((chunks,)), dma((chunks,)), dma((chunks,)),
            dma((2,)), dma((2,)), dma((chunks,)), dma((chunks,)), dma((chunks,)), dma((chunks,)),
            dma((4, CHIPS)), dma((4, CHIPS)), dma((4,)), dma((3, CHIPS)), dma((heads, 2)),
            dma((PEERS,)), dma((PEERS,)), dma((steps,)), dma((steps,)),
            dma((CHIPS,)), dma((CHIPS,)), dma((CHIPS,)), dma((CHIPS,)),
            pltpu.SemaphoreType.REGULAR, pltpu.SemaphoreType.REGULAR,
        ],
        compiler_params=pltpu.CompilerParams(
            collective_id=0, has_side_effects=True, vmem_limit_bytes=16350 * 2**12
        ),
        name="step",
    )(
        latent_in, actions[0].T, task_ids[None], valid[None], bins, fraction,
        action_mask.T, table, latent_cot[0],
        w_in[0], w_mid[0], w_dyn_out[0], w_q_out[0].transpose(0, 2, 1),
        b_in[0], g_in[0], beta_in[0], b_mid[0], g_mid[0], beta_mid[0],
        b_dyn_out, g_dyn_out, beta_dyn_out, b_q_out[0],
    )
    across = [[q * PEERS + r for q in range(groups)] for r in range(PEERS)]
    if groups > 1:
        small = lax.psum(small, "dp", axis_index_groups=across)

    def shape(*dims):
        return jax.ShapeDtypeStruct(dims, F32)

    lat_out, grad_out, part_in, part_mid, part_dyn, part_q, b_dyn, g_dyn, s_dyn, q_bias, grad_table, rms, *vecs = (
        pl.pallas_call(
            functools.partial(finish_kernel, (lat, in_width, hid, heads, bin_count, tasks, emb)),
            out_shape=[
                jax.ShapeDtypeStruct((rows, lat), B16),
                shape(rows, lat),
                shape(heads + 1, in_width, LANES),
                shape(heads + 1, hid, LANES),
                shape(LANES, lat),
                shape(heads, bin_count, LANES),
                shape(1, lat), shape(1, lat), shape(1, lat),
                shape(heads, 1, bin_count),
                shape(tasks, emb),
                shape(1, 2),
            ] + [shape(heads + 1, 1, LANES)] * 6,
            in_specs=[vmem] * 3 + [anywhere] * 2,
            out_specs=[anywhere] * 2 + [vmem] * 16,
            scratch_shapes=[dma((2,))],
            compiler_params=pltpu.CompilerParams(vmem_limit_bytes=40 * 2**20),
            name="finish",
        )(recv_q, recv_0, small, lat_out, grad_out)
    )

    def owned(piece, dim):
        if groups == 1:
            return piece
        piece = lax.psum_scatter(piece, "dp", scatter_dimension=dim, axis_index_groups=across, tiled=True)
        moves = [(q * PEERS + r, r * groups + q) for q in range(groups) for r in range(PEERS)]
        return lax.ppermute(piece, "dp", moves)

    part_in, part_mid, part_q = owned(part_in, 2), owned(part_mid, 2), owned(part_q, 2)
    part_dyn = owned(part_dyn, 0)
    vecs = [owned(v, 2).transpose(1, 0, 2) for v in vecs]
    return (
        lat_out[None],
        grad_out[None],
        part_in[None],
        *vecs[:3],
        part_mid[None],
        *vecs[3:],
        part_dyn[None],
        b_dyn,
        g_dyn,
        s_dyn,
        part_q.transpose(0, 2, 1)[None],
        q_bias.transpose(1, 0, 2),
        grad_table,
        rms,
    )


def solution(mesh):
    placed = (
        P("dp", None),
        P("section", "dp", None),
        P("dp"),
        P("dp"),
        P(),
        P("section", "dp"),
        P("section", "dp"),
        P("section", "dp", None),
        P("section", None, None, None),
        P("section", None, None),
        P("section", None, None),
        P("section", None, None),
        P("section", None, None, None),
        P("section", None, None),
        P("section", None, None),
        P("section", None, None),
        P("section", None, None),
        P("section", None),
        P("section", None),
        P("section", None),
        P("section", None, None, None),
        P("section", None, None),
        P(),
    )
    return jax.shard_map(
        on_device,
        mesh=mesh,
        in_specs=placed,
        out_specs=(
            P("section", "dp", None),
            P("section", "dp", None),
            P("section", None, None, "dp"),
            P("section", None, "dp"),
            P("section", None, "dp"),
            P("section", None, "dp"),
            P("section", None, None, "dp"),
            P("section", None, "dp"),
            P("section", None, "dp"),
            P("section", None, "dp"),
            P("section", "dp", None),
            P("section", None),
            P("section", None),
            P("section", None),
            P("section", None, "dp", None),
            P("section", None, None),
            P(),
            P("section", None),
        ),
        check_vma=False,
    )
```

```python
import functools

import jax
import jax.numpy as jnp
from jax import lax
from jax.experimental import pallas as pl
from jax.experimental.pallas import tpu as pltpu
from jax.sharding import PartitionSpec as P

GROUP = 8
EPS = 1e-05
F32 = jnp.float32
B16 = jnp.bfloat16
MESH = pl.DeviceIdType.MESH

LANES = 128
CHIPS = 4
PEERS = 2 * CHIPS
CHUNK = 128
QROWS = 256
SUB = 256
VECS = 16

NN = (((1,), (0,)), ((), ()))
NT = (((1,), (1,)), ((), ()))
TN = (((0,), (0,)), ((), ()))


def dot(a, b, dims=NN):
    return lax.dot_general(a, b, dims, preferred_element_type=F32)


def split_dot(a, b, dims=NN):
    high = a.astype(B16)
    low = (a - high.astype(F32)).astype(B16)
    return dot(high, b, dims) + dot(low, b, dims)


def split_dot_right(a, b, dims):
    high = b.astype(B16)
    low = (b - high.astype(F32)).astype(B16)
    return dot(a, high, dims) + dot(a, low, dims)


def norm_mish(x, gain, shift):
    center = x - jnp.mean(x, -1, keepdims=True)
    spread = jnp.mean(center * center, -1, keepdims=True)
    scale = lax.rsqrt(spread + EPS)
    n = center * scale
    u = n * gain + shift
    w = jnp.exp(jnp.minimum(u, 30.0))
    top = w * (w + 2.0)
    over = pltpu.reciprocal(top + 2.0, approx=True)
    act = u * (top * over)
    slope = (top + 4.0 * (u * (top - w)) * over) * (over * gain)
    return act, n, slope, scale


def padded(count):
    return (count + 15) // 16 * 16


def tiles(size, step=256):
    return [(lo, min(lo + step, size)) for lo in range(0, size, step)]


def eight_rows(x):
    return x.reshape(x.shape[0] // 8, 8, x.shape[1]).sum(0)


def each_sub(count, body):
    sub = min(SUB, count)
    for j in range(0, count, sub):
        body(j, sub)


def layer_forward(pre, count, bias, gain, shift, act_ref, act_at, n_ref, slope_ref, scale_ref, lane, at):
    def body(j, sub):
        x = pre[pl.ds(j, sub), :]
        if bias is not None:
            x = x + bias
        act, n, slope, scale = norm_mish(x, gain, shift)
        act_ref[pl.ds(act_at + j, sub), :] = act.astype(B16)
        here = pl.ds(at + j, sub)
        n_ref[here, :] = n.astype(n_ref.dtype)
        slope_ref[here, :] = slope.astype(slope_ref.dtype)
        scale_ref[here, lane : lane + 1] = scale

    each_sub(count, body)


def layer_backward(pre, count, n_ref, slope_ref, scale_ref, lane, at, out_ref, out_at, sums, first):
    def body(j, sub):
        here = pl.ds(at + j, sub)
        n = n_ref[here, :].astype(F32)
        dn = pre[pl.ds(j, sub), :] * slope_ref[here, :].astype(F32)
        by_n = dn * n
        mean_dn = jnp.mean(dn, -1, keepdims=True)
        mean_by_n = jnp.mean(by_n, -1, keepdims=True)
        out = (dn - mean_dn - n * mean_by_n) * scale_ref[here, lane : lane + 1]
        out_ref[pl.ds(out_at + j, sub), :] = out.astype(B16)
        sums[first : first + 8, :] += eight_rows(by_n)
        sums[first + 8 : first + 16, :] += eight_rows(dn)

    each_sub(count, body)


def step_kernel(dims, *refs):
    rows, lat, act_width, in_width, hid, heads, bins, tasks, emb, steps = dims
    side_width = in_width - lat
    at_mid = in_width + VECS
    at_out = at_mid + hid
    block = at_out + padded(bins)
    block0 = at_out + lat
    both = 2 * rows
    ones_at = in_width // LANES * LANES
    pieces = ((0, at_mid), (at_mid, at_out), (at_out, block0))
    (
        lat_in, acts, task, valid, bin_at, part_of, amask, table, cot_in, w_in, w_mid, w_dyn, w_q,
        b_in, g_in, s_in, b_mid, g_mid, s_mid, b_dyn, g_dyn, s_dyn, b_q,
        lat_out, grad_out, recv_q, recv_0, small_out,
        x, m, wi, wm, wq, wq_raw, wi0, wm0, wd, vec, bq, diag,
        lines, acting, vec_lines, ig, act1, act2, spg, fpg, qg, n1, d1, n2, d2, q_scales, pre,
        act1_0, act2_0, spg_0, fpg_0, n1_0, d1_0, n2_0, d2_0, scales,
        dyn_n, new_lat, lat_low, cot, arrived, pair_grad, pair_send,
        gb, half_q, half_0, sums, q_sums, dyn_sums, stat, small, small_mate, small_chips, small_half, small_steps, small_done,
        w_sem, in_sem, out_sem, lat_s, lat_r, px_s, px_r, side_s, side_r, pg_s, pg_r, gr_s, gr_r,
        half_s, half_r, own_s, rb_s, rb_r, sm_s, sm_r, ch_s, ch_r, tb_s, tb_r, up_s, up_r, dn_s, dn_r, up_ok, dn_ok,
    ) = refs
    section = lax.axis_index("section")
    d = lax.axis_index("dp")
    place = lax.rem(d, PEERS)
    base = d - place
    chip = place // 2
    core = lax.rem(place, 2)
    edge = (chip == 0) | (chip == CHIPS - 1)
    lower = chip < CHIPS // 2
    side_of = chip // 2
    last = steps - 1
    mate = base + chip * 2 + (1 - core)
    pair = base + (chip + 1 - 2 * lax.rem(chip, 2)) * 2 + core
    following = jnp.minimum(section + 1, last)
    before = jnp.maximum(section - 1, 0)
    chunks = rows // CHUNK
    jobs = jnp.where(edge, 2, 3)
    first_head = jnp.where(edge, 1, 3)

    def remote(src, dst, send, recv, to):
        return pltpu.make_async_remote_copy(
            src_ref=src, dst_ref=dst, send_sem=send, recv_sem=recv, device_id=to, device_id_type=MESH
        )

    def chunk_at(i):
        return pl.multiple_of(i * CHUNK, CHUNK)

    loads = [
        pltpu.make_async_copy(w_in.at[0], wi0.at[0:in_width], w_sem.at[0]),
        pltpu.make_async_copy(w_mid.at[0], wm0, w_sem.at[1]),
        pltpu.make_async_copy(w_dyn, wd, w_sem.at[2]),
    ]

    def job_loads(job):
        slot = lax.rem(job, 2)
        h = first_head + job
        return [
            pltpu.make_async_copy(w_in.at[h], wi.at[slot, 0:in_width], w_sem.at[3 + 3 * slot]),
            pltpu.make_async_copy(w_mid.at[h], wm.at[slot], w_sem.at[4 + 3 * slot]),
            pltpu.make_async_copy(w_q.at[h - 1], wq_raw.at[slot], w_sem.at[5 + 3 * slot]),
        ]

    load_cot = pltpu.make_async_copy(cot_in, cot, w_sem.at[9])

    def load_lat(i):
        here = pl.ds(chunk_at(i), CHUNK)
        return pltpu.make_async_copy(lat_in.at[here], x.at[here, 0:lat], in_sem.at[i])

    barrier = pltpu.get_barrier_semaphore()
    for other in range(1, PEERS):
        to = base + lax.rem(place + other, PEERS)
        pl.semaphore_signal(barrier, inc=1, device_id=(section, to), device_id_type=MESH)
    for other in range(1, steps):
        to = lax.rem(section + other, steps)
        pl.semaphore_signal(barrier, inc=1, device_id=(to, d), device_id_type=MESH)

    loads[0].start()

    @pl.when(section == 0)
    def _():
        for i in range(chunks):
            load_lat(i).start()

    for copy in loads[1:] + job_loads(jnp.int32(0)) + job_loads(jnp.int32(1)):
        copy.start()
    load_cot.start()

    head_lines = [task[...].astype(F32), valid[...].astype(F32), bin_at[...].astype(F32), part_of[...]]
    lines[0] = jnp.concatenate(head_lines + [jnp.zeros((4, rows), F32)], 0)
    acting[0] = acts[...]

    def one_hot(lo, count):
        task_lane = lax.broadcasted_iota(jnp.int32, (count, tasks), 1).astype(F32)
        return (m[lo : lo + count, 0:1] == task_lane).astype(F32).astype(B16)

    def prepare(which):
        lo = which * rows
        m[lo : lo + rows, 0:8] = lines[which].T
        hot = one_hot(lo, rows)
        mask = dot(amask[...].astype(F32).astype(B16), hot, NT)
        used = (acting[which].astype(F32) * mask).T
        x[lo : lo + rows, lat:in_width] = jnp.concatenate(
            [used.astype(B16), dot(hot, table[...]).astype(B16)], 1
        )

    lane = lax.broadcasted_iota(jnp.int32, (both, LANES), 1)
    x[:, ones_at : ones_at + LANES] = (lane == in_width - ones_at).astype(F32).astype(B16)
    prepare(0)
    for t, source in enumerate((b_in, g_in, s_in, b_mid, g_mid, s_mid)):
        vec[t, 0 : heads + 1, :] = source[...].astype(F32)
    shift = GROUP.bit_length() - 1
    diag[...] = (
        lax.shift_right_logical(lax.broadcasted_iota(jnp.int32, (lat, lat), 0), shift)
        == lax.shift_right_logical(lax.broadcasted_iota(jnp.int32, (lat, lat), 1), shift)
    ).astype(F32).astype(B16)

    def bias_rows(h):
        line = lax.broadcasted_iota(jnp.int32, (VECS, hid), 0)
        return jnp.where(line == 0, vec[0, pl.ds(h, 1), :], 0.0).astype(B16)

    wi0[in_width:at_mid, :] = bias_rows(0)
    stat[...] = jnp.zeros(stat.shape, F32)

    def clear():
        bq[...] = jnp.full(bq.shape, -1e30, F32)
        bq[0:heads, 0:bins] = b_q[...].astype(F32)
        wq[...] = jnp.zeros(wq.shape, B16)
        sums[...] = jnp.zeros(sums.shape, F32)
        ig[...] = jnp.zeros(ig.shape, F32)
        q_sums[...] = jnp.zeros(q_sums.shape, F32)
        dyn_sums[...] = jnp.zeros(dyn_sums.shape, F32)
        small[...] = jnp.zeros(small.shape, F32)

    pl.semaphore_wait(barrier, PEERS - 1 + steps - 1)

    side_copies = [
        remote(lines.at[0], lines.at[1], side_s.at[0], side_r.at[0], (section, pair)),
        remote(acting.at[0], acting.at[1], side_s.at[1], side_r.at[1], (section, pair)),
    ]
    for copy in side_copies:
        copy.start()

    def settle():
        clear()
        for copy in side_copies:
            copy.wait_recv()
        prepare(1)

    @pl.when(section == last)
    def _():
        arrived[...] = jnp.zeros(arrived.shape, B16)

    @pl.when(section > 0)
    def _():
        settle()

    for copy in loads:
        copy.wait()

    def vec_of(t, h):
        return vec[t, pl.ds(h, 1), :]

    def lat_copy(i):
        here = pl.ds(chunk_at(i), CHUNK)
        return remote(
            lat_low.at[here], x.at[here, 0:lat], lat_s.at[i], lat_r.at[i], (following, d)
        )

    def pair_copy(i):
        here = chunk_at(i)
        return remote(
            x.at[pl.ds(here, CHUNK), 0:lat], x.at[pl.ds(rows + here, CHUNK), 0:lat],
            px_s.at[i], px_r.at[i], (section, pair),
        )

    def lat_store(i):
        here = pl.ds(chunk_at(i), CHUNK)
        return pltpu.make_async_copy(lat_low.at[here], lat_out.at[here], out_sem.at[i])

    def forward_chunk(i, carry):
        at = chunk_at(i)
        here = pl.ds(at, CHUNK)

        @pl.when(section > 0)
        def _():
            lat_copy(i).wait_recv()

        @pl.when(section == 0)
        def _():
            load_lat(i).wait()

        pair_copy(i).start()
        pre[0:CHUNK, :] = dot(x[here, 0:at_mid], wi0[...])
        layer_forward(
            pre, CHUNK, None, vec[1, 0:1, :], vec[2, 0:1, :], act1_0, at, n1_0, d1_0, scales, 0, at
        )
        pre[0:CHUNK, :] = dot(act1_0[here, :], wm0[...])
        layer_forward(
            pre, CHUNK, vec[3, 0:1, :], vec[4, 0:1, :], vec[5, 0:1, :], act2_0, at, n2_0, d2_0, scales, 1, at
        )
        out = dot(act2_0[here, :], wd[...]) + b_dyn[...].astype(F32)
        center = out - jnp.mean(out, -1, keepdims=True)
        scale = lax.rsqrt(jnp.mean(center * center, -1, keepdims=True) + EPS)
        normal = center * scale
        dyn_n[here, :] = normal.astype(B16)
        scales[here, 2:3] = scale
        power = jnp.exp(normal * g_dyn[...].astype(F32) + s_dyn[...].astype(F32))
        fresh = power * pltpu.reciprocal(split_dot(power, diag[...]), approx=True)
        new_lat[here, :] = fresh
        low = fresh.astype(B16)
        lat_low[here, :] = low

        @pl.when(section < last)
        def _():
            lat_copy(i).start()

        lat_store(i).start()
        wide = low.astype(F32)
        stat[0:8, :] += eight_rows(m[here, 1:2] * (wide * wide))
        return carry

    lax.fori_loop(0, chunks, forward_chunk, 0)

    @pl.when(section == 0)
    def _():
        settle()

    def pg_copy(i):
        here = pl.ds(chunk_at(i), CHUNK)
        return remote(
            pair_send.at[here], pair_grad.at[here], pg_s.at[i], pg_r.at[i], (section, pair)
        )

    def q_chunk(job, at):
        here = pl.ds(at, QROWS)
        h = first_head + job
        slot = lax.rem(job, 2)
        pre[...] = dot(x[here, 0:at_mid], wi[slot])
        layer_forward(
            pre, QROWS, None, vec_of(1, h), vec_of(2, h), act1, at, n1, d1, q_scales, 0, 0
        )
        pre[...] = dot(act1[here, :], wm[slot])
        layer_forward(
            pre, QROWS, vec_of(3, h), vec_of(4, h), vec_of(5, h), act2, at, n2, d2, q_scales, 1, 0
        )
        logits = dot(act2[here, :], wq[slot], NT) + bq[pl.ds(h - 1, 1), :]
        power = jnp.exp(logits - jnp.max(logits, -1, keepdims=True))
        chance = power / jnp.sum(power, -1, keepdims=True)
        lane = lax.broadcasted_iota(jnp.int32, (QROWS, LANES), 1).astype(F32)
        low_bin = m[here, 2:3]
        part = m[here, 3:4]
        target = jnp.where(lane == low_bin, 1.0 - part, 0.0) + jnp.where(lane == low_bin + 1.0, part, 0.0)
        grad = (m[here, 1:2] * (chance - target)).astype(B16)
        qg[here, :] = grad
        q_sums[job] += eight_rows(grad.astype(F32))
        pre[...] = dot(grad, wq[slot])
        layer_backward(pre, QROWS, n2, d2, q_scales, 1, 0, spg, at, sums.at[0], 16)
        pre[...] = dot(spg[here, :], wm[slot], NT)
        layer_backward(pre, QROWS, n1, d1, q_scales, 0, 0, fpg, at, sums.at[0], 0)
        for lo, hi in tiles(in_width):
            ig[here, lo:hi] += dot(fpg[here, :], wi[slot, lo:hi, :], NT)

    q_chunks = both // QROWS
    own_chunks = rows // QROWS

    def q_job(job):
        for copy in job_loads(job):
            copy.wait()
        slot = lax.rem(job, 2)
        wq[slot, 0:bins, :] = wq_raw[slot]
        wi[slot, in_width:at_mid, :] = bias_rows(first_head + job)
        sums[0] = jnp.zeros(sums.shape[1:], F32)

        def body(i, carry):
            which = lax.rem(i + jnp.where(job == 0, 0, own_chunks), q_chunks)
            at = pl.multiple_of(which * QROWS, QROWS)

            @pl.when((job == 0) & (which == own_chunks))
            def _():
                def pair_here(j, carry):
                    pair_copy(j).wait_recv()
                    return carry

                lax.fori_loop(0, chunks, pair_here, 0)

            q_chunk(job, at)

            @pl.when((job == jobs - 1) & (which >= own_chunks))
            def _():
                for k in range(QROWS // CHUNK):
                    j = (which - own_chunks) * (QROWS // CHUNK) + k
                    to = chunk_at(j)
                    pair_send[pl.ds(to, CHUNK), :] = ig[pl.ds(rows + to, CHUNK), 0:lat].astype(B16)
                    pg_copy(j).start()

            return carry

        lax.fori_loop(0, q_chunks, body, 0)

        @pl.when(job + 2 < jobs)
        def _():
            for copy in job_loads(job + 2):
                copy.start()

    def half_copy(job, z, q):
        if q:
            src, dst = gb.at[1 - core, z, 0:block], half_q.at[job, z]
        else:
            src, dst = gb.at[1 - core, z], half_0.at[z]
        return remote(src, dst, half_s.at[job, z], half_r.at[job, z], (section, mate))

    def owner_copy(job, z):
        head = first_head + job - 1
        return remote(
            half_q.at[job, z], recv_q.at[head, side_of], rb_s.at[job, z], rb_r.at[head, side_of],
            (section, base + 2 * z + core),
        )

    def keep_copy(job):
        return pltpu.make_async_copy(
            half_q.at[job, chip], recv_q.at[first_head + job - 1, side_of], own_s.at[job]
        )

    def add_rows(dst, src, size):
        step = size // 4 // 16 * 16
        for part in range(4):
            span = slice(part * step, size if part == 3 else (part + 1) * step)
            dst[span, :] = (dst[span, :].astype(F32) + src[span, :].astype(F32)).astype(B16)

    def at_chip(z):
        return (section, base + 2 * z + core)

    def stripe(z):
        return pl.ds(pl.multiple_of(z * LANES, LANES), LANES)

    def up_piece(z, p):
        size = pieces[p][1] - pieces[p][0]
        return (act1.at[0:size, stripe(z)], act1.at[0:size, stripe(CHIPS + z)], act2.at[0:size, stripe(z)])[p]

    def down_piece(z, p):
        size = pieces[p][1] - pieces[p][0]
        return (spg.at[0:size, stripe(z)], spg.at[0:size, stripe(CHIPS + z)], act2.at[0:size, stripe(CHIPS + z)])[p]

    def up_copy(z, p):
        return remote(
            half_0.at[z, pieces[p][0] : pieces[p][1]], up_piece(z, p), up_s.at[z, p], up_r.at[z, p],
            at_chip(jnp.minimum(chip + 1, CHIPS - 1)),
        )

    def down_copy(z, p):
        return remote(
            half_0.at[z, pieces[p][0] : pieces[p][1]], down_piece(z, p), dn_s.at[z, p], dn_r.at[z, p],
            at_chip(jnp.maximum(chip - 1, 0)),
        )

    def add_piece(piece, z, p):
        lo, hi = pieces[p]
        half_0[z, lo:hi, :] = (half_0[z, lo:hi, :].astype(F32) + piece(z, p)[...].astype(F32)).astype(B16)

    def weight_grads(job, q):
        if q:
            count, a1, a2, sp, fp, own_sums = both, act1, act2, spg, fpg, 0
        else:
            count, a1, a2, sp, fp, own_sums = rows, act1_0, act2_0, spg_0, fpg_0, 1
        size = block if q else block0
        h = first_head + job if q else 0
        line_at = lax.broadcasted_iota(jnp.int32, (VECS, hid), 0)
        vectors = jnp.zeros((VECS, hid), F32)
        for t, (first, gain) in enumerate(((0, 1), (8, 1), (None, None), (16, 4), (24, 4))):
            if gain is not None:
                line = jnp.sum(sums[own_sums, first : first + 8, :], 0, keepdims=True) / vec_of(gain, h)
                vectors = jnp.where(line_at == t + 1, line, vectors)
        vec_lines[...] = vectors
        row_at = lax.broadcasted_iota(jnp.int32, (VECS, 2 * LANES), 0)

        def order(i):
            far_first = jnp.where(lower, CHIPS - 1 - i, i)
            pair_first = lax.rem(jnp.where(lower, CHIPS - i, i + CHIPS - 1), CHIPS)
            return jnp.where(edge, far_first, pair_first)

        def make(z):
            cols = pl.ds(pl.multiple_of(z * 2 * LANES, 2 * LANES), 2 * LANES)
            for left, right, first, size_of in ((x, fp, 0, at_mid), (a1, sp, at_mid, hid)):
                for lo, hi in tiles(size_of):
                    grad = dot(left[0:count, lo:hi], right[0:count, cols], TN)
                    if left is x and hi == at_mid:
                        plain = grad[0 : in_width - lo]
                        bias_mid = dot(x[0:count, ones_at : ones_at + LANES], sp[0:count, cols], TN)
                        bias_mid = bias_mid[in_width - ones_at : in_width - ones_at + 1]
                        lines_here = grad[in_width - lo :] + vec_lines[:, cols]
                        grad = jnp.concatenate([plain, jnp.where(row_at == 3, bias_mid, lines_here)], 0)
                    for p in range(2):
                        gb[p, z, first + lo : first + hi, :] = grad[:, p * LANES : (p + 1) * LANES].astype(B16)
            if q:
                g_out = dot(qg[0:count, :], a2[0:count, cols], TN)
                for p in range(2):
                    gb[p, z, at_out:block, :] = g_out[0 : block - at_out, p * LANES : (p + 1) * LANES].astype(B16)
            else:
                g_out = dot(a2[0:count, cols], arrived[0:count, :], TN)
                for p in range(2):
                    for t in range(lat // LANES):
                        gb[p, z, at_out + t * LANES : at_out + (t + 1) * LANES, :] = g_out[
                            p * LANES : (p + 1) * LANES, t * LANES : (t + 1) * LANES
                        ].astype(B16)
            half_copy(job, z, q).start()

        def finish(z):
            half_copy(job, z, q).wait_recv()
            if q:
                add_rows(half_q.at[job, z], gb.at[core, z], size)

                @pl.when(z != chip)
                def _():
                    owner_copy(job, z).start()

                @pl.when(z == chip)
                def _():
                    keep_copy(job).start()
            else:
                add_rows(half_0.at[z], gb.at[core, z], size)

                @pl.when((chip == 0) & (z != chip))
                def _():
                    for p in range(3):
                        up_copy(z, p).start()

                @pl.when((chip == CHIPS - 1) & (z != chip))
                def _():
                    for p in range(3):
                        down_copy(z, p).start()

        def body(i, carry):
            @pl.when(i < CHIPS)
            def _():
                make(order(i))

            if not q:
                @pl.when(i == 1)
                def _():
                    small_over_chips()

            @pl.when(i > 0)
            def _():
                finish(order(i - 1))

            return carry

        lax.fori_loop(0, CHIPS + 1, body, 0)

        def sent(z, carry):
            half_copy(job, z, q).wait_send()
            return carry

        lax.fori_loop(0, CHIPS, sent, 0)

    def back_copy(i):
        here = pl.ds(chunk_at(i), CHUNK)
        return remote(lat_low.at[here], arrived.at[here], gr_s.at[i], gr_r.at[i], (before, d))

    def grad_store(i):
        here = pl.ds(chunk_at(i), CHUNK)
        return pltpu.make_async_copy(ig.at[here, 0:lat], grad_out.at[here], out_sem.at[chunks + i])

    def lat_sent(i, carry):
        lat_store(i).wait()

        @pl.when(section < last)
        def _():
            lat_copy(i).wait_send()

        return carry

    def backward_chunk(i, carry):
        at = chunk_at(i)
        here = pl.ds(at, CHUNK)

        @pl.when(section < last)
        def _():
            back_copy(i).wait_recv()

        out_grad = cot[here, :].astype(F32) + arrived[here, :].astype(F32)
        fresh = new_lat[here, :]
        normal = dyn_n[here, :].astype(F32)
        norm_grad = fresh * (out_grad - split_dot(out_grad * fresh, diag[...]))
        by_n = norm_grad * normal
        gain = g_dyn[...].astype(F32)
        dm = norm_grad * gain
        mean_dm = jnp.mean(dm, -1, keepdims=True)
        mean_by_n = jnp.mean(by_n * gain, -1, keepdims=True)
        low = ((dm - mean_dm - normal * mean_by_n) * scales[here, 2:3]).astype(B16)
        arrived[here, :] = low
        dyn_sums[0:8, :] += eight_rows(low.astype(F32))
        dyn_sums[8:16, :] += eight_rows(by_n)
        dyn_sums[16:24, :] += eight_rows(norm_grad)
        pre[0:CHUNK, :] = dot(low, wd[...], NT)
        layer_backward(pre, CHUNK, n2_0, d2_0, scales, 1, at, spg_0, at, sums.at[1], 16)
        pre[0:CHUNK, :] = dot(spg_0[here, :], wm0[...], NT)
        layer_backward(pre, CHUNK, n1_0, d1_0, scales, 0, at, fpg_0, at, sums.at[1], 0)
        back_in = dot(fpg_0[here, :], wi0[0:in_width, :], NT)
        pg_copy(i).wait_recv()
        total = back_in[:, 0:lat] + ig[here, 0:lat] + pair_grad[here, :].astype(F32)
        lat_low[here, :] = total.astype(B16)

        @pl.when(section > 0)
        def _():
            back_copy(i).start()

        ig[here, 0:lat] = total
        grad_store(i).start()
        stat[8:16, :] += eight_rows(m[here, 1:2] * (total * total))
        ig[here, lat:in_width] += back_in[:, lat:in_width]
        return carry

    half_rows = small.shape[0] // 2
    my_rows = pl.ds(pl.multiple_of(core * half_rows, half_rows), half_rows)

    def to_mate(src, dst, k):
        return remote(src, dst, sm_s.at[k], sm_r.at[k], (section, mate))

    def small_to_mate():
        return to_mate(small, small_mate, 0)

    def small_to_chip(other):
        to = lax.rem(chip + other, CHIPS)
        return remote(
            small.at[my_rows], small_chips.at[chip], ch_s.at[other], ch_r.at[chip], (section, base + 2 * to + core)
        )

    def small_from_chip(other):
        to = lax.rem(chip + other, CHIPS)
        return remote(
            small.at[my_rows], small_chips.at[to], ch_s.at[other], ch_r.at[to], (section, base + 2 * to + core)
        )

    def small_to_section(other):
        to = lax.rem(section + other, steps)
        return remote(small_half, small_steps.at[section], tb_s.at[other], tb_r.at[section], (to, d))

    def small_from_section(other):
        source = lax.rem(section + other, steps)
        return remote(small_half, small_steps.at[source], tb_s.at[other], tb_r.at[source], (source, d))

    def small_back():
        return to_mate(small_done.at[my_rows], small_done.at[my_rows], 1)

    def small_over_chips():
        small_to_mate().wait_recv()
        small_to_mate().wait_send()
        small[...] += small_mate[...]
        small_chips[chip] = small[my_rows, :]
        for other in range(1, CHIPS):
            small_to_chip(other).start()

    def small_over_sections():
        for other in range(1, CHIPS):
            small_from_chip(other).wait_recv()
        total = small_chips[0]
        for source in range(1, CHIPS):
            total = total + small_chips[source]
        small_half[...] = total
        small_steps[section] = total
        for other in range(1, steps):
            small_to_section(other).start()

    def small_last():
        for other in range(1, steps):
            small_from_section(other).wait_recv()
        whole = small_steps[0]
        for source in range(1, steps):
            whole = whole + small_steps[source]
        row = lax.broadcasted_iota(jnp.int32, whole.shape, 0) + core * half_rows
        small_done[my_rows, :] = jnp.where(row < tasks, whole, small_half[...])
        small_back().start()
        for other in range(1, CHIPS):
            small_to_chip(other).wait_send()
        for other in range(1, steps):
            small_to_section(other).wait_send()
        small_back().wait_recv()
        small_back().wait_send()

    def send_small():
        table_part = jnp.zeros((tasks, side_width), F32)
        for lo in (0, rows):
            table_part += split_dot_right(one_hot(lo, rows), ig[lo : lo + rows, lat:in_width], TN)
        small[0:tasks, 0:emb] = table_part[:, side_width - emb :]
        for t in range(3):
            line = jnp.sum(dyn_sums[8 * t : 8 * t + 8, :], 0, keepdims=True)
            for part in range(lat // LANES):
                row = tasks + t * (lat // LANES) + part
                small[row : row + 1, :] = line[:, part * LANES : (part + 1) * LANES]
        q_lines = [jnp.sum(q_sums[job], 0, keepdims=True) for job in range(3)]
        for h in range(heads):
            line = jnp.zeros((1, LANES), F32)
            for job in range(3):
                line += jnp.where(first_head + job == h + 1, q_lines[job], 0.0)
            row = tasks + 3 * (lat // LANES) + h
            small[row : row + 1, :] = line
        row = tasks + 3 * (lat // LANES) + heads
        lane = lax.broadcasted_iota(jnp.int32, (1, LANES), 1)
        count = jnp.sum(m[0:rows, 1:2], 0, keepdims=True)
        lat_square = jnp.sum(jnp.sum(stat[0:8, :], 0, keepdims=True), 1, keepdims=True)
        grad_square = jnp.sum(jnp.sum(stat[8:16, :], 0, keepdims=True), 1, keepdims=True)
        small[row : row + 1, :] = jnp.where(
            lane == 0, count, jnp.where(lane == 1, lat_square, jnp.where(lane == 2, grad_square, 0.0))
        )
        small_to_mate().start()

    def turns(turn, carry):
        @pl.when(turn < jobs)
        def _():
            q_job(turn)

        @pl.when(turn == jobs)
        def _():
            load_cot.wait()
            lax.fori_loop(0, chunks, lat_sent, 0)
            lax.fori_loop(0, chunks, backward_chunk, 0)
            send_small()

        @pl.when((turn < jobs - 1) | ((turn == jobs - 1) & (section < last)) | ((turn == jobs) & (section == last)))
        def _():
            weight_grads(jnp.minimum(turn, jobs - 1), True)

        return carry

    lax.fori_loop(0, jobs + 1, turns, 0)

    @pl.when(chip > 0)
    def _():
        pl.semaphore_signal(up_ok, inc=1, device_id=at_chip(jnp.maximum(chip - 1, 0)), device_id_type=MESH)

    @pl.when(chip < CHIPS - 1)
    def _():
        pl.semaphore_signal(
            dn_ok, inc=1, device_id=at_chip(jnp.minimum(chip + 1, CHIPS - 1)), device_id_type=MESH
        )

    @pl.when(chip < CHIPS - 1)
    def _():
        pl.semaphore_wait(up_ok, 1)

    @pl.when(chip > 0)
    def _():
        pl.semaphore_wait(dn_ok, 1)

    weight_grads(jnp.int32(3), False)

    def hops(turn, carry):
        @pl.when(((turn == 0) == lower) & ~edge)
        def _():
            for t in range(CHIPS - 1, 1, -1):
                @pl.when(t > chip)
                def _():
                    for p in range(3):
                        up_copy(t, p).wait_recv()
                        add_piece(up_piece, t, p)
                        up_copy(t, p).start()

        @pl.when(((turn == 0) != lower) & ~edge)
        def _():
            for t in range(CHIPS - 2):
                @pl.when(t < chip)
                def _():
                    for p in range(3):
                        down_copy(t, p).wait_recv()
                        add_piece(down_piece, t, p)
                        down_copy(t, p).start()

        @pl.when(turn == 0)
        def _():
            small_over_sections()

        return carry

    lax.fori_loop(0, 2, hops, 0)

    for copy in side_copies:
        copy.wait_send()

    def sends(i, carry):
        pair_copy(i).wait_send()
        pg_copy(i).wait_send()
        grad_store(i).wait()

        @pl.when(section > 0)
        def _():
            back_copy(i).wait_send()

        return carry

    lax.fori_loop(0, chunks, sends, 0)

    def job_done(job, carry):
        def body(other, carry):
            owner_copy(job, lax.rem(chip + other, CHIPS)).wait_send()
            return carry

        lax.fori_loop(1, CHIPS, body, 0)
        keep_copy(job).wait()
        return carry

    lax.fori_loop(0, jobs, job_done, 0)
    for head in range(heads):
        for half in range(2):
            source = (0, CHIPS - 1)[half] if head < 2 else (1, CHIPS - 2)[half]

            @pl.when(chip != source)
            def _():
                remote(
                    half_q.at[0, 0], recv_q.at[head, half], rb_s.at[0, 0], rb_r.at[head, half], at_chip(source)
                ).wait_recv()

    @pl.when(chip > 0)
    def _():
        for p in range(3):
            up_copy(chip, p).wait_recv()
            add_piece(up_piece, chip, p)

    @pl.when(chip < CHIPS - 1)
    def _():
        for p in range(3):
            down_copy(chip, p).wait_recv()
            add_piece(down_piece, chip, p)

    keep_0 = pltpu.make_async_copy(half_0.at[chip], recv_0, own_s.at[3])
    keep_0.start()
    for t in range(CHIPS):
        @pl.when(t > chip)
        def _():
            for p in range(3):
                up_copy(t, p).wait_send()

        @pl.when(t < chip)
        def _():
            for p in range(3):
                down_copy(t, p).wait_send()

    small_last()
    done = pltpu.make_async_copy(small_done, small_out, out_sem.at[2 * chunks])
    done.start()
    done.wait()
    keep_0.wait()


def finish_kernel(dims, *refs):
    lat, in_width, hid, heads, bins, tasks, emb = dims
    at_mid = in_width + VECS
    at_out = at_mid + hid
    recv_q, recv_0, small_in, lat_in, grad_in = refs[:5]
    lat_out, grad_out, w_in, w_mid, w_dyn, w_q, b_dyn, g_dyn, s_dyn, b_q, table, rms = refs[5:17]
    vecs = refs[17:23]
    part_q, part_0, small, sum_in, sum_mid, lat_held, grad_held, in_sem, out_sem = refs[23:]
    loads = [pltpu.make_async_copy(recv_0, part_0, in_sem.at[0])]
    loads += [pltpu.make_async_copy(recv_q.at[h], part_q.at[h], in_sem.at[1 + h]) for h in range(heads)]
    load_small = pltpu.make_async_copy(small_in, small, in_sem.at[1 + heads])
    through = [
        pltpu.make_async_copy(lat_in, lat_held, in_sem.at[2 + heads]),
        pltpu.make_async_copy(grad_in, grad_held, in_sem.at[3 + heads]),
    ]
    copies = [
        pltpu.make_async_copy(lat_held, lat_out, out_sem.at[0]),
        pltpu.make_async_copy(grad_held, grad_out, out_sem.at[1]),
    ]
    for copy in through + loads + [load_small]:
        copy.start()

    def total(h, lo, hi):
        if h == 0:
            return part_0[lo:hi, :].astype(F32)
        return part_q[h - 1, 0, lo:hi, :].astype(F32) + part_q[h - 1, 1, lo:hi, :].astype(F32)

    for arriving, leaving in zip(through, copies):
        arriving.wait()
        leaving.start()
    for h in range(heads + 1):
        loads[h].wait()
        sum_in[h] = total(h, 0, in_width)
        sum_mid[h] = total(h, at_mid, at_out)
        copies.append(pltpu.make_async_copy(sum_in.at[h], w_in.at[h], out_sem.at[2 + 2 * h]))
        copies.append(pltpu.make_async_copy(sum_mid.at[h], w_mid.at[h], out_sem.at[3 + 2 * h]))
        for copy in copies[-2:]:
            copy.start()
        lines = total(h, in_width, at_mid)
        for t in range(6):
            vecs[t][h] = lines[t : t + 1, :]
        if h:
            w_q[h - 1] = total(h, at_out, at_out + padded(bins))[0:bins, :].reshape(bins, 1, LANES)
    for t in range(lat // LANES):
        w_dyn[:, t * LANES : (t + 1) * LANES] = total(0, at_out + t * LANES, at_out + (t + 1) * LANES)
    load_small.wait()
    table[...] = small[0:tasks, 0:emb]
    for t, out in enumerate((b_dyn, g_dyn, s_dyn)):
        for part in range(lat // LANES):
            row = tasks + t * (lat // LANES) + part
            out[0:1, part * LANES : (part + 1) * LANES] = small[row : row + 1, :]
    at_q = tasks + 3 * (lat // LANES)
    for h in range(heads):
        b_q[h] = small[at_q + h : at_q + h + 1, 0:bins]
    stat = small[at_q + heads : at_q + heads + 1, :]
    count = stat[:, 0:1]
    squares = jnp.concatenate([stat[:, 1:2] / count, stat[:, 2:3] / (count * lat)], 1)
    rms[...] = jnp.sqrt(squares)
    for copy in copies:
        copy.wait()


def on_device(
    latent_in, actions, task_ids, valid, action_mask, bins, fraction, latent_cot,
    w_in, b_in, g_in, beta_in, w_mid, b_mid, g_mid, beta_mid,
    w_dyn_out, b_dyn_out, g_dyn_out, beta_dyn_out, w_q_out, b_q_out, table,
):
    steps = lax.axis_size("section")
    spread = lax.axis_size("dp")
    groups = spread // PEERS
    rows, lat = latent_in.shape
    act_width = actions.shape[2]
    in_width, hid = w_in.shape[2:]
    heads = w_q_out.shape[1]
    bin_count = w_q_out.shape[-1]
    tasks, emb = table.shape
    block = in_width + VECS + hid + padded(bin_count)
    block0 = in_width + VECS + hid + lat
    chunks = rows // CHUNK
    small_rows = padded(tasks + 3 * (lat // LANES) + heads + 1)
    dims = (rows, lat, act_width, in_width, hid, heads, bin_count, tasks, emb, steps)
    anywhere = pl.BlockSpec(memory_space=pl.ANY)
    vmem = pl.BlockSpec(memory_space=pltpu.VMEM)
    hbm = pl.BlockSpec(memory_space=pltpu.HBM)
    dma = pltpu.SemaphoreType.DMA
    both = 2 * rows
    wide = pltpu.VMEM((rows, hid), B16)
    thin = pltpu.VMEM((rows, LANES), F32)
    low = pltpu.VMEM((rows, lat), B16)
    part_low = pltpu.VMEM((QROWS, hid), B16)
    q_wide = pltpu.VMEM((both, hid), B16)
    lat_out, grad_out, recv_q, recv_0, small = pl.pallas_call(
        functools.partial(step_kernel, dims),
        out_shape=[
            jax.ShapeDtypeStruct((rows, lat), B16),
            jax.ShapeDtypeStruct((rows, lat), F32),
            jax.ShapeDtypeStruct((heads, 2, block, LANES), B16),
            jax.ShapeDtypeStruct((block0, LANES), B16),
            jax.ShapeDtypeStruct((small_rows, LANES), F32),
        ],
        in_specs=[anywhere] + [vmem] * 7 + [anywhere] * 5 + [vmem] * 10,
        out_specs=[anywhere] * 5,
        scratch_shapes=[
            pltpu.VMEM((both, 6 * LANES), B16),
            pltpu.VMEM((both, LANES), F32),
            pltpu.VMEM((2, in_width + VECS, hid), B16),
            pltpu.VMEM((2, hid, hid), B16),
            pltpu.VMEM((2, LANES, hid), B16),
            pltpu.VMEM((2, bin_count, hid), B16),
            pltpu.VMEM((in_width + VECS, hid), B16),
            pltpu.VMEM((hid, hid), B16),
            pltpu.VMEM((hid, lat), B16),
            pltpu.VMEM((6, 8, hid), F32),
            pltpu.VMEM((8, LANES), F32),
            pltpu.VMEM((lat, lat), B16),
            pltpu.VMEM((2, 8, rows), F32),
            pltpu.VMEM((2, act_width, rows), B16),
            pltpu.VMEM((VECS, hid), F32),
            pltpu.VMEM((both, in_width), F32),
            q_wide, q_wide, q_wide, q_wide,
            pltpu.VMEM((both, LANES), B16),
            part_low, part_low, part_low, part_low,
            pltpu.VMEM((QROWS, LANES), F32),
            pltpu.VMEM((QROWS, hid), F32),
            wide, wide, wide, wide, wide, wide, wide, wide, thin,
            low,
            pltpu.VMEM((rows, lat), F32),
            low, low, low, low, low,
            pltpu.VMEM((2, CHIPS, block0, LANES), B16),
            pltpu.VMEM((3, CHIPS, block, LANES), B16),
            pltpu.VMEM((CHIPS, block0, LANES), B16),
            pltpu.VMEM((2, 32, hid), F32),
            pltpu.VMEM((3, 8, LANES), F32),
            pltpu.VMEM((24, lat), F32),
            pltpu.VMEM((16, lat), F32),
            pltpu.VMEM((small_rows, LANES), F32),
            pltpu.VMEM((small_rows, LANES), F32),
            pltpu.VMEM((CHIPS, small_rows // 2, LANES), F32),
            pltpu.VMEM((small_rows // 2, LANES), F32),
            pltpu.VMEM((steps, small_rows // 2, LANES), F32),
            pltpu.VMEM((small_rows, LANES), F32),
            dma((10,)), dma((chunks,)), dma((2 * chunks + 1,)),
            dma((chunks,)), dma((chunks,)), dma((chunks,)), dma((chunks,)),
            dma((2,)), dma((2,)), dma((chunks,)), dma((chunks,)), dma((chunks,)), dma((chunks,)),
            dma((4, CHIPS)), dma((4, CHIPS)), dma((4,)), dma((3, CHIPS)), dma((heads, 2)),
            dma((2,)), dma((2,)), dma((CHIPS,)), dma((CHIPS,)), dma((steps,)), dma((steps,)),
            dma((CHIPS, 3)), dma((CHIPS, 3)), dma((CHIPS, 3)), dma((CHIPS, 3)),
            pltpu.SemaphoreType.REGULAR, pltpu.SemaphoreType.REGULAR,
        ],
        compiler_params=pltpu.CompilerParams(
            collective_id=0, has_side_effects=True, vmem_limit_bytes=16350 * 2**12
        ),
        name="step",
    )(
        latent_in, actions[0].T, task_ids[None], valid[None], bins, fraction,
        action_mask.T, table, latent_cot[0],
        w_in[0], w_mid[0], w_dyn_out[0], w_q_out[0].transpose(0, 2, 1),
        b_in[0], g_in[0], beta_in[0], b_mid[0], g_mid[0], beta_mid[0],
        b_dyn_out, g_dyn_out, beta_dyn_out, b_q_out[0],
    )
    across = [[q * PEERS + r for q in range(groups)] for r in range(PEERS)]
    if groups > 1:
        small = lax.psum(small, "dp", axis_index_groups=across)

    def shape(*dims):
        return jax.ShapeDtypeStruct(dims, F32)

    lat_out, grad_out, part_in, part_mid, part_dyn, part_q, b_dyn, g_dyn, s_dyn, q_bias, grad_table, rms, *vecs = (
        pl.pallas_call(
            functools.partial(finish_kernel, (lat, in_width, hid, heads, bin_count, tasks, emb)),
            out_shape=[
                jax.ShapeDtypeStruct((rows, lat), B16),
                shape(rows, lat),
                shape(heads + 1, in_width, LANES),
                shape(heads + 1, hid, LANES),
                shape(LANES, lat),
                shape(heads, bin_count, 1, LANES),
                shape(1, lat), shape(1, lat), shape(1, lat),
                shape(heads, 1, bin_count),
                shape(tasks, emb),
                shape(1, 2),
            ] + [shape(heads + 1, 1, LANES)] * 6,
            in_specs=[hbm] * 5,
            out_specs=[hbm] * 4 + [vmem] * 14,
            scratch_shapes=[
                pltpu.VMEM((heads, 2, block, LANES), B16),
                pltpu.VMEM((block0, LANES), B16),
                pltpu.VMEM((small_rows, LANES), F32),
                pltpu.VMEM((heads + 1, in_width, LANES), F32),
                pltpu.VMEM((heads + 1, hid, LANES), F32),
                pltpu.VMEM((rows, lat), B16),
                pltpu.VMEM((rows, lat), F32),
                dma((heads + 4,)),
                dma((2 * heads + 4,)),
            ],
            compiler_params=pltpu.CompilerParams(vmem_limit_bytes=60 * 2**20),
            name="finish",
        )(recv_q, recv_0, small, lat_out, grad_out)
    )

    def owned(piece, dim):
        if groups == 1:
            return piece
        piece = lax.psum_scatter(piece, "dp", scatter_dimension=dim, axis_index_groups=across, tiled=True)
        moves = [(q * PEERS + r, r * groups + q) for q in range(groups) for r in range(PEERS)]
        return lax.ppermute(piece, "dp", moves)

    part_in, part_mid, part_q = owned(part_in, 2), owned(part_mid, 2), owned(part_q, 3)
    part_dyn = owned(part_dyn, 0)
    vecs = [owned(v, 2).transpose(1, 0, 2) for v in vecs]
    return (
        lat_out[None],
        grad_out[None],
        part_in[None],
        *vecs[:3],
        part_mid[None],
        *vecs[3:],
        part_dyn[None],
        b_dyn,
        g_dyn,
        s_dyn,
        part_q.transpose(2, 0, 3, 1),
        q_bias.transpose(1, 0, 2),
        grad_table,
        rms,
    )


def solution(mesh):
    placed = (
        P("dp", None),
        P("section", "dp", None),
        P("dp"),
        P("dp"),
        P(),
        P("section", "dp"),
        P("section", "dp"),
        P("section", "dp", None),
        P("section", None, None, None),
        P("section", None, None),
        P("section", None, None),
        P("section", None, None),
        P("section", None, None, None),
        P("section", None, None),
        P("section", None, None),
        P("section", None, None),
        P("section", None, None),
        P("section", None),
        P("section", None),
        P("section", None),
        P("section", None, None, None),
        P("section", None, None),
        P(),
    )
    return jax.shard_map(
        on_device,
        mesh=mesh,
        in_specs=placed,
        out_specs=(
            P("section", "dp", None),
            P("section", "dp", None),
            P("section", None, None, "dp"),
            P("section", None, "dp"),
            P("section", None, "dp"),
            P("section", None, "dp"),
            P("section", None, None, "dp"),
            P("section", None, "dp"),
            P("section", None, "dp"),
            P("section", None, "dp"),
            P("section", "dp", None),
            P("section", None),
            P("section", None),
            P("section", None),
            P("section", None, "dp", None),
            P("section", None, None),
            P(),
            P("section", None),
        ),
        check_vma=False,
    )
```

```python
import functools

import jax
import jax.numpy as jnp
from jax import lax
from jax.experimental import pallas as pl
from jax.experimental.pallas import tpu as pltpu
from jax.sharding import PartitionSpec as P

GROUP = 8
EPS = 1e-05
F32 = jnp.float32
B16 = jnp.bfloat16
MESH = pl.DeviceIdType.MESH

LANES = 128
CHIPS = 4
PEERS = 2 * CHIPS
CHUNK = 128
QROWS = 256
SUB = 256
VECS = 16

NN = (((1,), (0,)), ((), ()))
NT = (((1,), (1,)), ((), ()))
TN = (((0,), (0,)), ((), ()))


def dot(a, b, dims=NN):
    return lax.dot_general(a, b, dims, preferred_element_type=F32)


def split_dot(a, b, dims=NN):
    high = a.astype(B16)
    low = (a - high.astype(F32)).astype(B16)
    return dot(high, b, dims) + dot(low, b, dims)


def split_dot_right(a, b, dims):
    high = b.astype(B16)
    low = (b - high.astype(F32)).astype(B16)
    return dot(a, high, dims) + dot(a, low, dims)


def norm_mish(x, gain, shift):
    center = x - jnp.mean(x, -1, keepdims=True)
    spread = jnp.mean(center * center, -1, keepdims=True)
    scale = lax.rsqrt(spread + EPS)
    n = center * scale
    u = n * gain + shift
    w = jnp.exp(jnp.minimum(u, 30.0))
    top = w * (w + 2.0)
    over = pltpu.reciprocal(top + 2.0, approx=True)
    act = u * (top * over)
    slope = (top + 4.0 * (u * (top - w)) * over) * (over * gain)
    return act, n, slope, scale


def padded(count):
    return (count + 15) // 16 * 16


def tiles(size, step=256):
    return [(lo, min(lo + step, size)) for lo in range(0, size, step)]


def eight_rows(x):
    return x.reshape(x.shape[0] // 8, 8, x.shape[1]).sum(0)


def each_sub(count, body):
    sub = min(SUB, count)
    for j in range(0, count, sub):
        body(j, sub)


def layer_forward(pre, count, bias, gain, shift, act_ref, act_at, n_ref, slope_ref, scale_ref, lane, at):
    def body(j, sub):
        x = pre[pl.ds(j, sub), :]
        if bias is not None:
            x = x + bias
        act, n, slope, scale = norm_mish(x, gain, shift)
        act_ref[pl.ds(act_at + j, sub), :] = act.astype(B16)
        here = pl.ds(at + j, sub)
        n_ref[here, :] = n.astype(n_ref.dtype)
        slope_ref[here, :] = slope.astype(slope_ref.dtype)
        scale_ref[here, lane : lane + 1] = scale

    each_sub(count, body)


def layer_backward(pre, count, n_ref, slope_ref, scale_ref, lane, at, out_ref, out_at, sums, first):
    def body(j, sub):
        here = pl.ds(at + j, sub)
        n = n_ref[here, :].astype(F32)
        dn = pre[pl.ds(j, sub), :] * slope_ref[here, :].astype(F32)
        by_n = dn * n
        mean_dn = jnp.mean(dn, -1, keepdims=True)
        mean_by_n = jnp.mean(by_n, -1, keepdims=True)
        out = (dn - mean_dn - n * mean_by_n) * scale_ref[here, lane : lane + 1]
        out_ref[pl.ds(out_at + j, sub), :] = out.astype(B16)
        sums[first : first + 8, :] += eight_rows(by_n)
        sums[first + 8 : first + 16, :] += eight_rows(dn)

    each_sub(count, body)


def step_kernel(dims, *refs):
    rows, lat, act_width, in_width, hid, heads, bins, tasks, emb, steps = dims
    side_width = in_width - lat
    at_mid = in_width + VECS
    at_out = at_mid + hid
    block = at_out + padded(bins)
    block0 = at_out + lat
    both = 2 * rows
    ones_at = in_width // LANES * LANES
    pieces = ((0, at_mid), (at_mid, at_out), (at_out, block0))
    (
        lat_in, acts, task, valid, bin_at, part_of, amask, table, cot_in, w_in, w_mid, w_dyn, w_q,
        b_in, g_in, s_in, b_mid, g_mid, s_mid, b_dyn, g_dyn, s_dyn, b_q,
        lat_out, grad_out, recv_q, recv_0, small_out,
        x, m, wi, wm, wq, wq_raw, wi0, wm0, wd, vec, bq, diag,
        lines, acting, vec_lines, ig, act1, act2, spg, fpg, qg, n1, d1, n2, d2, q_scales, pre,
        act1_0, act2_0, spg_0, fpg_0, n1_0, d1_0, n2_0, d2_0, scales,
        dyn_n, new_lat, lat_low, cot, arrived, pair_grad, pair_send,
        gb, half_q, half_0, sums, q_sums, dyn_sums, stat, small, small_mate, small_chips, small_half, small_steps, small_done,
        w_sem, in_sem, out_sem, lat_s, lat_r, px_s, px_r, side_s, side_r, pg_s, pg_r, gr_s, gr_r,
        half_s, half_r, own_s, rb_s, rb_r, sm_s, sm_r, ch_s, ch_r, tb_s, tb_r, up_s, up_r, dn_s, dn_r, up_ok, dn_ok,
    ) = refs
    section = lax.axis_index("section")
    d = lax.axis_index("dp")
    place = lax.rem(d, PEERS)
    base = d - place
    chip = place // 2
    core = lax.rem(place, 2)
    edge = (chip == 0) | (chip == CHIPS - 1)
    lower = chip < CHIPS // 2
    side_of = chip // 2
    last = steps - 1
    mate = base + chip * 2 + (1 - core)
    pair = base + (chip + 1 - 2 * lax.rem(chip, 2)) * 2 + core
    following = jnp.minimum(section + 1, last)
    before = jnp.maximum(section - 1, 0)
    chunks = rows // CHUNK
    jobs = jnp.where(edge, 2, 3)
    first_head = jnp.where(edge, 1, 3)

    def remote(src, dst, send, recv, to):
        return pltpu.make_async_remote_copy(
            src_ref=src, dst_ref=dst, send_sem=send, recv_sem=recv, device_id=to, device_id_type=MESH
        )

    def chunk_at(i):
        return pl.multiple_of(i * CHUNK, CHUNK)

    loads = [
        pltpu.make_async_copy(w_in.at[0], wi0.at[0:in_width], w_sem.at[0]),
        pltpu.make_async_copy(w_mid.at[0], wm0, w_sem.at[1]),
        pltpu.make_async_copy(w_dyn, wd, w_sem.at[2]),
    ]

    def job_loads(job):
        slot = lax.rem(job, 2)
        h = first_head + job
        return [
            pltpu.make_async_copy(w_in.at[h], wi.at[slot, 0:in_width], w_sem.at[3 + 3 * slot]),
            pltpu.make_async_copy(w_mid.at[h], wm.at[slot], w_sem.at[4 + 3 * slot]),
            pltpu.make_async_copy(w_q.at[h - 1], wq_raw.at[slot], w_sem.at[5 + 3 * slot]),
        ]

    load_cot = pltpu.make_async_copy(cot_in, cot, w_sem.at[9])

    def load_lat(i):
        here = pl.ds(chunk_at(i), CHUNK)
        return pltpu.make_async_copy(lat_in.at[here], x.at[here, 0:lat], in_sem.at[i])

    barrier = pltpu.get_barrier_semaphore()
    for other in range(1, PEERS):
        to = base + lax.rem(place + other, PEERS)
        pl.semaphore_signal(barrier, inc=1, device_id=(section, to), device_id_type=MESH)
    for other in range(1, steps):
        to = lax.rem(section + other, steps)
        pl.semaphore_signal(barrier, inc=1, device_id=(to, d), device_id_type=MESH)

    loads[0].start()

    @pl.when(section == 0)
    def _():
        for i in range(chunks):
            load_lat(i).start()

    for copy in loads[1:] + job_loads(jnp.int32(0)) + job_loads(jnp.int32(1)):
        copy.start()
    load_cot.start()

    head_lines = [task[...].astype(F32), valid[...].astype(F32), bin_at[...].astype(F32), part_of[...]]
    lines[0] = jnp.concatenate(head_lines + [jnp.zeros((4, rows), F32)], 0)
    acting[0] = acts[...]

    def one_hot(lo, count):
        task_lane = lax.broadcasted_iota(jnp.int32, (count, tasks), 1).astype(F32)
        return (m[lo : lo + count, 0:1] == task_lane).astype(F32).astype(B16)

    def prepare(which):
        lo = which * rows
        m[lo : lo + rows, 0:8] = lines[which].T
        hot = one_hot(lo, rows)
        mask = dot(amask[...].astype(F32).astype(B16), hot, NT)
        used = (acting[which].astype(F32) * mask).T
        x[lo : lo + rows, lat:in_width] = jnp.concatenate(
            [used.astype(B16), dot(hot, table[...]).astype(B16)], 1
        )

    lane = lax.broadcasted_iota(jnp.int32, (both, LANES), 1)
    x[:, ones_at : ones_at + LANES] = (lane == in_width - ones_at).astype(F32).astype(B16)
    prepare(0)
    for t, source in enumerate((b_in, g_in, s_in, b_mid, g_mid, s_mid)):
        vec[t, 0 : heads + 1, :] = source[...].astype(F32)
    shift = GROUP.bit_length() - 1
    diag[...] = (
        lax.shift_right_logical(lax.broadcasted_iota(jnp.int32, diag.shape, 0), shift)
        == lax.shift_right_logical(lax.broadcasted_iota(jnp.int32, diag.shape, 1), shift)
    ).astype(F32).astype(B16)

    def group_sums(values):
        width = diag.shape[0]
        return jnp.concatenate(
            [split_dot(values[:, lo : lo + width], diag[...]) for lo in range(0, lat, width)], 1
        )

    def bias_rows(h):
        line = lax.broadcasted_iota(jnp.int32, (VECS, hid), 0)
        return jnp.where(line == 0, vec[0, pl.ds(h, 1), :], 0.0).astype(B16)

    wi0[in_width:at_mid, :] = bias_rows(0)
    stat[...] = jnp.zeros(stat.shape, F32)

    def clear():
        bq[...] = jnp.full(bq.shape, -1e30, F32)
        bq[0:heads, 0:bins] = b_q[...].astype(F32)
        wq[...] = jnp.zeros(wq.shape, B16)
        sums[...] = jnp.zeros(sums.shape, F32)
        ig[...] = jnp.zeros(ig.shape, F32)
        q_sums[...] = jnp.zeros(q_sums.shape, F32)
        dyn_sums[...] = jnp.zeros(dyn_sums.shape, F32)
        small[...] = jnp.zeros(small.shape, F32)

    pl.semaphore_wait(barrier, PEERS - 1 + steps - 1)

    side_copies = [
        remote(lines.at[0], lines.at[1], side_s.at[0], side_r.at[0], (section, pair)),
        remote(acting.at[0], acting.at[1], side_s.at[1], side_r.at[1], (section, pair)),
    ]
    for copy in side_copies:
        copy.start()

    def settle():
        clear()
        for copy in side_copies:
            copy.wait_recv()
        prepare(1)

    @pl.when(section == last)
    def _():
        arrived[...] = jnp.zeros(arrived.shape, B16)

    @pl.when(section > 0)
    def _():
        settle()

    for copy in loads:
        copy.wait()

    def vec_of(t, h):
        return vec[t, pl.ds(h, 1), :]

    def lat_copy(i):
        here = pl.ds(chunk_at(i), CHUNK)
        return remote(
            lat_low.at[here], x.at[here, 0:lat], lat_s.at[i], lat_r.at[i], (following, d)
        )

    def pair_copy(i):
        here = chunk_at(i)
        return remote(
            x.at[pl.ds(here, CHUNK), 0:lat], x.at[pl.ds(rows + here, CHUNK), 0:lat],
            px_s.at[i], px_r.at[i], (section, pair),
        )

    def lat_store(i):
        here = pl.ds(chunk_at(i), CHUNK)
        return pltpu.make_async_copy(lat_low.at[here], lat_out.at[here], out_sem.at[i])

    def forward_chunk(i, carry):
        at = chunk_at(i)
        here = pl.ds(at, CHUNK)

        @pl.when(section > 0)
        def _():
            lat_copy(i).wait_recv()

        @pl.when(section == 0)
        def _():
            load_lat(i).wait()

        pair_copy(i).start()
        pre[0:CHUNK, :] = dot(x[here, 0:at_mid], wi0[...])
        layer_forward(
            pre, CHUNK, None, vec[1, 0:1, :], vec[2, 0:1, :], act1_0, at, n1_0, d1_0, scales, 0, at
        )
        pre[0:CHUNK, :] = dot(act1_0[here, :], wm0[...])
        layer_forward(
            pre, CHUNK, vec[3, 0:1, :], vec[4, 0:1, :], vec[5, 0:1, :], act2_0, at, n2_0, d2_0, scales, 1, at
        )
        out = dot(act2_0[here, :], wd[...]) + b_dyn[...].astype(F32)
        center = out - jnp.mean(out, -1, keepdims=True)
        scale = lax.rsqrt(jnp.mean(center * center, -1, keepdims=True) + EPS)
        normal = center * scale
        dyn_n[here, :] = normal.astype(B16)
        scales[here, 2:3] = scale
        power = jnp.exp(normal * g_dyn[...].astype(F32) + s_dyn[...].astype(F32))
        fresh = power * pltpu.reciprocal(group_sums(power), approx=True)
        new_lat[here, :] = fresh
        low = fresh.astype(B16)
        lat_low[here, :] = low

        @pl.when(section < last)
        def _():
            lat_copy(i).start()

        lat_store(i).start()
        wide = low.astype(F32)
        stat[0:8, :] += eight_rows(m[here, 1:2] * (wide * wide))
        return carry

    lax.fori_loop(0, chunks, forward_chunk, 0)

    @pl.when(section == 0)
    def _():
        settle()

    def pg_copy(i):
        here = pl.ds(chunk_at(i), CHUNK)
        return remote(
            pair_send.at[here], pair_grad.at[here], pg_s.at[i], pg_r.at[i], (section, pair)
        )

    def q_chunk(job, at):
        here = pl.ds(at, QROWS)
        h = first_head + job
        slot = lax.rem(job, 2)
        pre[...] = dot(x[here, 0:at_mid], wi[slot])
        layer_forward(
            pre, QROWS, None, vec_of(1, h), vec_of(2, h), act1, at, n1, d1, q_scales, 0, 0
        )
        pre[...] = dot(act1[here, :], wm[slot])
        layer_forward(
            pre, QROWS, vec_of(3, h), vec_of(4, h), vec_of(5, h), act2, at, n2, d2, q_scales, 1, 0
        )
        logits = dot(act2[here, :], wq[slot], NT) + bq[pl.ds(h - 1, 1), :]
        power = jnp.exp(logits - jnp.max(logits, -1, keepdims=True))
        chance = power / jnp.sum(power, -1, keepdims=True)
        lane = lax.broadcasted_iota(jnp.int32, (QROWS, LANES), 1).astype(F32)
        low_bin = m[here, 2:3]
        part = m[here, 3:4]
        target = jnp.where(lane == low_bin, 1.0 - part, 0.0) + jnp.where(lane == low_bin + 1.0, part, 0.0)
        grad = (m[here, 1:2] * (chance - target)).astype(B16)
        qg[here, :] = grad
        q_sums[job] += eight_rows(grad.astype(F32))
        pre[...] = dot(grad, wq[slot])
        layer_backward(pre, QROWS, n2, d2, q_scales, 1, 0, spg, at, sums.at[0], 16)
        pre[...] = dot(spg[here, :], wm[slot], NT)
        layer_backward(pre, QROWS, n1, d1, q_scales, 0, 0, fpg, at, sums.at[0], 0)
        for lo, hi in tiles(in_width):
            ig[here, lo:hi] += dot(fpg[here, :], wi[slot, lo:hi, :], NT)

    q_chunks = both // QROWS
    own_chunks = rows // QROWS

    def q_job(job):
        for copy in job_loads(job):
            copy.wait()
        slot = lax.rem(job, 2)
        wq[slot, 0:bins, :] = wq_raw[slot]
        wi[slot, in_width:at_mid, :] = bias_rows(first_head + job)
        sums[0] = jnp.zeros(sums.shape[1:], F32)

        def body(i, carry):
            which = lax.rem(i + jnp.where(job == 0, 0, own_chunks), q_chunks)
            at = pl.multiple_of(which * QROWS, QROWS)

            @pl.when((job == 0) & (which == own_chunks))
            def _():
                def pair_here(j, carry):
                    pair_copy(j).wait_recv()
                    return carry

                lax.fori_loop(0, chunks, pair_here, 0)

            q_chunk(job, at)

            @pl.when((job == jobs - 1) & (which >= own_chunks))
            def _():
                for k in range(QROWS // CHUNK):
                    j = (which - own_chunks) * (QROWS // CHUNK) + k
                    to = chunk_at(j)
                    pair_send[pl.ds(to, CHUNK), :] = ig[pl.ds(rows + to, CHUNK), 0:lat].astype(B16)
                    pg_copy(j).start()

            return carry

        lax.fori_loop(0, q_chunks, body, 0)

        @pl.when(job + 2 < jobs)
        def _():
            for copy in job_loads(job + 2):
                copy.start()

    def half_copy(job, z, q):
        if q:
            src, dst = gb.at[1 - core, z, 0:block], half_q.at[job, z]
        else:
            src, dst = gb.at[1 - core, z], half_0.at[z]
        return remote(src, dst, half_s.at[job, z], half_r.at[job, z], (section, mate))

    def owner_copy(job, z):
        head = first_head + job - 1
        return remote(
            half_q.at[job, z], recv_q.at[head, side_of], rb_s.at[job, z], rb_r.at[head, side_of],
            (section, base + 2 * z + core),
        )

    def keep_copy(job):
        return pltpu.make_async_copy(
            half_q.at[job, chip], recv_q.at[first_head + job - 1, side_of], own_s.at[job]
        )

    def add_rows(dst, src, size):
        step = size // 4 // 16 * 16
        for part in range(4):
            span = slice(part * step, size if part == 3 else (part + 1) * step)
            dst[span, :] = (dst[span, :].astype(F32) + src[span, :].astype(F32)).astype(B16)

    def at_chip(z):
        return (section, base + 2 * z + core)

    def stripe(z):
        return pl.ds(pl.multiple_of(z * LANES, LANES), LANES)

    def up_piece(z, p):
        size = pieces[p][1] - pieces[p][0]
        return (act1.at[0:size, stripe(z)], act1.at[0:size, stripe(CHIPS + z)], act2.at[0:size, stripe(z)])[p]

    def down_piece(z, p):
        size = pieces[p][1] - pieces[p][0]
        return (spg.at[0:size, stripe(z)], spg.at[0:size, stripe(CHIPS + z)], act2.at[0:size, stripe(CHIPS + z)])[p]

    def up_copy(z, p):
        return remote(
            half_0.at[z, pieces[p][0] : pieces[p][1]], up_piece(z, p), up_s.at[z, p], up_r.at[z, p],
            at_chip(jnp.minimum(chip + 1, CHIPS - 1)),
        )

    def down_copy(z, p):
        return remote(
            half_0.at[z, pieces[p][0] : pieces[p][1]], down_piece(z, p), dn_s.at[z, p], dn_r.at[z, p],
            at_chip(jnp.maximum(chip - 1, 0)),
        )

    def add_piece(piece, z, p):
        lo, hi = pieces[p]
        half_0[z, lo:hi, :] = (half_0[z, lo:hi, :].astype(F32) + piece(z, p)[...].astype(F32)).astype(B16)

    def weight_grads(job, q):
        if q:
            count, a1, a2, sp, fp, own_sums = both, act1, act2, spg, fpg, 0
        else:
            count, a1, a2, sp, fp, own_sums = rows, act1_0, act2_0, spg_0, fpg_0, 1
        size = block if q else block0
        h = first_head + job if q else 0
        line_at = lax.broadcasted_iota(jnp.int32, (VECS, hid), 0)
        vectors = jnp.zeros((VECS, hid), F32)
        for t, (first, gain) in enumerate(((0, 1), (8, 1), (None, None), (16, 4), (24, 4))):
            if gain is not None:
                line = jnp.sum(sums[own_sums, first : first + 8, :], 0, keepdims=True) / vec_of(gain, h)
                vectors = jnp.where(line_at == t + 1, line, vectors)
        vec_lines[...] = vectors
        row_at = lax.broadcasted_iota(jnp.int32, (VECS, 2 * LANES), 0)

        def order(i):
            far_first = jnp.where(lower, CHIPS - 1 - i, i)
            pair_first = lax.rem(jnp.where(lower, CHIPS - i, i + CHIPS - 1), CHIPS)
            return jnp.where(edge, far_first, pair_first)

        def make(z):
            cols = pl.ds(pl.multiple_of(z * 2 * LANES, 2 * LANES), 2 * LANES)
            for left, right, first, size_of in ((x, fp, 0, at_mid), (a1, sp, at_mid, hid)):
                for lo, hi in tiles(size_of):
                    grad = dot(left[0:count, lo:hi], right[0:count, cols], TN)
                    if left is x and hi == at_mid:
                        plain = grad[0 : in_width - lo]
                        bias_mid = dot(x[0:count, ones_at : ones_at + LANES], sp[0:count, cols], TN)
                        bias_mid = bias_mid[in_width - ones_at : in_width - ones_at + 1]
                        lines_here = grad[in_width - lo :] + vec_lines[:, cols]
                        grad = jnp.concatenate([plain, jnp.where(row_at == 3, bias_mid, lines_here)], 0)
                    for p in range(2):
                        gb[p, z, first + lo : first + hi, :] = grad[:, p * LANES : (p + 1) * LANES].astype(B16)
            if q:
                g_out = dot(qg[0:count, :], a2[0:count, cols], TN)
                for p in range(2):
                    gb[p, z, at_out:block, :] = g_out[0 : block - at_out, p * LANES : (p + 1) * LANES].astype(B16)
            else:
                g_out = dot(a2[0:count, cols], arrived[0:count, :], TN)
                for p in range(2):
                    for t in range(lat // LANES):
                        gb[p, z, at_out + t * LANES : at_out + (t + 1) * LANES, :] = g_out[
                            p * LANES : (p + 1) * LANES, t * LANES : (t + 1) * LANES
                        ].astype(B16)
            half_copy(job, z, q).start()

        def finish(z):
            half_copy(job, z, q).wait_recv()
            if q:
                add_rows(half_q.at[job, z], gb.at[core, z], size)

                @pl.when(z != chip)
                def _():
                    owner_copy(job, z).start()

                @pl.when(z == chip)
                def _():
                    keep_copy(job).start()
            else:
                add_rows(half_0.at[z], gb.at[core, z], size)

                @pl.when((chip == 0) & (z != chip))
                def _():
                    for p in range(3):
                        up_copy(z, p).start()

                @pl.when((chip == CHIPS - 1) & (z != chip))
                def _():
                    for p in range(3):
                        down_copy(z, p).start()

        def body(i, carry):
            @pl.when(i < CHIPS)
            def _():
                make(order(i))

            if not q:
                @pl.when(i == 1)
                def _():
                    small_over_chips()

            @pl.when(i > 0)
            def _():
                finish(order(i - 1))

            return carry

        lax.fori_loop(0, CHIPS + 1, body, 0)

        def sent(z, carry):
            half_copy(job, z, q).wait_send()
            return carry

        lax.fori_loop(0, CHIPS, sent, 0)

    def back_copy(i):
        here = pl.ds(chunk_at(i), CHUNK)
        return remote(lat_low.at[here], arrived.at[here], gr_s.at[i], gr_r.at[i], (before, d))

    def grad_store(i):
        here = pl.ds(chunk_at(i), CHUNK)
        return pltpu.make_async_copy(ig.at[here, 0:lat], grad_out.at[here], out_sem.at[chunks + i])

    def lat_sent(i, carry):
        lat_store(i).wait()

        @pl.when(section < last)
        def _():
            lat_copy(i).wait_send()

        return carry

    def backward_chunk(i, carry):
        at = chunk_at(i)
        here = pl.ds(at, CHUNK)

        @pl.when(section < last)
        def _():
            back_copy(i).wait_recv()

        out_grad = cot[here, :].astype(F32) + arrived[here, :].astype(F32)
        fresh = new_lat[here, :]
        normal = dyn_n[here, :].astype(F32)
        norm_grad = fresh * (out_grad - group_sums(out_grad * fresh))
        by_n = norm_grad * normal
        gain = g_dyn[...].astype(F32)
        dm = norm_grad * gain
        mean_dm = jnp.mean(dm, -1, keepdims=True)
        mean_by_n = jnp.mean(by_n * gain, -1, keepdims=True)
        low = ((dm - mean_dm - normal * mean_by_n) * scales[here, 2:3]).astype(B16)
        arrived[here, :] = low
        dyn_sums[0:8, :] += eight_rows(low.astype(F32))
        dyn_sums[8:16, :] += eight_rows(by_n)
        dyn_sums[16:24, :] += eight_rows(norm_grad)
        pre[0:CHUNK, :] = dot(low, wd[...], NT)
        layer_backward(pre, CHUNK, n2_0, d2_0, scales, 1, at, spg_0, at, sums.at[1], 16)
        pre[0:CHUNK, :] = dot(spg_0[here, :], wm0[...], NT)
        layer_backward(pre, CHUNK, n1_0, d1_0, scales, 0, at, fpg_0, at, sums.at[1], 0)
        back_in = dot(fpg_0[here, :], wi0[0:in_width, :], NT)
        pg_copy(i).wait_recv()
        total = back_in[:, 0:lat] + ig[here, 0:lat] + pair_grad[here, :].astype(F32)
        lat_low[here, :] = total.astype(B16)

        @pl.when(section > 0)
        def _():
            back_copy(i).start()

        ig[here, 0:lat] = total
        grad_store(i).start()
        stat[8:16, :] += eight_rows(m[here, 1:2] * (total * total))
        ig[here, lat:in_width] += back_in[:, lat:in_width]
        return carry

    half_rows = small.shape[0] // 2
    my_rows = pl.ds(pl.multiple_of(core * half_rows, half_rows), half_rows)

    def to_mate(src, dst, k):
        return remote(src, dst, sm_s.at[k], sm_r.at[k], (section, mate))

    def small_to_mate():
        return to_mate(small, small_mate, 0)

    def small_to_chip(other):
        to = lax.rem(chip + other, CHIPS)
        return remote(
            small.at[my_rows], small_chips.at[chip], ch_s.at[other], ch_r.at[chip], (section, base + 2 * to + core)
        )

    def small_from_chip(other):
        to = lax.rem(chip + other, CHIPS)
        return remote(
            small.at[my_rows], small_chips.at[to], ch_s.at[other], ch_r.at[to], (section, base + 2 * to + core)
        )

    def small_to_section(other):
        to = lax.rem(section + other, steps)
        return remote(small_half, small_steps.at[section], tb_s.at[other], tb_r.at[section], (to, d))

    def small_from_section(other):
        source = lax.rem(section + other, steps)
        return remote(small_half, small_steps.at[source], tb_s.at[other], tb_r.at[source], (source, d))

    def small_back():
        return to_mate(small_done.at[my_rows], small_done.at[my_rows], 1)

    def small_over_chips():
        small_to_mate().wait_recv()
        small_to_mate().wait_send()
        small[...] += small_mate[...]
        small_chips[chip] = small[my_rows, :]
        for other in range(1, CHIPS):
            small_to_chip(other).start()

    def small_over_sections():
        for other in range(1, CHIPS):
            small_from_chip(other).wait_recv()
        total = small_chips[0]
        for source in range(1, CHIPS):
            total = total + small_chips[source]
        small_half[...] = total
        small_steps[section] = total
        for other in range(1, steps):
            small_to_section(other).start()

    def small_last():
        for other in range(1, steps):
            small_from_section(other).wait_recv()
        whole = small_steps[0]
        for source in range(1, steps):
            whole = whole + small_steps[source]
        row = lax.broadcasted_iota(jnp.int32, whole.shape, 0) + core * half_rows
        small_done[my_rows, :] = jnp.where(row < tasks, whole, small_half[...])
        small_back().start()
        for other in range(1, CHIPS):
            small_to_chip(other).wait_send()
        for other in range(1, steps):
            small_to_section(other).wait_send()
        small_back().wait_recv()
        small_back().wait_send()

    def send_small():
        table_part = jnp.zeros((tasks, side_width), F32)
        for lo in (0, rows):
            table_part += split_dot_right(one_hot(lo, rows), ig[lo : lo + rows, lat:in_width], TN)
        small[0:tasks, 0:emb] = table_part[:, side_width - emb :]
        for t in range(3):
            line = jnp.sum(dyn_sums[8 * t : 8 * t + 8, :], 0, keepdims=True)
            for part in range(lat // LANES):
                row = tasks + t * (lat // LANES) + part
                small[row : row + 1, :] = line[:, part * LANES : (part + 1) * LANES]
        q_lines = [jnp.sum(q_sums[job], 0, keepdims=True) for job in range(3)]
        for h in range(heads):
            line = jnp.zeros((1, LANES), F32)
            for job in range(3):
                line += jnp.where(first_head + job == h + 1, q_lines[job], 0.0)
            row = tasks + 3 * (lat // LANES) + h
            small[row : row + 1, :] = line
        row = tasks + 3 * (lat // LANES) + heads
        lane = lax.broadcasted_iota(jnp.int32, (1, LANES), 1)
        count = jnp.sum(m[0:rows, 1:2], 0, keepdims=True)
        lat_square = jnp.sum(jnp.sum(stat[0:8, :], 0, keepdims=True), 1, keepdims=True)
        grad_square = jnp.sum(jnp.sum(stat[8:16, :], 0, keepdims=True), 1, keepdims=True)
        small[row : row + 1, :] = jnp.where(
            lane == 0, count, jnp.where(lane == 1, lat_square, jnp.where(lane == 2, grad_square, 0.0))
        )
        small_to_mate().start()

    def turns(turn, carry):
        @pl.when(turn < jobs)
        def _():
            q_job(turn)

        @pl.when(turn == jobs)
        def _():
            load_cot.wait()
            lax.fori_loop(0, chunks, lat_sent, 0)
            lax.fori_loop(0, chunks, backward_chunk, 0)
            send_small()

        @pl.when((turn < jobs - 1) | ((turn == jobs - 1) & (section < last)) | ((turn == jobs) & (section == last)))
        def _():
            weight_grads(jnp.minimum(turn, jobs - 1), True)

        return carry

    lax.fori_loop(0, jobs + 1, turns, 0)

    @pl.when(chip > 0)
    def _():
        pl.semaphore_signal(up_ok, inc=1, device_id=at_chip(jnp.maximum(chip - 1, 0)), device_id_type=MESH)

    @pl.when(chip < CHIPS - 1)
    def _():
        pl.semaphore_signal(
            dn_ok, inc=1, device_id=at_chip(jnp.minimum(chip + 1, CHIPS - 1)), device_id_type=MESH
        )

    @pl.when(chip < CHIPS - 1)
    def _():
        pl.semaphore_wait(up_ok, 1)

    @pl.when(chip > 0)
    def _():
        pl.semaphore_wait(dn_ok, 1)

    weight_grads(jnp.int32(3), False)

    def hops(turn, carry):
        @pl.when(((turn == 0) == lower) & ~edge)
        def _():
            for t in range(CHIPS - 1, 1, -1):
                @pl.when(t > chip)
                def _():
                    for p in range(3):
                        up_copy(t, p).wait_recv()
                        add_piece(up_piece, t, p)
                        up_copy(t, p).start()

        @pl.when(((turn == 0) != lower) & ~edge)
        def _():
            for t in range(CHIPS - 2):
                @pl.when(t < chip)
                def _():
                    for p in range(3):
                        down_copy(t, p).wait_recv()
                        add_piece(down_piece, t, p)
                        down_copy(t, p).start()

        @pl.when(turn == 0)
        def _():
            small_over_sections()

        return carry

    lax.fori_loop(0, 2, hops, 0)

    small_last()
    done = pltpu.make_async_copy(small_done, small_out, out_sem.at[2 * chunks])
    done.start()

    for copy in side_copies:
        copy.wait_send()

    def sends(i, carry):
        pair_copy(i).wait_send()
        pg_copy(i).wait_send()
        grad_store(i).wait()

        @pl.when(section > 0)
        def _():
            back_copy(i).wait_send()

        return carry

    lax.fori_loop(0, chunks, sends, 0)

    def job_done(job, carry):
        def body(other, carry):
            owner_copy(job, lax.rem(chip + other, CHIPS)).wait_send()
            return carry

        lax.fori_loop(1, CHIPS, body, 0)
        keep_copy(job).wait()
        return carry

    lax.fori_loop(0, jobs, job_done, 0)
    for head in range(heads):
        for half in range(2):
            source = (0, CHIPS - 1)[half] if head < 2 else (1, CHIPS - 2)[half]

            @pl.when(chip != source)
            def _():
                remote(
                    half_q.at[0, 0], recv_q.at[head, half], rb_s.at[0, 0], rb_r.at[head, half], at_chip(source)
                ).wait_recv()

    @pl.when(chip > 0)
    def _():
        for p in range(3):
            up_copy(chip, p).wait_recv()
            add_piece(up_piece, chip, p)

    @pl.when(chip < CHIPS - 1)
    def _():
        for p in range(3):
            down_copy(chip, p).wait_recv()
            add_piece(down_piece, chip, p)

    keep_0 = pltpu.make_async_copy(half_0.at[chip], recv_0, own_s.at[3])
    keep_0.start()
    for t in range(CHIPS):
        @pl.when(t > chip)
        def _():
            for p in range(3):
                up_copy(t, p).wait_send()

        @pl.when(t < chip)
        def _():
            for p in range(3):
                down_copy(t, p).wait_send()

    done.wait()
    keep_0.wait()


def finish_kernel(dims, *refs):
    lat, in_width, hid, heads, bins, tasks, emb = dims
    at_mid = in_width + VECS
    at_out = at_mid + hid
    recv_q, recv_0, small_in, lat_in, grad_in = refs[:5]
    lat_out, grad_out, w_in, w_mid, w_dyn, w_q, b_dyn, g_dyn, s_dyn, b_q, table, rms = refs[5:17]
    vecs = refs[17:23]
    part_q, part_0, small, sum_in, sum_mid, lat_held, grad_held, in_sem, out_sem = refs[23:]
    loads = [pltpu.make_async_copy(recv_0, part_0, in_sem.at[0])]
    loads += [pltpu.make_async_copy(recv_q.at[h], part_q.at[h], in_sem.at[1 + h]) for h in range(heads)]
    load_small = pltpu.make_async_copy(small_in, small, in_sem.at[1 + heads])
    through = [
        pltpu.make_async_copy(lat_in, lat_held, in_sem.at[2 + heads]),
        pltpu.make_async_copy(grad_in, grad_held, in_sem.at[3 + heads]),
    ]
    copies = [
        pltpu.make_async_copy(lat_held, lat_out, out_sem.at[0]),
        pltpu.make_async_copy(grad_held, grad_out, out_sem.at[1]),
    ]
    order = list(range(1, heads + 1)) + [0]
    for copy in [loads[h] for h in order] + through + [load_small]:
        copy.start()

    def total(h, lo, hi):
        if h == 0:
            return part_0[lo:hi, :].astype(F32)
        return part_q[h - 1, 0, lo:hi, :].astype(F32) + part_q[h - 1, 1, lo:hi, :].astype(F32)

    for h in order:
        loads[h].wait()
        sum_mid[h] = total(h, at_mid, at_out)
        sum_in[h] = total(h, 0, in_width)
        copies.append(pltpu.make_async_copy(sum_in.at[h], w_in.at[h], out_sem.at[2 + 2 * h]))
        copies.append(pltpu.make_async_copy(sum_mid.at[h], w_mid.at[h], out_sem.at[3 + 2 * h]))
        for copy in copies[-2:]:
            copy.start()
        lines = total(h, in_width, at_mid)
        for t in range(6):
            vecs[t][h] = lines[t : t + 1, :]
        if h:
            w_q[h - 1] = total(h, at_out, at_out + padded(bins))[0:bins, :].reshape(bins, 1, LANES)
    for arriving, leaving in zip(through, copies):
        arriving.wait()
        leaving.start()
    for t in range(lat // LANES):
        w_dyn[:, t * LANES : (t + 1) * LANES] = total(0, at_out + t * LANES, at_out + (t + 1) * LANES)
    load_small.wait()
    table[...] = small[0:tasks, 0:emb]
    for t, out in enumerate((b_dyn, g_dyn, s_dyn)):
        for part in range(lat // LANES):
            row = tasks + t * (lat // LANES) + part
            out[0:1, part * LANES : (part + 1) * LANES] = small[row : row + 1, :]
    at_q = tasks + 3 * (lat // LANES)
    for h in range(heads):
        b_q[h] = small[at_q + h : at_q + h + 1, 0:bins]
    stat = small[at_q + heads : at_q + heads + 1, :]
    count = stat[:, 0:1]
    squares = jnp.concatenate([stat[:, 1:2] / count, stat[:, 2:3] / (count * lat)], 1)
    rms[...] = jnp.sqrt(squares)
    for copy in copies:
        copy.wait()


def on_device(
    latent_in, actions, task_ids, valid, action_mask, bins, fraction, latent_cot,
    w_in, b_in, g_in, beta_in, w_mid, b_mid, g_mid, beta_mid,
    w_dyn_out, b_dyn_out, g_dyn_out, beta_dyn_out, w_q_out, b_q_out, table,
):
    steps = lax.axis_size("section")
    spread = lax.axis_size("dp")
    groups = spread // PEERS
    rows, lat = latent_in.shape
    act_width = actions.shape[2]
    in_width, hid = w_in.shape[2:]
    heads = w_q_out.shape[1]
    bin_count = w_q_out.shape[-1]
    tasks, emb = table.shape
    block = in_width + VECS + hid + padded(bin_count)
    block0 = in_width + VECS + hid + lat
    chunks = rows // CHUNK
    small_rows = padded(tasks + 3 * (lat // LANES) + heads + 1)
    dims = (rows, lat, act_width, in_width, hid, heads, bin_count, tasks, emb, steps)
    anywhere = pl.BlockSpec(memory_space=pl.ANY)
    vmem = pl.BlockSpec(memory_space=pltpu.VMEM)
    hbm = pl.BlockSpec(memory_space=pltpu.HBM)
    dma = pltpu.SemaphoreType.DMA
    both = 2 * rows
    wide = pltpu.VMEM((rows, hid), B16)
    thin = pltpu.VMEM((rows, LANES), F32)
    low = pltpu.VMEM((rows, lat), B16)
    part_low = pltpu.VMEM((QROWS, hid), B16)
    q_wide = pltpu.VMEM((both, hid), B16)
    lat_out, grad_out, recv_q, recv_0, small = pl.pallas_call(
        functools.partial(step_kernel, dims),
        out_shape=[
            jax.ShapeDtypeStruct((rows, lat), B16),
            jax.ShapeDtypeStruct((rows, lat), F32),
            jax.ShapeDtypeStruct((heads, 2, block, LANES), B16),
            jax.ShapeDtypeStruct((block0, LANES), B16),
            jax.ShapeDtypeStruct((small_rows, LANES), F32),
        ],
        in_specs=[anywhere] + [vmem] * 7 + [anywhere] * 5 + [vmem] * 10,
        out_specs=[anywhere] * 5,
        scratch_shapes=[
            pltpu.VMEM((both, 6 * LANES), B16),
            pltpu.VMEM((both, LANES), F32),
            pltpu.VMEM((2, in_width + VECS, hid), B16),
            pltpu.VMEM((2, hid, hid), B16),
            pltpu.VMEM((2, LANES, hid), B16),
            pltpu.VMEM((2, bin_count, hid), B16),
            pltpu.VMEM((in_width + VECS, hid), B16),
            pltpu.VMEM((hid, hid), B16),
            pltpu.VMEM((hid, lat), B16),
            pltpu.VMEM((6, 8, hid), F32),
            pltpu.VMEM((8, LANES), F32),
            pltpu.VMEM((2 * LANES, 2 * LANES), B16),
            pltpu.VMEM((2, 8, rows), F32),
            pltpu.VMEM((2, act_width, rows), B16),
            pltpu.VMEM((VECS, hid), F32),
            pltpu.VMEM((both, in_width), F32),
            q_wide, q_wide, q_wide, q_wide,
            pltpu.VMEM((both, LANES), B16),
            part_low, part_low, part_low, part_low,
            pltpu.VMEM((QROWS, LANES), F32),
            pltpu.VMEM((QROWS, hid), F32),
            wide, wide, wide, wide, wide, wide, wide, wide, thin,
            low,
            pltpu.VMEM((rows, lat), F32),
            low, low, low, low, low,
            pltpu.VMEM((2, CHIPS, block0, LANES), B16),
            pltpu.VMEM((3, CHIPS, block, LANES), B16),
            pltpu.VMEM((CHIPS, block0, LANES), B16),
            pltpu.VMEM((2, 32, hid), F32),
            pltpu.VMEM((3, 8, LANES), F32),
            pltpu.VMEM((24, lat), F32),
            pltpu.VMEM((16, lat), F32),
            pltpu.VMEM((small_rows, LANES), F32),
            pltpu.VMEM((small_rows, LANES), F32),
            pltpu.VMEM((CHIPS, small_rows // 2, LANES), F32),
            pltpu.VMEM((small_rows // 2, LANES), F32),
            pltpu.VMEM((steps, small_rows // 2, LANES), F32),
            pltpu.VMEM((small_rows, LANES), F32),
            dma((10,)), dma((chunks,)), dma((2 * chunks + 1,)),
            dma((chunks,)), dma((chunks,)), dma((chunks,)), dma((chunks,)),
            dma((2,)), dma((2,)), dma((chunks,)), dma((chunks,)), dma((chunks,)), dma((chunks,)),
            dma((4, CHIPS)), dma((4, CHIPS)), dma((4,)), dma((3, CHIPS)), dma((heads, 2)),
            dma((2,)), dma((2,)), dma((CHIPS,)), dma((CHIPS,)), dma((steps,)), dma((steps,)),
            dma((CHIPS, 3)), dma((CHIPS, 3)), dma((CHIPS, 3)), dma((CHIPS, 3)),
            pltpu.SemaphoreType.REGULAR, pltpu.SemaphoreType.REGULAR,
        ],
        compiler_params=pltpu.CompilerParams(
            collective_id=0, has_side_effects=True, vmem_limit_bytes=16350 * 2**12
        ),
        name="step",
    )(
        latent_in, actions[0].T, task_ids[None], valid[None], bins, fraction,
        action_mask.T, table, latent_cot[0],
        w_in[0], w_mid[0], w_dyn_out[0], w_q_out[0].transpose(0, 2, 1),
        b_in[0], g_in[0], beta_in[0], b_mid[0], g_mid[0], beta_mid[0],
        b_dyn_out, g_dyn_out, beta_dyn_out, b_q_out[0],
    )
    across = [[q * PEERS + r for q in range(groups)] for r in range(PEERS)]
    if groups > 1:
        small = lax.psum(small, "dp", axis_index_groups=across)

    def shape(*dims):
        return jax.ShapeDtypeStruct(dims, F32)

    lat_out, grad_out, part_in, part_mid, part_dyn, part_q, b_dyn, g_dyn, s_dyn, q_bias, grad_table, rms, *vecs = (
        pl.pallas_call(
            functools.partial(finish_kernel, (lat, in_width, hid, heads, bin_count, tasks, emb)),
            out_shape=[
                jax.ShapeDtypeStruct((rows, lat), B16),
                shape(rows, lat),
                shape(heads + 1, in_width, LANES),
                shape(heads + 1, hid, LANES),
                shape(LANES, lat),
                shape(heads, bin_count, 1, LANES),
                shape(1, lat), shape(1, lat), shape(1, lat),
                shape(heads, 1, bin_count),
                shape(tasks, emb),
                shape(1, 2),
            ] + [shape(heads + 1, 1, LANES)] * 6,
            in_specs=[hbm] * 5,
            out_specs=[hbm] * 4 + [vmem] * 14,
            scratch_shapes=[
                pltpu.VMEM((heads, 2, block, LANES), B16),
                pltpu.VMEM((block0, LANES), B16),
                pltpu.VMEM((small_rows, LANES), F32),
                pltpu.VMEM((heads + 1, in_width, LANES), F32),
                pltpu.VMEM((heads + 1, hid, LANES), F32),
                pltpu.VMEM((rows, lat), B16),
                pltpu.VMEM((rows, lat), F32),
                dma((heads + 4,)),
                dma((2 * heads + 4,)),
            ],
            compiler_params=pltpu.CompilerParams(vmem_limit_bytes=60 * 2**20),
            name="finish",
        )(recv_q, recv_0, small, lat_out, grad_out)
    )

    def owned(piece, dim):
        if groups == 1:
            return piece
        piece = lax.psum_scatter(piece, "dp", scatter_dimension=dim, axis_index_groups=across, tiled=True)
        moves = [(q * PEERS + r, r * groups + q) for q in range(groups) for r in range(PEERS)]
        return lax.ppermute(piece, "dp", moves)

    part_in, part_mid, part_q = owned(part_in, 2), owned(part_mid, 2), owned(part_q, 3)
    part_dyn = owned(part_dyn, 0)
    vecs = [owned(v, 2).transpose(1, 0, 2) for v in vecs]
    return (
        lat_out[None],
        grad_out[None],
        part_in[None],
        *vecs[:3],
        part_mid[None],
        *vecs[3:],
        part_dyn[None],
        b_dyn,
        g_dyn,
        s_dyn,
        part_q.transpose(2, 0, 3, 1),
        q_bias.transpose(1, 0, 2),
        grad_table,
        rms,
    )


def solution(mesh):
    placed = (
        P("dp", None),
        P("section", "dp", None),
        P("dp"),
        P("dp"),
        P(),
        P("section", "dp"),
        P("section", "dp"),
        P("section", "dp", None),
        P("section", None, None, None),
        P("section", None, None),
        P("section", None, None),
        P("section", None, None),
        P("section", None, None, None),
        P("section", None, None),
        P("section", None, None),
        P("section", None, None),
        P("section", None, None),
        P("section", None),
        P("section", None),
        P("section", None),
        P("section", None, None, None),
        P("section", None, None),
        P(),
    )
    return jax.shard_map(
        on_device,
        mesh=mesh,
        in_specs=placed,
        out_specs=(
            P("section", "dp", None),
            P("section", "dp", None),
            P("section", None, None, "dp"),
            P("section", None, "dp"),
            P("section", None, "dp"),
            P("section", None, "dp"),
            P("section", None, None, "dp"),
            P("section", None, "dp"),
            P("section", None, "dp"),
            P("section", None, "dp"),
            P("section", "dp", None),
            P("section", None),
            P("section", None),
            P("section", None),
            P("section", None, "dp", None),
            P("section", None, None),
            P(),
            P("section", None),
        ),
        check_vma=False,
    )
```

```python
import functools

import jax
import jax.numpy as jnp
from jax import lax
from jax.experimental import pallas as pl
from jax.experimental.pallas import tpu as pltpu
from jax.sharding import PartitionSpec as P

GROUP = 8
EPS = 1e-05
F32 = jnp.float32
B16 = jnp.bfloat16
MESH = pl.DeviceIdType.MESH

LANES = 128
CHIPS = 4
PEERS = 2 * CHIPS
CHUNK = 128
QROWS = 256
SUB = 256
VECS = 16

NN = (((1,), (0,)), ((), ()))
NT = (((1,), (1,)), ((), ()))
TN = (((0,), (0,)), ((), ()))


def dot(a, b, dims=NN):
    return lax.dot_general(a, b, dims, preferred_element_type=F32)


def split_dot(a, b, dims=NN):
    high = a.astype(B16)
    low = (a - high.astype(F32)).astype(B16)
    return dot(high, b, dims) + dot(low, b, dims)


def split_dot_right(a, b, dims):
    high = b.astype(B16)
    low = (b - high.astype(F32)).astype(B16)
    return dot(a, high, dims) + dot(a, low, dims)


def norm_mish(x, gain, shift):
    center = x - jnp.mean(x, -1, keepdims=True)
    spread = jnp.mean(center * center, -1, keepdims=True)
    scale = lax.rsqrt(spread + EPS)
    n = center * scale
    u = n * gain + shift
    w = jnp.exp(jnp.minimum(u, 30.0))
    top = w * (w + 2.0)
    over = pltpu.reciprocal(top + 2.0, approx=True)
    act = u * (top * over)
    slope = (top + 4.0 * (u * (top - w)) * over) * (over * gain)
    return act, n, slope, scale


def padded(count):
    return (count + 15) // 16 * 16


def tiles(size, step=256):
    return [(lo, min(lo + step, size)) for lo in range(0, size, step)]


def eight_rows(x):
    return x.reshape(x.shape[0] // 8, 8, x.shape[1]).sum(0)


def each_sub(count, body):
    sub = min(SUB, count)
    for j in range(0, count, sub):
        body(j, sub)


def layer_forward(pre, count, bias, gain, shift, act_ref, act_at, n_ref, slope_ref, scale_ref, lane, at):
    def body(j, sub):
        x = pre[pl.ds(j, sub), :]
        if bias is not None:
            x = x + bias
        act, n, slope, scale = norm_mish(x, gain, shift)
        act_ref[pl.ds(act_at + j, sub), :] = act.astype(B16)
        here = pl.ds(at + j, sub)
        n_ref[here, :] = n.astype(n_ref.dtype)
        slope_ref[here, :] = slope.astype(slope_ref.dtype)
        scale_ref[here, lane : lane + 1] = scale

    each_sub(count, body)


def layer_backward(pre, count, n_ref, slope_ref, scale_ref, lane, at, out_ref, out_at, sums, first):
    def body(j, sub):
        here = pl.ds(at + j, sub)
        n = n_ref[here, :].astype(F32)
        dn = pre[pl.ds(j, sub), :] * slope_ref[here, :].astype(F32)
        by_n = dn * n
        mean_dn = jnp.mean(dn, -1, keepdims=True)
        mean_by_n = jnp.mean(by_n, -1, keepdims=True)
        out = (dn - mean_dn - n * mean_by_n) * scale_ref[here, lane : lane + 1]
        out_ref[pl.ds(out_at + j, sub), :] = out.astype(B16)
        sums[first : first + 8, :] += eight_rows(by_n)
        sums[first + 8 : first + 16, :] += eight_rows(dn)

    each_sub(count, body)


def step_kernel(dims, *refs):
    rows, lat, act_width, in_width, hid, heads, bins, tasks, emb, steps = dims
    side_width = in_width - lat
    at_mid = in_width + VECS
    at_out = at_mid + hid
    block = at_out + padded(bins)
    block0 = at_out + lat
    both = 2 * rows
    ones_at = in_width // LANES * LANES
    pieces = ((0, at_mid), (at_mid, at_out), (at_out, block0))
    (
        lat_in, acts, task, valid, bin_at, part_of, amask, table, cot_in, w_in, w_mid, w_dyn, w_q,
        b_in, g_in, s_in, b_mid, g_mid, s_mid, b_dyn, g_dyn, s_dyn, b_q,
        lat_out, grad_out, recv_q, recv_0, small_out,
        x, m, wi, wm, wq, wq_raw, wi0, wm0, wd, vec, bq, diag,
        lines, acting, vec_lines, ig, act1, act2, spg, fpg, qg, n1, d1, n2, d2, q_scales, pre,
        act1_0, act2_0, spg_0, fpg_0, n1_0, d1_0, n2_0, d2_0, scales,
        dyn_n, new_lat, lat_low, cot, arrived, pair_grad, pair_send,
        gb, half_q, half_0, sums, q_sums, dyn_sums, stat, small, small_mate, small_chips, small_half, small_steps, small_done,
        w_sem, in_sem, out_sem, lat_s, lat_r, px_s, px_r, side_s, side_r, pg_s, pg_r, gr_s, gr_r,
        half_s, half_r, own_s, rb_s, rb_r, sm_s, sm_r, ch_s, ch_r, tb_s, tb_r, up_s, up_r, dn_s, dn_r, up_ok, dn_ok,
    ) = refs
    section = lax.axis_index("section")
    d = lax.axis_index("dp")
    place = lax.rem(d, PEERS)
    base = d - place
    chip = place // 2
    core = lax.rem(place, 2)
    edge = (chip == 0) | (chip == CHIPS - 1)
    lower = chip < CHIPS // 2
    side_of = chip // 2
    last = steps - 1
    mate = base + chip * 2 + (1 - core)
    pair = base + (chip + 1 - 2 * lax.rem(chip, 2)) * 2 + core
    following = jnp.minimum(section + 1, last)
    before = jnp.maximum(section - 1, 0)
    chunks = rows // CHUNK
    jobs = jnp.where(edge, 2, 3)
    held = (section == steps - 1) & edge
    farthest = CHIPS - 1 - chip
    first_head = jnp.where(edge, 1, 3)

    def remote(src, dst, send, recv, to):
        return pltpu.make_async_remote_copy(
            src_ref=src, dst_ref=dst, send_sem=send, recv_sem=recv, device_id=to, device_id_type=MESH
        )

    def chunk_at(i):
        return pl.multiple_of(i * CHUNK, CHUNK)

    loads = [
        pltpu.make_async_copy(w_in.at[0], wi0.at[0:in_width], w_sem.at[0]),
        pltpu.make_async_copy(w_mid.at[0], wm0, w_sem.at[1]),
        pltpu.make_async_copy(w_dyn, wd, w_sem.at[2]),
    ]

    def job_loads(job):
        slot = lax.rem(job, 2)
        h = first_head + job
        return [
            pltpu.make_async_copy(w_in.at[h], wi.at[slot, 0:in_width], w_sem.at[3 + 3 * slot]),
            pltpu.make_async_copy(w_mid.at[h], wm.at[slot], w_sem.at[4 + 3 * slot]),
            pltpu.make_async_copy(w_q.at[h - 1], wq_raw.at[slot], w_sem.at[5 + 3 * slot]),
        ]

    load_cot = pltpu.make_async_copy(cot_in, cot, w_sem.at[9])

    def load_lat(i):
        here = pl.ds(chunk_at(i), CHUNK)
        return pltpu.make_async_copy(lat_in.at[here], x.at[here, 0:lat], in_sem.at[i])

    barrier = pltpu.get_barrier_semaphore()
    for other in range(1, PEERS):
        to = base + lax.rem(place + other, PEERS)
        pl.semaphore_signal(barrier, inc=1, device_id=(section, to), device_id_type=MESH)
    for other in range(1, steps):
        to = lax.rem(section + other, steps)
        pl.semaphore_signal(barrier, inc=1, device_id=(to, d), device_id_type=MESH)

    loads[0].start()

    @pl.when(section == 0)
    def _():
        for i in range(chunks):
            load_lat(i).start()

    for copy in loads[1:] + job_loads(jnp.int32(0)) + job_loads(jnp.int32(1)):
        copy.start()
    load_cot.start()

    head_lines = [task[...].astype(F32), valid[...].astype(F32), bin_at[...].astype(F32), part_of[...]]
    lines[0] = jnp.concatenate(head_lines + [jnp.zeros((4, rows), F32)], 0)
    acting[0] = acts[...]

    def one_hot(lo, count):
        task_lane = lax.broadcasted_iota(jnp.int32, (count, tasks), 1).astype(F32)
        return (m[lo : lo + count, 0:1] == task_lane).astype(F32).astype(B16)

    def prepare(which):
        lo = which * rows
        m[lo : lo + rows, 0:8] = lines[which].T
        hot = one_hot(lo, rows)
        mask = dot(amask[...].astype(F32).astype(B16), hot, NT)
        used = (acting[which].astype(F32) * mask).T
        x[lo : lo + rows, lat:in_width] = jnp.concatenate(
            [used.astype(B16), dot(hot, table[...]).astype(B16)], 1
        )

    lane = lax.broadcasted_iota(jnp.int32, (both, LANES), 1)
    x[:, ones_at : ones_at + LANES] = (lane == in_width - ones_at).astype(F32).astype(B16)
    prepare(0)
    for t, source in enumerate((b_in, g_in, s_in, b_mid, g_mid, s_mid)):
        vec[t, 0 : heads + 1, :] = source[...].astype(F32)
    shift = GROUP.bit_length() - 1
    diag[...] = (
        lax.shift_right_logical(lax.broadcasted_iota(jnp.int32, diag.shape, 0), shift)
        == lax.shift_right_logical(lax.broadcasted_iota(jnp.int32, diag.shape, 1), shift)
    ).astype(F32).astype(B16)

    def group_sums(values):
        width = diag.shape[0]
        return jnp.concatenate(
            [split_dot(values[:, lo : lo + width], diag[...]) for lo in range(0, lat, width)], 1
        )

    def bias_rows(h):
        line = lax.broadcasted_iota(jnp.int32, (VECS, hid), 0)
        return jnp.where(line == 0, vec[0, pl.ds(h, 1), :], 0.0).astype(B16)

    wi0[in_width:at_mid, :] = bias_rows(0)
    stat[...] = jnp.zeros(stat.shape, F32)

    def clear():
        bq[...] = jnp.full(bq.shape, -1e30, F32)
        bq[0:heads, 0:bins] = b_q[...].astype(F32)
        wq[...] = jnp.zeros(wq.shape, B16)
        sums[...] = jnp.zeros(sums.shape, F32)
        ig[...] = jnp.zeros(ig.shape, F32)
        q_sums[...] = jnp.zeros(q_sums.shape, F32)
        dyn_sums[...] = jnp.zeros(dyn_sums.shape, F32)
        small[...] = jnp.zeros(small.shape, F32)

    pl.semaphore_wait(barrier, PEERS - 1 + steps - 1)

    side_copies = [
        remote(lines.at[0], lines.at[1], side_s.at[0], side_r.at[0], (section, pair)),
        remote(acting.at[0], acting.at[1], side_s.at[1], side_r.at[1], (section, pair)),
    ]
    for copy in side_copies:
        copy.start()

    def settle():
        clear()
        for copy in side_copies:
            copy.wait_recv()
        prepare(1)

    @pl.when(section == last)
    def _():
        arrived[...] = jnp.zeros(arrived.shape, B16)

    @pl.when(section > 0)
    def _():
        settle()

    for copy in loads:
        copy.wait()

    def vec_of(t, h):
        return vec[t, pl.ds(h, 1), :]

    def lat_copy(i):
        here = pl.ds(chunk_at(i), CHUNK)
        return remote(
            lat_low.at[here], x.at[here, 0:lat], lat_s.at[i], lat_r.at[i], (following, d)
        )

    def pair_copy(i):
        here = chunk_at(i)
        return remote(
            x.at[pl.ds(here, CHUNK), 0:lat], x.at[pl.ds(rows + here, CHUNK), 0:lat],
            px_s.at[i], px_r.at[i], (section, pair),
        )

    def lat_store(i):
        here = pl.ds(chunk_at(i), CHUNK)
        return pltpu.make_async_copy(lat_low.at[here], lat_out.at[here], out_sem.at[i])

    def forward_chunk(i, carry):
        at = chunk_at(i)
        here = pl.ds(at, CHUNK)

        @pl.when(section > 0)
        def _():
            lat_copy(i).wait_recv()

        @pl.when(section == 0)
        def _():
            load_lat(i).wait()

        pair_copy(i).start()
        pre[0:CHUNK, :] = dot(x[here, 0:at_mid], wi0[...])
        layer_forward(
            pre, CHUNK, None, vec[1, 0:1, :], vec[2, 0:1, :], act1_0, at, n1_0, d1_0, scales, 0, at
        )
        pre[0:CHUNK, :] = dot(act1_0[here, :], wm0[...])
        layer_forward(
            pre, CHUNK, vec[3, 0:1, :], vec[4, 0:1, :], vec[5, 0:1, :], act2_0, at, n2_0, d2_0, scales, 1, at
        )
        out = dot(act2_0[here, :], wd[...]) + b_dyn[...].astype(F32)
        center = out - jnp.mean(out, -1, keepdims=True)
        scale = lax.rsqrt(jnp.mean(center * center, -1, keepdims=True) + EPS)
        normal = center * scale
        dyn_n[here, :] = normal.astype(B16)
        scales[here, 2:3] = scale
        power = jnp.exp(normal * g_dyn[...].astype(F32) + s_dyn[...].astype(F32))
        fresh = power * pltpu.reciprocal(group_sums(power), approx=True)
        new_lat[here, :] = fresh
        low = fresh.astype(B16)
        lat_low[here, :] = low

        @pl.when(section < last)
        def _():
            lat_copy(i).start()

        lat_store(i).start()
        wide = low.astype(F32)
        stat[0:8, :] += eight_rows(m[here, 1:2] * (wide * wide))
        return carry

    lax.fori_loop(0, chunks, forward_chunk, 0)

    @pl.when(section == 0)
    def _():
        settle()

    def pg_copy(i):
        here = pl.ds(chunk_at(i), CHUNK)
        return remote(
            pair_send.at[here], pair_grad.at[here], pg_s.at[i], pg_r.at[i], (section, pair)
        )

    def q_chunk(job, at):
        here = pl.ds(at, QROWS)
        h = first_head + job
        slot = lax.rem(job, 2)
        pre[...] = dot(x[here, 0:at_mid], wi[slot])
        layer_forward(
            pre, QROWS, None, vec_of(1, h), vec_of(2, h), act1, at, n1, d1, q_scales, 0, 0
        )
        pre[...] = dot(act1[here, :], wm[slot])
        layer_forward(
            pre, QROWS, vec_of(3, h), vec_of(4, h), vec_of(5, h), act2, at, n2, d2, q_scales, 1, 0
        )
        logits = dot(act2[here, :], wq[slot], NT) + bq[pl.ds(h - 1, 1), :]
        power = jnp.exp(logits - jnp.max(logits, -1, keepdims=True))
        chance = power / jnp.sum(power, -1, keepdims=True)
        lane = lax.broadcasted_iota(jnp.int32, (QROWS, LANES), 1).astype(F32)
        low_bin = m[here, 2:3]
        part = m[here, 3:4]
        target = jnp.where(lane == low_bin, 1.0 - part, 0.0) + jnp.where(lane == low_bin + 1.0, part, 0.0)
        grad = (m[here, 1:2] * (chance - target)).astype(B16)
        qg[here, :] = grad
        q_sums[job] += eight_rows(grad.astype(F32))
        pre[...] = dot(grad, wq[slot])
        layer_backward(pre, QROWS, n2, d2, q_scales, 1, 0, spg, at, sums.at[0], 16)
        pre[...] = dot(spg[here, :], wm[slot], NT)
        layer_backward(pre, QROWS, n1, d1, q_scales, 0, 0, fpg, at, sums.at[0], 0)
        for lo, hi in tiles(in_width):
            ig[here, lo:hi] += dot(fpg[here, :], wi[slot, lo:hi, :], NT)

    q_chunks = both // QROWS
    own_chunks = rows // QROWS

    def q_job(job):
        for copy in job_loads(job):
            copy.wait()
        slot = lax.rem(job, 2)
        wq[slot, 0:bins, :] = wq_raw[slot]
        wi[slot, in_width:at_mid, :] = bias_rows(first_head + job)
        sums[0] = jnp.zeros(sums.shape[1:], F32)

        def body(i, carry):
            which = lax.rem(i + jnp.where(job == 0, 0, own_chunks), q_chunks)
            at = pl.multiple_of(which * QROWS, QROWS)

            @pl.when((job == 0) & (which == own_chunks))
            def _():
                def pair_here(j, carry):
                    pair_copy(j).wait_recv()
                    return carry

                lax.fori_loop(0, chunks, pair_here, 0)

            q_chunk(job, at)

            @pl.when((job == jobs - 1) & (which >= own_chunks))
            def _():
                for k in range(QROWS // CHUNK):
                    j = (which - own_chunks) * (QROWS // CHUNK) + k
                    to = chunk_at(j)
                    pair_send[pl.ds(to, CHUNK), :] = ig[pl.ds(rows + to, CHUNK), 0:lat].astype(B16)
                    pg_copy(j).start()

            return carry

        lax.fori_loop(0, q_chunks, body, 0)

        @pl.when(job + 2 < jobs)
        def _():
            for copy in job_loads(job + 2):
                copy.start()

    def half_copy(job, z, q):
        if q:
            src, dst = gb.at[1 - core, z, 0:block], half_q.at[job, z]
        else:
            src, dst = gb.at[1 - core, z], half_0.at[z]
        return remote(src, dst, half_s.at[job, z], half_r.at[job, z], (section, mate))

    def owner_copy(job, z):
        head = first_head + job - 1
        return remote(
            half_q.at[job, z], recv_q.at[head, side_of], rb_s.at[job, z], rb_r.at[head, side_of],
            (section, base + 2 * z + core),
        )

    def keep_copy(job):
        return pltpu.make_async_copy(
            half_q.at[job, chip], recv_q.at[first_head + job - 1, side_of], own_s.at[job]
        )

    def add_rows(dst, src, size):
        step = size // 4 // 16 * 16
        for part in range(4):
            span = slice(part * step, size if part == 3 else (part + 1) * step)
            dst[span, :] = (dst[span, :].astype(F32) + src[span, :].astype(F32)).astype(B16)

    def at_chip(z):
        return (section, base + 2 * z + core)

    def stripe(z):
        return pl.ds(pl.multiple_of(z * LANES, LANES), LANES)

    def up_piece(z, p):
        size = pieces[p][1] - pieces[p][0]
        return (act1.at[0:size, stripe(z)], act1.at[0:size, stripe(CHIPS + z)], act2.at[0:size, stripe(z)])[p]

    def down_piece(z, p):
        size = pieces[p][1] - pieces[p][0]
        return (spg.at[0:size, stripe(z)], spg.at[0:size, stripe(CHIPS + z)], act2.at[0:size, stripe(CHIPS + z)])[p]

    def up_copy(z, p):
        return remote(
            half_0.at[z, pieces[p][0] : pieces[p][1]], up_piece(z, p), up_s.at[z, p], up_r.at[z, p],
            at_chip(jnp.minimum(chip + 1, CHIPS - 1)),
        )

    def down_copy(z, p):
        return remote(
            half_0.at[z, pieces[p][0] : pieces[p][1]], down_piece(z, p), dn_s.at[z, p], dn_r.at[z, p],
            at_chip(jnp.maximum(chip - 1, 0)),
        )

    def add_piece(piece, z, p):
        lo, hi = pieces[p]
        half_0[z, lo:hi, :] = (half_0[z, lo:hi, :].astype(F32) + piece(z, p)[...].astype(F32)).astype(B16)

    def weight_grads(job, q):
        if q:
            count, a1, a2, sp, fp, own_sums = both, act1, act2, spg, fpg, 0
        else:
            count, a1, a2, sp, fp, own_sums = rows, act1_0, act2_0, spg_0, fpg_0, 1
        size = block if q else block0
        h = first_head + job if q else 0
        line_at = lax.broadcasted_iota(jnp.int32, (VECS, hid), 0)
        vectors = jnp.zeros((VECS, hid), F32)
        for t, (first, gain) in enumerate(((0, 1), (8, 1), (None, None), (16, 4), (24, 4))):
            if gain is not None:
                line = jnp.sum(sums[own_sums, first : first + 8, :], 0, keepdims=True) / vec_of(gain, h)
                vectors = jnp.where(line_at == t + 1, line, vectors)
        vec_lines[...] = vectors
        row_at = lax.broadcasted_iota(jnp.int32, (VECS, 2 * LANES), 0)

        def order(i):
            far_first = jnp.where(lower, CHIPS - 1 - i, i)
            pair_first = lax.rem(jnp.where(lower, CHIPS - i, i + CHIPS - 1), CHIPS)
            return jnp.where(edge, far_first, pair_first)

        def make(z):
            cols = pl.ds(pl.multiple_of(z * 2 * LANES, 2 * LANES), 2 * LANES)
            for left, right, first, size_of in ((x, fp, 0, at_mid), (a1, sp, at_mid, hid)):
                for lo, hi in tiles(size_of):
                    grad = dot(left[0:count, lo:hi], right[0:count, cols], TN)
                    if left is x and hi == at_mid:
                        plain = grad[0 : in_width - lo]
                        bias_mid = dot(x[0:count, ones_at : ones_at + LANES], sp[0:count, cols], TN)
                        bias_mid = bias_mid[in_width - ones_at : in_width - ones_at + 1]
                        lines_here = grad[in_width - lo :] + vec_lines[:, cols]
                        grad = jnp.concatenate([plain, jnp.where(row_at == 3, bias_mid, lines_here)], 0)
                    for p in range(2):
                        gb[p, z, first + lo : first + hi, :] = grad[:, p * LANES : (p + 1) * LANES].astype(B16)
            if q:
                g_out = dot(qg[0:count, :], a2[0:count, cols], TN)
                for p in range(2):
                    gb[p, z, at_out:block, :] = g_out[0 : block - at_out, p * LANES : (p + 1) * LANES].astype(B16)
            else:
                g_out = dot(a2[0:count, cols], arrived[0:count, :], TN)
                for p in range(2):
                    for t in range(lat // LANES):
                        gb[p, z, at_out + t * LANES : at_out + (t + 1) * LANES, :] = g_out[
                            p * LANES : (p + 1) * LANES, t * LANES : (t + 1) * LANES
                        ].astype(B16)
            half_copy(job, z, q).start()

        def finish(z):
            half_copy(job, z, q).wait_recv()
            if q:
                add_rows(half_q.at[job, z], gb.at[core, z], size)

                @pl.when((z != chip) & ~((job == jobs - 1) & held & (z == farthest)))
                def _():
                    owner_copy(job, z).start()

                @pl.when(z == chip)
                def _():
                    keep_copy(job).start()
            else:
                add_rows(half_0.at[z], gb.at[core, z], size)

                @pl.when((chip == 0) & (z != chip))
                def _():
                    for p in range(3):
                        up_copy(z, p).start()

                @pl.when((chip == CHIPS - 1) & (z != chip))
                def _():
                    for p in range(3):
                        down_copy(z, p).start()

        def body(i, carry):
            @pl.when(i < CHIPS)
            def _():
                make(order(i))

            if not q:
                @pl.when(i == 1)
                def _():
                    small_over_chips()

            @pl.when(i > 0)
            def _():
                finish(order(i - 1))

            return carry

        lax.fori_loop(0, CHIPS + 1, body, 0)

        def sent(z, carry):
            half_copy(job, z, q).wait_send()
            return carry

        lax.fori_loop(0, CHIPS, sent, 0)

    def back_copy(i):
        here = pl.ds(chunk_at(i), CHUNK)
        return remote(lat_low.at[here], arrived.at[here], gr_s.at[i], gr_r.at[i], (before, d))

    def grad_store(i):
        here = pl.ds(chunk_at(i), CHUNK)
        return pltpu.make_async_copy(ig.at[here, 0:lat], grad_out.at[here], out_sem.at[chunks + i])

    def lat_sent(i, carry):
        lat_store(i).wait()

        @pl.when(section < last)
        def _():
            lat_copy(i).wait_send()

        return carry

    def backward_chunk(i, carry):
        at = chunk_at(i)
        here = pl.ds(at, CHUNK)

        @pl.when(section < last)
        def _():
            back_copy(i).wait_recv()

        out_grad = cot[here, :].astype(F32) + arrived[here, :].astype(F32)
        fresh = new_lat[here, :]
        normal = dyn_n[here, :].astype(F32)
        norm_grad = fresh * (out_grad - group_sums(out_grad * fresh))
        by_n = norm_grad * normal
        gain = g_dyn[...].astype(F32)
        dm = norm_grad * gain
        mean_dm = jnp.mean(dm, -1, keepdims=True)
        mean_by_n = jnp.mean(by_n * gain, -1, keepdims=True)
        low = ((dm - mean_dm - normal * mean_by_n) * scales[here, 2:3]).astype(B16)
        arrived[here, :] = low
        dyn_sums[0:8, :] += eight_rows(low.astype(F32))
        dyn_sums[8:16, :] += eight_rows(by_n)
        dyn_sums[16:24, :] += eight_rows(norm_grad)
        pre[0:CHUNK, :] = dot(low, wd[...], NT)
        layer_backward(pre, CHUNK, n2_0, d2_0, scales, 1, at, spg_0, at, sums.at[1], 16)
        pre[0:CHUNK, :] = dot(spg_0[here, :], wm0[...], NT)
        layer_backward(pre, CHUNK, n1_0, d1_0, scales, 0, at, fpg_0, at, sums.at[1], 0)
        back_in = dot(fpg_0[here, :], wi0[0:in_width, :], NT)
        pg_copy(i).wait_recv()

        @pl.when((i == chunks - 1) & held)
        def _():
            owner_copy(jobs - 1, farthest).start()

        total = back_in[:, 0:lat] + ig[here, 0:lat] + pair_grad[here, :].astype(F32)
        lat_low[here, :] = total.astype(B16)

        @pl.when(section > 0)
        def _():
            back_copy(i).start()

        ig[here, 0:lat] = total
        grad_store(i).start()
        stat[8:16, :] += eight_rows(m[here, 1:2] * (total * total))
        ig[here, lat:in_width] += back_in[:, lat:in_width]
        return carry

    half_rows = small.shape[0] // 2
    my_rows = pl.ds(pl.multiple_of(core * half_rows, half_rows), half_rows)

    def to_mate(src, dst, k):
        return remote(src, dst, sm_s.at[k], sm_r.at[k], (section, mate))

    def small_to_mate():
        return to_mate(small, small_mate, 0)

    def small_to_chip(other):
        to = lax.rem(chip + other, CHIPS)
        return remote(
            small.at[my_rows], small_chips.at[chip], ch_s.at[other], ch_r.at[chip], (section, base + 2 * to + core)
        )

    def small_from_chip(other):
        to = lax.rem(chip + other, CHIPS)
        return remote(
            small.at[my_rows], small_chips.at[to], ch_s.at[other], ch_r.at[to], (section, base + 2 * to + core)
        )

    def small_to_section(other):
        to = lax.rem(section + other, steps)
        return remote(small_half, small_steps.at[section], tb_s.at[other], tb_r.at[section], (to, d))

    def small_from_section(other):
        source = lax.rem(section + other, steps)
        return remote(small_half, small_steps.at[source], tb_s.at[other], tb_r.at[source], (source, d))

    def small_back():
        return to_mate(small_done.at[my_rows], small_done.at[my_rows], 1)

    def small_over_chips():
        small_to_mate().wait_recv()
        small_to_mate().wait_send()
        small[...] += small_mate[...]
        small_chips[chip] = small[my_rows, :]
        for other in range(1, CHIPS):
            small_to_chip(other).start()

    def small_over_sections():
        for other in range(1, CHIPS):
            small_from_chip(other).wait_recv()
        total = small_chips[0]
        for source in range(1, CHIPS):
            total = total + small_chips[source]
        small_half[...] = total
        small_steps[section] = total
        for other in range(1, steps):
            small_to_section(other).start()

    def small_last():
        for other in range(1, steps):
            small_from_section(other).wait_recv()
        whole = small_steps[0]
        for source in range(1, steps):
            whole = whole + small_steps[source]
        row = lax.broadcasted_iota(jnp.int32, whole.shape, 0) + core * half_rows
        small_done[my_rows, :] = jnp.where(row < tasks, whole, small_half[...])
        small_back().start()
        for other in range(1, CHIPS):
            small_to_chip(other).wait_send()
        for other in range(1, steps):
            small_to_section(other).wait_send()
        small_back().wait_recv()
        small_back().wait_send()

    def send_small():
        table_part = jnp.zeros((tasks, side_width), F32)
        for lo in (0, rows):
            table_part += split_dot_right(one_hot(lo, rows), ig[lo : lo + rows, lat:in_width], TN)
        small[0:tasks, 0:emb] = table_part[:, side_width - emb :]
        for t in range(3):
            line = jnp.sum(dyn_sums[8 * t : 8 * t + 8, :], 0, keepdims=True)
            for part in range(lat // LANES):
                row = tasks + t * (lat // LANES) + part
                small[row : row + 1, :] = line[:, part * LANES : (part + 1) * LANES]
        q_lines = [jnp.sum(q_sums[job], 0, keepdims=True) for job in range(3)]
        for h in range(heads):
            line = jnp.zeros((1, LANES), F32)
            for job in range(3):
                line += jnp.where(first_head + job == h + 1, q_lines[job], 0.0)
            row = tasks + 3 * (lat // LANES) + h
            small[row : row + 1, :] = line
        row = tasks + 3 * (lat // LANES) + heads
        lane = lax.broadcasted_iota(jnp.int32, (1, LANES), 1)
        count = jnp.sum(m[0:rows, 1:2], 0, keepdims=True)
        lat_square = jnp.sum(jnp.sum(stat[0:8, :], 0, keepdims=True), 1, keepdims=True)
        grad_square = jnp.sum(jnp.sum(stat[8:16, :], 0, keepdims=True), 1, keepdims=True)
        small[row : row + 1, :] = jnp.where(
            lane == 0, count, jnp.where(lane == 1, lat_square, jnp.where(lane == 2, grad_square, 0.0))
        )
        small_to_mate().start()

    waits = (section == last) & ~edge

    def turns(turn, carry):
        @pl.when(turn < jobs)
        def _():
            q_job(turn)

        @pl.when(turn == jobs)
        def _():
            load_cot.wait()
            lax.fori_loop(0, chunks, lat_sent, 0)
            lax.fori_loop(0, chunks, backward_chunk, 0)
            send_small()

        @pl.when((turn < jobs - 1) | ((turn == jobs - 1) & ~waits) | ((turn == jobs) & waits))
        def _():
            weight_grads(jnp.minimum(turn, jobs - 1), True)

        return carry

    lax.fori_loop(0, jobs + 1, turns, 0)

    @pl.when(chip > 0)
    def _():
        pl.semaphore_signal(up_ok, inc=1, device_id=at_chip(jnp.maximum(chip - 1, 0)), device_id_type=MESH)

    @pl.when(chip < CHIPS - 1)
    def _():
        pl.semaphore_signal(
            dn_ok, inc=1, device_id=at_chip(jnp.minimum(chip + 1, CHIPS - 1)), device_id_type=MESH
        )

    @pl.when(chip < CHIPS - 1)
    def _():
        pl.semaphore_wait(up_ok, 1)

    @pl.when(chip > 0)
    def _():
        pl.semaphore_wait(dn_ok, 1)

    weight_grads(jnp.int32(3), False)

    def hops(turn, carry):
        @pl.when(((turn == 0) == lower) & ~edge)
        def _():
            for t in range(CHIPS - 1, 1, -1):
                @pl.when(t > chip)
                def _():
                    for p in range(3):
                        up_copy(t, p).wait_recv()
                        add_piece(up_piece, t, p)
                        up_copy(t, p).start()

        @pl.when(((turn == 0) != lower) & ~edge)
        def _():
            for t in range(CHIPS - 2):
                @pl.when(t < chip)
                def _():
                    for p in range(3):
                        down_copy(t, p).wait_recv()
                        add_piece(down_piece, t, p)
                        down_copy(t, p).start()

        @pl.when(turn == 0)
        def _():
            small_over_sections()

        return carry

    lax.fori_loop(0, 2, hops, 0)

    small_last()
    done = pltpu.make_async_copy(small_done, small_out, out_sem.at[2 * chunks])
    done.start()

    for copy in side_copies:
        copy.wait_send()

    def sends(i, carry):
        pair_copy(i).wait_send()
        pg_copy(i).wait_send()
        grad_store(i).wait()

        @pl.when(section > 0)
        def _():
            back_copy(i).wait_send()

        return carry

    lax.fori_loop(0, chunks, sends, 0)

    def job_done(job, carry):
        def body(other, carry):
            owner_copy(job, lax.rem(chip + other, CHIPS)).wait_send()
            return carry

        lax.fori_loop(1, CHIPS, body, 0)
        keep_copy(job).wait()
        return carry

    lax.fori_loop(0, jobs, job_done, 0)
    for head in range(heads):
        for half in range(2):
            source = (0, CHIPS - 1)[half] if head < 2 else (1, CHIPS - 2)[half]

            @pl.when(chip != source)
            def _():
                remote(
                    half_q.at[0, 0], recv_q.at[head, half], rb_s.at[0, 0], rb_r.at[head, half], at_chip(source)
                ).wait_recv()

    @pl.when(chip > 0)
    def _():
        for p in range(3):
            up_copy(chip, p).wait_recv()
            add_piece(up_piece, chip, p)

    @pl.when(chip < CHIPS - 1)
    def _():
        for p in range(3):
            down_copy(chip, p).wait_recv()
            add_piece(down_piece, chip, p)

    keep_0 = pltpu.make_async_copy(half_0.at[chip], recv_0, own_s.at[3])
    keep_0.start()
    for t in range(CHIPS):
        @pl.when(t > chip)
        def _():
            for p in range(3):
                up_copy(t, p).wait_send()

        @pl.when(t < chip)
        def _():
            for p in range(3):
                down_copy(t, p).wait_send()

    done.wait()
    keep_0.wait()


def finish_kernel(dims, *refs):
    lat, in_width, hid, heads, bins, tasks, emb = dims
    at_mid = in_width + VECS
    at_out = at_mid + hid
    recv_q, recv_0, small_in, lat_in, grad_in = refs[:5]
    lat_out, grad_out, w_in, w_mid, w_dyn, w_q, b_dyn, g_dyn, s_dyn, b_q, table, rms = refs[5:17]
    vecs = refs[17:23]
    part_q, part_0, small, sum_in, sum_mid, lat_held, grad_held, in_sem, out_sem = refs[23:]
    loads = [pltpu.make_async_copy(recv_0, part_0, in_sem.at[0])]
    loads += [pltpu.make_async_copy(recv_q.at[h], part_q.at[h], in_sem.at[1 + h]) for h in range(heads)]
    load_small = pltpu.make_async_copy(small_in, small, in_sem.at[1 + heads])
    through = [
        pltpu.make_async_copy(lat_in, lat_held, in_sem.at[2 + heads]),
        pltpu.make_async_copy(grad_in, grad_held, in_sem.at[3 + heads]),
    ]
    copies = [
        pltpu.make_async_copy(lat_held, lat_out, out_sem.at[0]),
        pltpu.make_async_copy(grad_held, grad_out, out_sem.at[1]),
    ]
    order = list(range(1, heads + 1)) + [0]
    for copy in [loads[h] for h in order] + through + [load_small]:
        copy.start()

    def total(h, lo, hi):
        if h == 0:
            return part_0[lo:hi, :].astype(F32)
        return part_q[h - 1, 0, lo:hi, :].astype(F32) + part_q[h - 1, 1, lo:hi, :].astype(F32)

    for h in order:
        loads[h].wait()
        sum_mid[h] = total(h, at_mid, at_out)
        sum_in[h] = total(h, 0, in_width)
        copies.append(pltpu.make_async_copy(sum_in.at[h], w_in.at[h], out_sem.at[2 + 2 * h]))
        copies.append(pltpu.make_async_copy(sum_mid.at[h], w_mid.at[h], out_sem.at[3 + 2 * h]))
        for copy in copies[-2:]:
            copy.start()
        lines = total(h, in_width, at_mid)
        for t in range(6):
            vecs[t][h] = lines[t : t + 1, :]
        if h:
            w_q[h - 1] = total(h, at_out, at_out + padded(bins))[0:bins, :].reshape(bins, 1, LANES)
    for arriving, leaving in zip(through, copies):
        arriving.wait()
        leaving.start()
    for t in range(lat // LANES):
        w_dyn[:, t * LANES : (t + 1) * LANES] = total(0, at_out + t * LANES, at_out + (t + 1) * LANES)
    load_small.wait()
    table[...] = small[0:tasks, 0:emb]
    for t, out in enumerate((b_dyn, g_dyn, s_dyn)):
        for part in range(lat // LANES):
            row = tasks + t * (lat // LANES) + part
            out[0:1, part * LANES : (part + 1) * LANES] = small[row : row + 1, :]
    at_q = tasks + 3 * (lat // LANES)
    for h in range(heads):
        b_q[h] = small[at_q + h : at_q + h + 1, 0:bins]
    stat = small[at_q + heads : at_q + heads + 1, :]
    count = stat[:, 0:1]
    squares = jnp.concatenate([stat[:, 1:2] / count, stat[:, 2:3] / (count * lat)], 1)
    rms[...] = jnp.sqrt(squares)
    for copy in copies:
        copy.wait()


def on_device(
    latent_in, actions, task_ids, valid, action_mask, bins, fraction, latent_cot,
    w_in, b_in, g_in, beta_in, w_mid, b_mid, g_mid, beta_mid,
    w_dyn_out, b_dyn_out, g_dyn_out, beta_dyn_out, w_q_out, b_q_out, table,
):
    steps = lax.axis_size("section")
    spread = lax.axis_size("dp")
    groups = spread // PEERS
    rows, lat = latent_in.shape
    act_width = actions.shape[2]
    in_width, hid = w_in.shape[2:]
    heads = w_q_out.shape[1]
    bin_count = w_q_out.shape[-1]
    tasks, emb = table.shape
    block = in_width + VECS + hid + padded(bin_count)
    block0 = in_width + VECS + hid + lat
    chunks = rows // CHUNK
    small_rows = padded(tasks + 3 * (lat // LANES) + heads + 1)
    dims = (rows, lat, act_width, in_width, hid, heads, bin_count, tasks, emb, steps)
    anywhere = pl.BlockSpec(memory_space=pl.ANY)
    vmem = pl.BlockSpec(memory_space=pltpu.VMEM)
    hbm = pl.BlockSpec(memory_space=pltpu.HBM)
    dma = pltpu.SemaphoreType.DMA
    both = 2 * rows
    wide = pltpu.VMEM((rows, hid), B16)
    thin = pltpu.VMEM((rows, LANES), F32)
    low = pltpu.VMEM((rows, lat), B16)
    part_low = pltpu.VMEM((QROWS, hid), B16)
    q_wide = pltpu.VMEM((both, hid), B16)
    lat_out, grad_out, recv_q, recv_0, small = pl.pallas_call(
        functools.partial(step_kernel, dims),
        out_shape=[
            jax.ShapeDtypeStruct((rows, lat), B16),
            jax.ShapeDtypeStruct((rows, lat), F32),
            jax.ShapeDtypeStruct((heads, 2, block, LANES), B16),
            jax.ShapeDtypeStruct((block0, LANES), B16),
            jax.ShapeDtypeStruct((small_rows, LANES), F32),
        ],
        in_specs=[anywhere] + [vmem] * 7 + [anywhere] * 5 + [vmem] * 10,
        out_specs=[anywhere] * 5,
        scratch_shapes=[
            pltpu.VMEM((both, 6 * LANES), B16),
            pltpu.VMEM((both, LANES), F32),
            pltpu.VMEM((2, in_width + VECS, hid), B16),
            pltpu.VMEM((2, hid, hid), B16),
            pltpu.VMEM((2, LANES, hid), B16),
            pltpu.VMEM((2, bin_count, hid), B16),
            pltpu.VMEM((in_width + VECS, hid), B16),
            pltpu.VMEM((hid, hid), B16),
            pltpu.VMEM((hid, lat), B16),
            pltpu.VMEM((6, 8, hid), F32),
            pltpu.VMEM((8, LANES), F32),
            pltpu.VMEM((2 * LANES, 2 * LANES), B16),
            pltpu.VMEM((2, 8, rows), F32),
            pltpu.VMEM((2, act_width, rows), B16),
            pltpu.VMEM((VECS, hid), F32),
            pltpu.VMEM((both, in_width), F32),
            q_wide, q_wide, q_wide, q_wide,
            pltpu.VMEM((both, LANES), B16),
            part_low, part_low, part_low, part_low,
            pltpu.VMEM((QROWS, LANES), F32),
            pltpu.VMEM((QROWS, hid), F32),
            wide, wide, wide, wide, wide, wide, wide, wide, thin,
            low,
            pltpu.VMEM((rows, lat), F32),
            low, low, low, low, low,
            pltpu.VMEM((2, CHIPS, block0, LANES), B16),
            pltpu.VMEM((3, CHIPS, block, LANES), B16),
            pltpu.VMEM((CHIPS, block0, LANES), B16),
            pltpu.VMEM((2, 32, hid), F32),
            pltpu.VMEM((3, 8, LANES), F32),
            pltpu.VMEM((24, lat), F32),
            pltpu.VMEM((16, lat), F32),
            pltpu.VMEM((small_rows, LANES), F32),
            pltpu.VMEM((small_rows, LANES), F32),
            pltpu.VMEM((CHIPS, small_rows // 2, LANES), F32),
            pltpu.VMEM((small_rows // 2, LANES), F32),
            pltpu.VMEM((steps, small_rows // 2, LANES), F32),
            pltpu.VMEM((small_rows, LANES), F32),
            dma((10,)), dma((chunks,)), dma((2 * chunks + 1,)),
            dma((chunks,)), dma((chunks,)), dma((chunks,)), dma((chunks,)),
            dma((2,)), dma((2,)), dma((chunks,)), dma((chunks,)), dma((chunks,)), dma((chunks,)),
            dma((4, CHIPS)), dma((4, CHIPS)), dma((4,)), dma((3, CHIPS)), dma((heads, 2)),
            dma((2,)), dma((2,)), dma((CHIPS,)), dma((CHIPS,)), dma((steps,)), dma((steps,)),
            dma((CHIPS, 3)), dma((CHIPS, 3)), dma((CHIPS, 3)), dma((CHIPS, 3)),
            pltpu.SemaphoreType.REGULAR, pltpu.SemaphoreType.REGULAR,
        ],
        compiler_params=pltpu.CompilerParams(
            collective_id=0, has_side_effects=True, vmem_limit_bytes=16350 * 2**12
        ),
        name="step",
    )(
        latent_in, actions[0].T, task_ids[None], valid[None], bins, fraction,
        action_mask.T, table, latent_cot[0],
        w_in[0], w_mid[0], w_dyn_out[0], w_q_out[0].transpose(0, 2, 1),
        b_in[0], g_in[0], beta_in[0], b_mid[0], g_mid[0], beta_mid[0],
        b_dyn_out, g_dyn_out, beta_dyn_out, b_q_out[0],
    )
    across = [[q * PEERS + r for q in range(groups)] for r in range(PEERS)]
    if groups > 1:
        small = lax.psum(small, "dp", axis_index_groups=across)

    def shape(*dims):
        return jax.ShapeDtypeStruct(dims, F32)

    lat_out, grad_out, part_in, part_mid, part_dyn, part_q, b_dyn, g_dyn, s_dyn, q_bias, grad_table, rms, *vecs = (
        pl.pallas_call(
            functools.partial(finish_kernel, (lat, in_width, hid, heads, bin_count, tasks, emb)),
            out_shape=[
                jax.ShapeDtypeStruct((rows, lat), B16),
                shape(rows, lat),
                shape(heads + 1, in_width, LANES),
                shape(heads + 1, hid, LANES),
                shape(LANES, lat),
                shape(heads, bin_count, 1, LANES),
                shape(1, lat), shape(1, lat), shape(1, lat),
                shape(heads, 1, bin_count),
                shape(tasks, emb),
                shape(1, 2),
            ] + [shape(heads + 1, 1, LANES)] * 6,
            in_specs=[hbm] * 5,
            out_specs=[hbm] * 4 + [vmem] * 14,
            scratch_shapes=[
                pltpu.VMEM((heads, 2, block, LANES), B16),
                pltpu.VMEM((block0, LANES), B16),
                pltpu.VMEM((small_rows, LANES), F32),
                pltpu.VMEM((heads + 1, in_width, LANES), F32),
                pltpu.VMEM((heads + 1, hid, LANES), F32),
                pltpu.VMEM((rows, lat), B16),
                pltpu.VMEM((rows, lat), F32),
                dma((heads + 4,)),
                dma((2 * heads + 4,)),
            ],
            compiler_params=pltpu.CompilerParams(vmem_limit_bytes=60 * 2**20),
            name="finish",
        )(recv_q, recv_0, small, lat_out, grad_out)
    )

    def owned(piece, dim):
        if groups == 1:
            return piece
        piece = lax.psum_scatter(piece, "dp", scatter_dimension=dim, axis_index_groups=across, tiled=True)
        moves = [(q * PEERS + r, r * groups + q) for q in range(groups) for r in range(PEERS)]
        return lax.ppermute(piece, "dp", moves)

    part_in, part_mid, part_q = owned(part_in, 2), owned(part_mid, 2), owned(part_q, 3)
    part_dyn = owned(part_dyn, 0)
    vecs = [owned(v, 2).transpose(1, 0, 2) for v in vecs]
    return (
        lat_out[None],
        grad_out[None],
        part_in[None],
        *vecs[:3],
        part_mid[None],
        *vecs[3:],
        part_dyn[None],
        b_dyn,
        g_dyn,
        s_dyn,
        part_q.transpose(2, 0, 3, 1),
        q_bias.transpose(1, 0, 2),
        grad_table,
        rms,
    )


def solution(mesh):
    placed = (
        P("dp", None),
        P("section", "dp", None),
        P("dp"),
        P("dp"),
        P(),
        P("section", "dp"),
        P("section", "dp"),
        P("section", "dp", None),
        P("section", None, None, None),
        P("section", None, None),
        P("section", None, None),
        P("section", None, None),
        P("section", None, None, None),
        P("section", None, None),
        P("section", None, None),
        P("section", None, None),
        P("section", None, None),
        P("section", None),
        P("section", None),
        P("section", None),
        P("section", None, None, None),
        P("section", None, None),
        P(),
    )
    return jax.shard_map(
        on_device,
        mesh=mesh,
        in_specs=placed,
        out_specs=(
            P("section", "dp", None),
            P("section", "dp", None),
            P("section", None, None, "dp"),
            P("section", None, "dp"),
            P("section", None, "dp"),
            P("section", None, "dp"),
            P("section", None, None, "dp"),
            P("section", None, "dp"),
            P("section", None, "dp"),
            P("section", None, "dp"),
            P("section", "dp", None),
            P("section", None),
            P("section", None),
            P("section", None),
            P("section", None, "dp", None),
            P("section", None, None),
            P(),
            P("section", None),
        ),
        check_vma=False,
    )
```

```python
import functools

import jax
import jax.numpy as jnp
from jax import lax
from jax.experimental import pallas as pl
from jax.experimental.pallas import tpu as pltpu
from jax.sharding import PartitionSpec as P

GROUP = 8
EPS = 1e-05
F32 = jnp.float32
B16 = jnp.bfloat16
MESH = pl.DeviceIdType.MESH

LANES = 128
CHIPS = 4
PEERS = 2 * CHIPS
CHUNK = 128
QROWS = 256
SUB = 256
VECS = 16

NN = (((1,), (0,)), ((), ()))
NT = (((1,), (1,)), ((), ()))
TN = (((0,), (0,)), ((), ()))


def dot(a, b, dims=NN):
    return lax.dot_general(a, b, dims, preferred_element_type=F32)


def split_dot(a, b, dims=NN):
    high = a.astype(B16)
    low = (a - high.astype(F32)).astype(B16)
    return dot(high, b, dims) + dot(low, b, dims)


def split_dot_right(a, b, dims):
    high = b.astype(B16)
    low = (b - high.astype(F32)).astype(B16)
    return dot(a, high, dims) + dot(a, low, dims)


def norm_mish(x, gain, shift):
    center = x - jnp.mean(x, -1, keepdims=True)
    spread = jnp.mean(center * center, -1, keepdims=True)
    scale = lax.rsqrt(spread + EPS)
    n = center * scale
    u = n * gain + shift
    w = jnp.exp(jnp.minimum(u, 30.0))
    top = w * (w + 2.0)
    over = pltpu.reciprocal(top + 2.0, approx=True)
    act = u * (top * over)
    slope = (top + 4.0 * (u * (top - w)) * over) * (over * gain)
    return act, n, slope, scale


def padded(count):
    return (count + 15) // 16 * 16


def tiles(size, step=256):
    return [(lo, min(lo + step, size)) for lo in range(0, size, step)]


def eight_rows(x):
    return x.reshape(x.shape[0] // 8, 8, x.shape[1]).sum(0)


def each_sub(count, body):
    sub = min(SUB, count)
    for j in range(0, count, sub):
        body(j, sub)


def layer_forward(pre, count, bias, gain, shift, act_ref, act_at, n_ref, slope_ref, scale_ref, lane, at):
    def body(j, sub):
        x = pre[pl.ds(j, sub), :]
        if bias is not None:
            x = x + bias
        act, n, slope, scale = norm_mish(x, gain, shift)
        act_ref[pl.ds(act_at + j, sub), :] = act.astype(B16)
        here = pl.ds(at + j, sub)
        n_ref[here, :] = n.astype(n_ref.dtype)
        slope_ref[here, :] = slope.astype(slope_ref.dtype)
        scale_ref[here, lane : lane + 1] = scale

    each_sub(count, body)


def layer_backward(pre, count, n_ref, slope_ref, scale_ref, lane, at, out_ref, out_at, sums, first):
    def body(j, sub):
        here = pl.ds(at + j, sub)
        n = n_ref[here, :].astype(F32)
        dn = pre[pl.ds(j, sub), :] * slope_ref[here, :].astype(F32)
        by_n = dn * n
        mean_dn = jnp.mean(dn, -1, keepdims=True)
        mean_by_n = jnp.mean(by_n, -1, keepdims=True)
        out = (dn - mean_dn - n * mean_by_n) * scale_ref[here, lane : lane + 1]
        out_ref[pl.ds(out_at + j, sub), :] = out.astype(B16)
        sums[first : first + 8, :] += eight_rows(by_n)
        sums[first + 8 : first + 16, :] += eight_rows(dn)

    each_sub(count, body)


def step_kernel(dims, *refs):
    rows, lat, act_width, in_width, hid, heads, bins, tasks, emb, steps = dims
    side_width = in_width - lat
    at_mid = in_width + VECS
    at_out = at_mid + hid
    block = at_out + padded(bins)
    block0 = at_out + lat
    both = 2 * rows
    ones_at = in_width // LANES * LANES
    pieces = ((0, at_mid), (at_mid, at_out), (at_out, block0))
    (
        lat_in, acts, task, valid, bin_at, part_of, amask, table, cot_in, w_in, w_mid, w_dyn, w_q,
        b_in, g_in, s_in, b_mid, g_mid, s_mid, b_dyn, g_dyn, s_dyn, b_q,
        lat_out, grad_out, recv_q, recv_0, small_out,
        x, m, wi, wm, wq, wq_raw, wi0, wm0, wd, vec, bq, diag,
        lines, acting, vec_lines, ig, act1, act2, spg, fpg, qg, n1, d1, n2, d2, q_scales, pre,
        act1_0, act2_0, spg_0, fpg_0, n1_0, d1_0, n2_0, d2_0, scales,
        dyn_n, new_lat, lat_low, cot, arrived, pair_grad, pair_send,
        gb, half_q, half_0, sums, q_sums, dyn_sums, stat, small, small_mate, small_chips, small_half, small_steps, small_done,
        w_sem, in_sem, out_sem, lat_s, lat_r, px_s, px_r, side_s, side_r, pg_s, pg_r, gr_s, gr_r,
        half_s, half_r, own_s, rb_s, rb_r, sm_s, sm_r, ch_s, ch_r, tb_s, tb_r, up_s, up_r, dn_s, dn_r, up_ok, dn_ok,
    ) = refs
    section = lax.axis_index("section")
    d = lax.axis_index("dp")
    place = lax.rem(d, PEERS)
    base = d - place
    chip = place // 2
    core = lax.rem(place, 2)
    edge = (chip == 0) | (chip == CHIPS - 1)
    lower = chip < CHIPS // 2
    side_of = chip // 2
    last = steps - 1
    mate = base + chip * 2 + (1 - core)
    pair = base + (chip + 1 - 2 * lax.rem(chip, 2)) * 2 + core
    following = jnp.minimum(section + 1, last)
    before = jnp.maximum(section - 1, 0)
    chunks = rows // CHUNK
    jobs = jnp.where(edge, 2, 3)
    held = (section >= steps - 2) & edge
    farthest = CHIPS - 1 - chip
    first_head = jnp.where(edge, 1, 3)

    def remote(src, dst, send, recv, to):
        return pltpu.make_async_remote_copy(
            src_ref=src, dst_ref=dst, send_sem=send, recv_sem=recv, device_id=to, device_id_type=MESH
        )

    def chunk_at(i):
        return pl.multiple_of(i * CHUNK, CHUNK)

    loads = [
        pltpu.make_async_copy(w_in.at[0], wi0.at[0:in_width], w_sem.at[0]),
        pltpu.make_async_copy(w_mid.at[0], wm0, w_sem.at[1]),
        pltpu.make_async_copy(w_dyn, wd, w_sem.at[2]),
    ]

    def job_loads(job):
        slot = lax.rem(job, 2)
        h = first_head + job
        return [
            pltpu.make_async_copy(w_in.at[h], wi.at[slot, 0:in_width], w_sem.at[3 + 3 * slot]),
            pltpu.make_async_copy(w_mid.at[h], wm.at[slot], w_sem.at[4 + 3 * slot]),
            pltpu.make_async_copy(w_q.at[h - 1], wq_raw.at[slot], w_sem.at[5 + 3 * slot]),
        ]

    load_cot = pltpu.make_async_copy(cot_in, cot, w_sem.at[9])

    def load_lat(i):
        here = pl.ds(chunk_at(i), CHUNK)
        return pltpu.make_async_copy(lat_in.at[here], x.at[here, 0:lat], in_sem.at[i])

    barrier = pltpu.get_barrier_semaphore()
    for other in range(1, PEERS):
        to = base + lax.rem(place + other, PEERS)
        pl.semaphore_signal(barrier, inc=1, device_id=(section, to), device_id_type=MESH)
    for other in range(1, steps):
        to = lax.rem(section + other, steps)
        pl.semaphore_signal(barrier, inc=1, device_id=(to, d), device_id_type=MESH)

    loads[0].start()

    @pl.when(section == 0)
    def _():
        for i in range(chunks):
            load_lat(i).start()

    for copy in loads[1:] + job_loads(jnp.int32(0)) + job_loads(jnp.int32(1)):
        copy.start()
    load_cot.start()

    head_lines = [task[...].astype(F32), valid[...].astype(F32), bin_at[...].astype(F32), part_of[...]]
    lines[0] = jnp.concatenate(head_lines + [jnp.zeros((4, rows), F32)], 0)
    acting[0] = acts[...]

    def one_hot(lo, count):
        task_lane = lax.broadcasted_iota(jnp.int32, (count, tasks), 1).astype(F32)
        return (m[lo : lo + count, 0:1] == task_lane).astype(F32).astype(B16)

    def prepare(which):
        lo = which * rows
        m[lo : lo + rows, 0:8] = lines[which].T
        hot = one_hot(lo, rows)
        mask = dot(amask[...].astype(F32).astype(B16), hot, NT)
        used = (acting[which].astype(F32) * mask).T
        x[lo : lo + rows, lat:in_width] = jnp.concatenate(
            [used.astype(B16), dot(hot, table[...]).astype(B16)], 1
        )

    lane = lax.broadcasted_iota(jnp.int32, (both, LANES), 1)
    x[:, ones_at : ones_at + LANES] = (lane == in_width - ones_at).astype(F32).astype(B16)
    prepare(0)
    for t, source in enumerate((b_in, g_in, s_in, b_mid, g_mid, s_mid)):
        vec[t, 0 : heads + 1, :] = source[...].astype(F32)
    shift = GROUP.bit_length() - 1
    diag[...] = (
        lax.shift_right_logical(lax.broadcasted_iota(jnp.int32, diag.shape, 0), shift)
        == lax.shift_right_logical(lax.broadcasted_iota(jnp.int32, diag.shape, 1), shift)
    ).astype(F32).astype(B16)

    def group_sums(values):
        width = diag.shape[0]
        return jnp.concatenate(
            [split_dot(values[:, lo : lo + width], diag[...]) for lo in range(0, lat, width)], 1
        )

    def bias_rows(h):
        line = lax.broadcasted_iota(jnp.int32, (VECS, hid), 0)
        return jnp.where(line == 0, vec[0, pl.ds(h, 1), :], 0.0).astype(B16)

    wi0[in_width:at_mid, :] = bias_rows(0)
    stat[...] = jnp.zeros(stat.shape, F32)

    def clear():
        bq[...] = jnp.full(bq.shape, -1e30, F32)
        bq[0:heads, 0:bins] = b_q[...].astype(F32)
        wq[...] = jnp.zeros(wq.shape, B16)
        sums[...] = jnp.zeros(sums.shape, F32)
        ig[...] = jnp.zeros(ig.shape, F32)
        q_sums[...] = jnp.zeros(q_sums.shape, F32)
        dyn_sums[...] = jnp.zeros(dyn_sums.shape, F32)
        small[...] = jnp.zeros(small.shape, F32)

    pl.semaphore_wait(barrier, PEERS - 1 + steps - 1)

    side_copies = [
        remote(lines.at[0], lines.at[1], side_s.at[0], side_r.at[0], (section, pair)),
        remote(acting.at[0], acting.at[1], side_s.at[1], side_r.at[1], (section, pair)),
    ]
    for copy in side_copies:
        copy.start()

    def settle():
        clear()
        for copy in side_copies:
            copy.wait_recv()
        prepare(1)

    @pl.when(section == last)
    def _():
        arrived[...] = jnp.zeros(arrived.shape, B16)

    @pl.when(section > 0)
    def _():
        settle()

    for copy in loads:
        copy.wait()

    def vec_of(t, h):
        return vec[t, pl.ds(h, 1), :]

    def lat_copy(i):
        here = pl.ds(chunk_at(i), CHUNK)
        return remote(
            lat_low.at[here], x.at[here, 0:lat], lat_s.at[i], lat_r.at[i], (following, d)
        )

    def pair_copy(i):
        here = chunk_at(i)
        return remote(
            x.at[pl.ds(here, CHUNK), 0:lat], x.at[pl.ds(rows + here, CHUNK), 0:lat],
            px_s.at[i], px_r.at[i], (section, pair),
        )

    def lat_store(i):
        here = pl.ds(chunk_at(i), CHUNK)
        return pltpu.make_async_copy(lat_low.at[here], lat_out.at[here], out_sem.at[i])

    def forward_chunk(i, carry):
        at = chunk_at(i)
        here = pl.ds(at, CHUNK)

        @pl.when(section > 0)
        def _():
            lat_copy(i).wait_recv()

        @pl.when(section == 0)
        def _():
            load_lat(i).wait()

        pair_copy(i).start()
        pre[0:CHUNK, :] = dot(x[here, 0:at_mid], wi0[...])
        layer_forward(
            pre, CHUNK, None, vec[1, 0:1, :], vec[2, 0:1, :], act1_0, at, n1_0, d1_0, scales, 0, at
        )
        pre[0:CHUNK, :] = dot(act1_0[here, :], wm0[...])
        layer_forward(
            pre, CHUNK, vec[3, 0:1, :], vec[4, 0:1, :], vec[5, 0:1, :], act2_0, at, n2_0, d2_0, scales, 1, at
        )
        out = dot(act2_0[here, :], wd[...]) + b_dyn[...].astype(F32)
        center = out - jnp.mean(out, -1, keepdims=True)
        scale = lax.rsqrt(jnp.mean(center * center, -1, keepdims=True) + EPS)
        normal = center * scale
        dyn_n[here, :] = normal.astype(B16)
        scales[here, 2:3] = scale
        power = jnp.exp(normal * g_dyn[...].astype(F32) + s_dyn[...].astype(F32))
        fresh = power * pltpu.reciprocal(group_sums(power), approx=True)
        new_lat[here, :] = fresh
        low = fresh.astype(B16)
        lat_low[here, :] = low

        @pl.when(section < last)
        def _():
            lat_copy(i).start()

        lat_store(i).start()
        wide = low.astype(F32)
        stat[0:8, :] += eight_rows(m[here, 1:2] * (wide * wide))
        return carry

    lax.fori_loop(0, chunks, forward_chunk, 0)

    @pl.when(section == 0)
    def _():
        settle()

    def pg_copy(i):
        here = pl.ds(chunk_at(i), CHUNK)
        return remote(
            pair_send.at[here], pair_grad.at[here], pg_s.at[i], pg_r.at[i], (section, pair)
        )

    def q_chunk(job, at):
        here = pl.ds(at, QROWS)
        h = first_head + job
        slot = lax.rem(job, 2)
        pre[...] = dot(x[here, 0:at_mid], wi[slot])
        layer_forward(
            pre, QROWS, None, vec_of(1, h), vec_of(2, h), act1, at, n1, d1, q_scales, 0, 0
        )
        pre[...] = dot(act1[here, :], wm[slot])
        layer_forward(
            pre, QROWS, vec_of(3, h), vec_of(4, h), vec_of(5, h), act2, at, n2, d2, q_scales, 1, 0
        )
        logits = dot(act2[here, :], wq[slot], NT) + bq[pl.ds(h - 1, 1), :]
        power = jnp.exp(logits - jnp.max(logits, -1, keepdims=True))
        chance = power / jnp.sum(power, -1, keepdims=True)
        lane = lax.broadcasted_iota(jnp.int32, (QROWS, LANES), 1).astype(F32)
        low_bin = m[here, 2:3]
        part = m[here, 3:4]
        target = jnp.where(lane == low_bin, 1.0 - part, 0.0) + jnp.where(lane == low_bin + 1.0, part, 0.0)
        grad = (m[here, 1:2] * (chance - target)).astype(B16)
        qg[here, :] = grad
        q_sums[job] += eight_rows(grad.astype(F32))
        pre[...] = dot(grad, wq[slot])
        layer_backward(pre, QROWS, n2, d2, q_scales, 1, 0, spg, at, sums.at[0], 16)
        pre[...] = dot(spg[here, :], wm[slot], NT)
        layer_backward(pre, QROWS, n1, d1, q_scales, 0, 0, fpg, at, sums.at[0], 0)
        for lo, hi in tiles(in_width):
            ig[here, lo:hi] += dot(fpg[here, :], wi[slot, lo:hi, :], NT)

    q_chunks = both // QROWS
    own_chunks = rows // QROWS

    def q_job(job):
        for copy in job_loads(job):
            copy.wait()
        slot = lax.rem(job, 2)
        wq[slot, 0:bins, :] = wq_raw[slot]
        wi[slot, in_width:at_mid, :] = bias_rows(first_head + job)
        sums[0] = jnp.zeros(sums.shape[1:], F32)

        def body(i, carry):
            which = lax.rem(i + jnp.where(job == 0, 0, own_chunks), q_chunks)
            at = pl.multiple_of(which * QROWS, QROWS)

            @pl.when((job == 0) & (which == own_chunks))
            def _():
                def pair_here(j, carry):
                    pair_copy(j).wait_recv()
                    return carry

                lax.fori_loop(0, chunks, pair_here, 0)

            q_chunk(job, at)

            @pl.when((job == jobs - 1) & (which >= own_chunks))
            def _():
                for k in range(QROWS // CHUNK):
                    j = (which - own_chunks) * (QROWS // CHUNK) + k
                    to = chunk_at(j)
                    pair_send[pl.ds(to, CHUNK), :] = ig[pl.ds(rows + to, CHUNK), 0:lat].astype(B16)
                    pg_copy(j).start()

            return carry

        lax.fori_loop(0, q_chunks, body, 0)

        @pl.when(job + 2 < jobs)
        def _():
            for copy in job_loads(job + 2):
                copy.start()

    def half_copy(job, z, q):
        if q:
            src, dst = gb.at[1 - core, z, 0:block], half_q.at[job, z]
        else:
            src, dst = gb.at[1 - core, z], half_0.at[z]
        return remote(src, dst, half_s.at[job, z], half_r.at[job, z], (section, mate))

    def owner_copy(job, z):
        head = first_head + job - 1
        return remote(
            half_q.at[job, z], recv_q.at[head, side_of], rb_s.at[job, z], rb_r.at[head, side_of],
            (section, base + 2 * z + core),
        )

    def keep_copy(job):
        return pltpu.make_async_copy(
            half_q.at[job, chip], recv_q.at[first_head + job - 1, side_of], own_s.at[job]
        )

    def add_rows(dst, src, size):
        step = size // 4 // 16 * 16
        for part in range(4):
            span = slice(part * step, size if part == 3 else (part + 1) * step)
            dst[span, :] = (dst[span, :].astype(F32) + src[span, :].astype(F32)).astype(B16)

    def at_chip(z):
        return (section, base + 2 * z + core)

    def stripe(z):
        return pl.ds(pl.multiple_of(z * LANES, LANES), LANES)

    def up_piece(z, p):
        size = pieces[p][1] - pieces[p][0]
        return (act1.at[0:size, stripe(z)], act1.at[0:size, stripe(CHIPS + z)], act2.at[0:size, stripe(z)])[p]

    def down_piece(z, p):
        size = pieces[p][1] - pieces[p][0]
        return (spg.at[0:size, stripe(z)], spg.at[0:size, stripe(CHIPS + z)], act2.at[0:size, stripe(CHIPS + z)])[p]

    def up_copy(z, p):
        return remote(
            half_0.at[z, pieces[p][0] : pieces[p][1]], up_piece(z, p), up_s.at[z, p], up_r.at[z, p],
            at_chip(jnp.minimum(chip + 1, CHIPS - 1)),
        )

    def down_copy(z, p):
        return remote(
            half_0.at[z, pieces[p][0] : pieces[p][1]], down_piece(z, p), dn_s.at[z, p], dn_r.at[z, p],
            at_chip(jnp.maximum(chip - 1, 0)),
        )

    def add_piece(piece, z, p):
        lo, hi = pieces[p]
        half_0[z, lo:hi, :] = (half_0[z, lo:hi, :].astype(F32) + piece(z, p)[...].astype(F32)).astype(B16)

    def weight_grads(job, q):
        if q:
            count, a1, a2, sp, fp, own_sums = both, act1, act2, spg, fpg, 0
        else:
            count, a1, a2, sp, fp, own_sums = rows, act1_0, act2_0, spg_0, fpg_0, 1
        size = block if q else block0
        h = first_head + job if q else 0
        line_at = lax.broadcasted_iota(jnp.int32, (VECS, hid), 0)
        vectors = jnp.zeros((VECS, hid), F32)
        for t, (first, gain) in enumerate(((0, 1), (8, 1), (None, None), (16, 4), (24, 4))):
            if gain is not None:
                line = jnp.sum(sums[own_sums, first : first + 8, :], 0, keepdims=True) / vec_of(gain, h)
                vectors = jnp.where(line_at == t + 1, line, vectors)
        vec_lines[...] = vectors
        row_at = lax.broadcasted_iota(jnp.int32, (VECS, 2 * LANES), 0)

        def order(i):
            far_first = jnp.where(lower, CHIPS - 1 - i, i)
            pair_first = lax.rem(jnp.where(lower, CHIPS - i, i + CHIPS - 1), CHIPS)
            return jnp.where(edge, far_first, pair_first)

        def make(z):
            cols = pl.ds(pl.multiple_of(z * 2 * LANES, 2 * LANES), 2 * LANES)
            for left, right, first, size_of in ((x, fp, 0, at_mid), (a1, sp, at_mid, hid)):
                for lo, hi in tiles(size_of):
                    grad = dot(left[0:count, lo:hi], right[0:count, cols], TN)
                    if left is x and hi == at_mid:
                        plain = grad[0 : in_width - lo]
                        bias_mid = dot(x[0:count, ones_at : ones_at + LANES], sp[0:count, cols], TN)
                        bias_mid = bias_mid[in_width - ones_at : in_width - ones_at + 1]
                        lines_here = grad[in_width - lo :] + vec_lines[:, cols]
                        grad = jnp.concatenate([plain, jnp.where(row_at == 3, bias_mid, lines_here)], 0)
                    for p in range(2):
                        gb[p, z, first + lo : first + hi, :] = grad[:, p * LANES : (p + 1) * LANES].astype(B16)
            if q:
                g_out = dot(qg[0:count, :], a2[0:count, cols], TN)
                for p in range(2):
                    gb[p, z, at_out:block, :] = g_out[0 : block - at_out, p * LANES : (p + 1) * LANES].astype(B16)
            else:
                g_out = dot(a2[0:count, cols], arrived[0:count, :], TN)
                for p in range(2):
                    for t in range(lat // LANES):
                        gb[p, z, at_out + t * LANES : at_out + (t + 1) * LANES, :] = g_out[
                            p * LANES : (p + 1) * LANES, t * LANES : (t + 1) * LANES
                        ].astype(B16)
            half_copy(job, z, q).start()

        def finish(z):
            half_copy(job, z, q).wait_recv()
            if q:
                add_rows(half_q.at[job, z], gb.at[core, z], size)

                @pl.when((z != chip) & ~((job == jobs - 1) & held & (z == farthest)))
                def _():
                    owner_copy(job, z).start()

                @pl.when(z == chip)
                def _():
                    keep_copy(job).start()
            else:
                add_rows(half_0.at[z], gb.at[core, z], size)

                @pl.when((chip == 0) & (z != chip))
                def _():
                    for p in range(3):
                        up_copy(z, p).start()

                @pl.when((chip == CHIPS - 1) & (z != chip))
                def _():
                    for p in range(3):
                        down_copy(z, p).start()

        def body(i, carry):
            @pl.when(i < CHIPS)
            def _():
                make(order(i))

            if not q:
                @pl.when(i == 1)
                def _():
                    small_over_chips()

            @pl.when(i > 0)
            def _():
                finish(order(i - 1))

            return carry

        lax.fori_loop(0, CHIPS + 1, body, 0)

        def sent(z, carry):
            half_copy(job, z, q).wait_send()
            return carry

        lax.fori_loop(0, CHIPS, sent, 0)

    def back_copy(i):
        here = pl.ds(chunk_at(i), CHUNK)
        return remote(lat_low.at[here], arrived.at[here], gr_s.at[i], gr_r.at[i], (before, d))

    def grad_store(i):
        here = pl.ds(chunk_at(i), CHUNK)
        return pltpu.make_async_copy(ig.at[here, 0:lat], grad_out.at[here], out_sem.at[chunks + i])

    def lat_sent(i, carry):
        lat_store(i).wait()

        @pl.when(section < last)
        def _():
            lat_copy(i).wait_send()

        return carry

    def backward_chunk(i, carry):
        at = chunk_at(i)
        here = pl.ds(at, CHUNK)

        @pl.when(section < last)
        def _():
            back_copy(i).wait_recv()

        out_grad = cot[here, :].astype(F32) + arrived[here, :].astype(F32)
        fresh = new_lat[here, :]
        normal = dyn_n[here, :].astype(F32)
        norm_grad = fresh * (out_grad - group_sums(out_grad * fresh))
        by_n = norm_grad * normal
        gain = g_dyn[...].astype(F32)
        dm = norm_grad * gain
        mean_dm = jnp.mean(dm, -1, keepdims=True)
        mean_by_n = jnp.mean(by_n * gain, -1, keepdims=True)
        low = ((dm - mean_dm - normal * mean_by_n) * scales[here, 2:3]).astype(B16)
        arrived[here, :] = low
        dyn_sums[0:8, :] += eight_rows(low.astype(F32))
        dyn_sums[8:16, :] += eight_rows(by_n)
        dyn_sums[16:24, :] += eight_rows(norm_grad)
        pre[0:CHUNK, :] = dot(low, wd[...], NT)
        layer_backward(pre, CHUNK, n2_0, d2_0, scales, 1, at, spg_0, at, sums.at[1], 16)
        pre[0:CHUNK, :] = dot(spg_0[here, :], wm0[...], NT)
        layer_backward(pre, CHUNK, n1_0, d1_0, scales, 0, at, fpg_0, at, sums.at[1], 0)
        back_in = dot(fpg_0[here, :], wi0[0:in_width, :], NT)
        pg_copy(i).wait_recv()

        @pl.when((i == chunks - 1) & held)
        def _():
            owner_copy(jobs - 1, farthest).start()

        total = back_in[:, 0:lat] + ig[here, 0:lat] + pair_grad[here, :].astype(F32)
        lat_low[here, :] = total.astype(B16)

        @pl.when(section > 0)
        def _():
            back_copy(i).start()

        ig[here, 0:lat] = total
        grad_store(i).start()
        stat[8:16, :] += eight_rows(m[here, 1:2] * (total * total))
        ig[here, lat:in_width] += back_in[:, lat:in_width]
        return carry

    half_rows = small.shape[0] // 2
    my_rows = pl.ds(pl.multiple_of(core * half_rows, half_rows), half_rows)

    def to_mate(src, dst, k):
        return remote(src, dst, sm_s.at[k], sm_r.at[k], (section, mate))

    def small_to_mate():
        return to_mate(small, small_mate, 0)

    def small_to_chip(other):
        to = lax.rem(chip + other, CHIPS)
        return remote(
            small.at[my_rows], small_chips.at[chip], ch_s.at[other], ch_r.at[chip], (section, base + 2 * to + core)
        )

    def small_from_chip(other):
        to = lax.rem(chip + other, CHIPS)
        return remote(
            small.at[my_rows], small_chips.at[to], ch_s.at[other], ch_r.at[to], (section, base + 2 * to + core)
        )

    def small_to_section(other):
        to = lax.rem(section + other, steps)
        return remote(small_half, small_steps.at[section], tb_s.at[other], tb_r.at[section], (to, d))

    def small_from_section(other):
        source = lax.rem(section + other, steps)
        return remote(small_half, small_steps.at[source], tb_s.at[other], tb_r.at[source], (source, d))

    def small_back():
        return to_mate(small_done.at[my_rows], small_done.at[my_rows], 1)

    def small_over_chips():
        small_to_mate().wait_recv()
        small_to_mate().wait_send()
        small[...] += small_mate[...]
        small_chips[chip] = small[my_rows, :]
        for other in range(1, CHIPS):
            small_to_chip(other).start()

    def small_over_sections():
        for other in range(1, CHIPS):
            small_from_chip(other).wait_recv()
        total = small_chips[0]
        for source in range(1, CHIPS):
            total = total + small_chips[source]
        small_half[...] = total
        small_steps[section] = total
        for other in range(1, steps):
            small_to_section(other).start()

    def small_last():
        for other in range(1, steps):
            small_from_section(other).wait_recv()
        whole = small_steps[0]
        for source in range(1, steps):
            whole = whole + small_steps[source]
        row = lax.broadcasted_iota(jnp.int32, whole.shape, 0) + core * half_rows
        small_done[my_rows, :] = jnp.where(row < tasks, whole, small_half[...])
        small_back().start()
        for other in range(1, CHIPS):
            small_to_chip(other).wait_send()
        for other in range(1, steps):
            small_to_section(other).wait_send()
        small_back().wait_recv()
        small_back().wait_send()

    def send_small():
        table_part = jnp.zeros((tasks, side_width), F32)
        for lo in (0, rows):
            table_part += split_dot_right(one_hot(lo, rows), ig[lo : lo + rows, lat:in_width], TN)
        small[0:tasks, 0:emb] = table_part[:, side_width - emb :]
        for t in range(3):
            line = jnp.sum(dyn_sums[8 * t : 8 * t + 8, :], 0, keepdims=True)
            for part in range(lat // LANES):
                row = tasks + t * (lat // LANES) + part
                small[row : row + 1, :] = line[:, part * LANES : (part + 1) * LANES]
        q_lines = [jnp.sum(q_sums[job], 0, keepdims=True) for job in range(3)]
        for h in range(heads):
            line = jnp.zeros((1, LANES), F32)
            for job in range(3):
                line += jnp.where(first_head + job == h + 1, q_lines[job], 0.0)
            row = tasks + 3 * (lat // LANES) + h
            small[row : row + 1, :] = line
        row = tasks + 3 * (lat // LANES) + heads
        lane = lax.broadcasted_iota(jnp.int32, (1, LANES), 1)
        count = jnp.sum(m[0:rows, 1:2], 0, keepdims=True)
        lat_square = jnp.sum(jnp.sum(stat[0:8, :], 0, keepdims=True), 1, keepdims=True)
        grad_square = jnp.sum(jnp.sum(stat[8:16, :], 0, keepdims=True), 1, keepdims=True)
        small[row : row + 1, :] = jnp.where(
            lane == 0, count, jnp.where(lane == 1, lat_square, jnp.where(lane == 2, grad_square, 0.0))
        )
        small_to_mate().start()

    waits = (section == last) & ~edge

    def turns(turn, carry):
        @pl.when(turn < jobs)
        def _():
            q_job(turn)

        @pl.when(turn == jobs)
        def _():
            load_cot.wait()
            lax.fori_loop(0, chunks, lat_sent, 0)
            lax.fori_loop(0, chunks, backward_chunk, 0)
            send_small()

        @pl.when((turn < jobs - 1) | ((turn == jobs - 1) & ~waits) | ((turn == jobs) & waits))
        def _():
            weight_grads(jnp.minimum(turn, jobs - 1), True)

            @pl.when((turn >= jobs - 1) & (chip > 0))
            def _():
                pl.semaphore_signal(up_ok, inc=1, device_id=at_chip(jnp.maximum(chip - 1, 0)), device_id_type=MESH)

            @pl.when((turn >= jobs - 1) & (chip < CHIPS - 1))
            def _():
                pl.semaphore_signal(
                    dn_ok, inc=1, device_id=at_chip(jnp.minimum(chip + 1, CHIPS - 1)), device_id_type=MESH
                )

        return carry

    lax.fori_loop(0, jobs + 1, turns, 0)

    @pl.when(chip < CHIPS - 1)
    def _():
        pl.semaphore_wait(up_ok, 1)

    @pl.when(chip > 0)
    def _():
        pl.semaphore_wait(dn_ok, 1)

    weight_grads(jnp.int32(3), False)

    def hops(turn, carry):
        @pl.when(((turn == 0) == lower) & ~edge)
        def _():
            for t in range(CHIPS - 1, 1, -1):
                @pl.when(t > chip)
                def _():
                    for p in range(3):
                        up_copy(t, p).wait_recv()
                        add_piece(up_piece, t, p)
                        up_copy(t, p).start()

        @pl.when(((turn == 0) != lower) & ~edge)
        def _():
            for t in range(CHIPS - 2):
                @pl.when(t < chip)
                def _():
                    for p in range(3):
                        down_copy(t, p).wait_recv()
                        add_piece(down_piece, t, p)
                        down_copy(t, p).start()

        @pl.when(turn == 0)
        def _():
            small_over_sections()

        return carry

    lax.fori_loop(0, 2, hops, 0)

    small_last()
    done = pltpu.make_async_copy(small_done, small_out, out_sem.at[2 * chunks])
    done.start()

    for copy in side_copies:
        copy.wait_send()

    def sends(i, carry):
        pair_copy(i).wait_send()
        pg_copy(i).wait_send()
        grad_store(i).wait()

        @pl.when(section > 0)
        def _():
            back_copy(i).wait_send()

        return carry

    lax.fori_loop(0, chunks, sends, 0)

    def job_done(job, carry):
        def body(other, carry):
            owner_copy(job, lax.rem(chip + other, CHIPS)).wait_send()
            return carry

        lax.fori_loop(1, CHIPS, body, 0)
        keep_copy(job).wait()
        return carry

    lax.fori_loop(0, jobs, job_done, 0)
    for head in range(heads):
        for half in range(2):
            source = (0, CHIPS - 1)[half] if head < 2 else (1, CHIPS - 2)[half]

            @pl.when(chip != source)
            def _():
                remote(
                    half_q.at[0, 0], recv_q.at[head, half], rb_s.at[0, 0], rb_r.at[head, half], at_chip(source)
                ).wait_recv()

    @pl.when(chip > 0)
    def _():
        for p in range(3):
            up_copy(chip, p).wait_recv()
            add_piece(up_piece, chip, p)

    @pl.when(chip < CHIPS - 1)
    def _():
        for p in range(3):
            down_copy(chip, p).wait_recv()
            add_piece(down_piece, chip, p)

    keep_0 = pltpu.make_async_copy(half_0.at[chip], recv_0, own_s.at[3])
    keep_0.start()
    for t in range(CHIPS):
        @pl.when(t > chip)
        def _():
            for p in range(3):
                up_copy(t, p).wait_send()

        @pl.when(t < chip)
        def _():
            for p in range(3):
                down_copy(t, p).wait_send()

    done.wait()
    keep_0.wait()


def finish_kernel(dims, *refs):
    lat, in_width, hid, heads, bins, tasks, emb = dims
    at_mid = in_width + VECS
    at_out = at_mid + hid
    recv_q, recv_0, small_in, lat_in, grad_in = refs[:5]
    lat_out, grad_out, w_in, w_mid, w_dyn, w_q, b_dyn, g_dyn, s_dyn, b_q, table, rms = refs[5:17]
    vecs = refs[17:23]
    part_q, part_0, small, sum_in, sum_mid, lat_held, grad_held, in_sem, out_sem = refs[23:]
    loads = [pltpu.make_async_copy(recv_0, part_0, in_sem.at[0])]
    loads += [pltpu.make_async_copy(recv_q.at[h], part_q.at[h], in_sem.at[1 + h]) for h in range(heads)]
    load_small = pltpu.make_async_copy(small_in, small, in_sem.at[1 + heads])
    through = [
        pltpu.make_async_copy(lat_in, lat_held, in_sem.at[2 + heads]),
        pltpu.make_async_copy(grad_in, grad_held, in_sem.at[3 + heads]),
    ]
    copies = [
        pltpu.make_async_copy(lat_held, lat_out, out_sem.at[0]),
        pltpu.make_async_copy(grad_held, grad_out, out_sem.at[1]),
    ]
    order = list(range(1, heads + 1)) + [0]
    for copy in [loads[h] for h in order] + through + [load_small]:
        copy.start()

    def total(h, lo, hi):
        if h == 0:
            return part_0[lo:hi, :].astype(F32)
        return part_q[h - 1, 0, lo:hi, :].astype(F32) + part_q[h - 1, 1, lo:hi, :].astype(F32)

    for h in order:
        loads[h].wait()
        sum_mid[h] = total(h, at_mid, at_out)
        sum_in[h] = total(h, 0, in_width)
        copies.append(pltpu.make_async_copy(sum_in.at[h], w_in.at[h], out_sem.at[2 + 2 * h]))
        copies.append(pltpu.make_async_copy(sum_mid.at[h], w_mid.at[h], out_sem.at[3 + 2 * h]))
        for copy in copies[-2:]:
            copy.start()
        lines = total(h, in_width, at_mid)
        for t in range(6):
            vecs[t][h] = lines[t : t + 1, :]
        if h:
            w_q[h - 1] = total(h, at_out, at_out + padded(bins))[0:bins, :].reshape(bins, 1, LANES)
    for arriving, leaving in zip(through, copies):
        arriving.wait()
        leaving.start()
    for t in range(lat // LANES):
        w_dyn[:, t * LANES : (t + 1) * LANES] = total(0, at_out + t * LANES, at_out + (t + 1) * LANES)
    load_small.wait()
    table[...] = small[0:tasks, 0:emb]
    for t, out in enumerate((b_dyn, g_dyn, s_dyn)):
        for part in range(lat // LANES):
            row = tasks + t * (lat // LANES) + part
            out[0:1, part * LANES : (part + 1) * LANES] = small[row : row + 1, :]
    at_q = tasks + 3 * (lat // LANES)
    for h in range(heads):
        b_q[h] = small[at_q + h : at_q + h + 1, 0:bins]
    stat = small[at_q + heads : at_q + heads + 1, :]
    count = stat[:, 0:1]
    squares = jnp.concatenate([stat[:, 1:2] / count, stat[:, 2:3] / (count * lat)], 1)
    rms[...] = jnp.sqrt(squares)
    for copy in copies:
        copy.wait()


def on_device(
    latent_in, actions, task_ids, valid, action_mask, bins, fraction, latent_cot,
    w_in, b_in, g_in, beta_in, w_mid, b_mid, g_mid, beta_mid,
    w_dyn_out, b_dyn_out, g_dyn_out, beta_dyn_out, w_q_out, b_q_out, table,
):
    steps = lax.axis_size("section")
    spread = lax.axis_size("dp")
    groups = spread // PEERS
    rows, lat = latent_in.shape
    act_width = actions.shape[2]
    in_width, hid = w_in.shape[2:]
    heads = w_q_out.shape[1]
    bin_count = w_q_out.shape[-1]
    tasks, emb = table.shape
    block = in_width + VECS + hid + padded(bin_count)
    block0 = in_width + VECS + hid + lat
    chunks = rows // CHUNK
    small_rows = padded(tasks + 3 * (lat // LANES) + heads + 1)
    dims = (rows, lat, act_width, in_width, hid, heads, bin_count, tasks, emb, steps)
    anywhere = pl.BlockSpec(memory_space=pl.ANY)
    vmem = pl.BlockSpec(memory_space=pltpu.VMEM)
    hbm = pl.BlockSpec(memory_space=pltpu.HBM)
    dma = pltpu.SemaphoreType.DMA
    both = 2 * rows
    wide = pltpu.VMEM((rows, hid), B16)
    thin = pltpu.VMEM((rows, LANES), F32)
    low = pltpu.VMEM((rows, lat), B16)
    part_low = pltpu.VMEM((QROWS, hid), B16)
    q_wide = pltpu.VMEM((both, hid), B16)
    lat_out, grad_out, recv_q, recv_0, small = pl.pallas_call(
        functools.partial(step_kernel, dims),
        out_shape=[
            jax.ShapeDtypeStruct((rows, lat), B16),
            jax.ShapeDtypeStruct((rows, lat), F32),
            jax.ShapeDtypeStruct((heads, 2, block, LANES), B16),
            jax.ShapeDtypeStruct((block0, LANES), B16),
            jax.ShapeDtypeStruct((small_rows, LANES), F32),
        ],
        in_specs=[anywhere] + [vmem] * 7 + [anywhere] * 5 + [vmem] * 10,
        out_specs=[anywhere] * 5,
        scratch_shapes=[
            pltpu.VMEM((both, 6 * LANES), B16),
            pltpu.VMEM((both, LANES), F32),
            pltpu.VMEM((2, in_width + VECS, hid), B16),
            pltpu.VMEM((2, hid, hid), B16),
            pltpu.VMEM((2, LANES, hid), B16),
            pltpu.VMEM((2, bin_count, hid), B16),
            pltpu.VMEM((in_width + VECS, hid), B16),
            pltpu.VMEM((hid, hid), B16),
            pltpu.VMEM((hid, lat), B16),
            pltpu.VMEM((6, 8, hid), F32),
            pltpu.VMEM((8, LANES), F32),
            pltpu.VMEM((2 * LANES, 2 * LANES), B16),
            pltpu.VMEM((2, 8, rows), F32),
            pltpu.VMEM((2, act_width, rows), B16),
            pltpu.VMEM((VECS, hid), F32),
            pltpu.VMEM((both, in_width), F32),
            q_wide, q_wide, q_wide, q_wide,
            pltpu.VMEM((both, LANES), B16),
            part_low, part_low, part_low, part_low,
            pltpu.VMEM((QROWS, LANES), F32),
            pltpu.VMEM((QROWS, hid), F32),
            wide, wide, wide, wide, wide, wide, wide, wide, thin,
            low,
            pltpu.VMEM((rows, lat), F32),
            low, low, low, low, low,
            pltpu.VMEM((2, CHIPS, block0, LANES), B16),
            pltpu.VMEM((3, CHIPS, block, LANES), B16),
            pltpu.VMEM((CHIPS, block0, LANES), B16),
            pltpu.VMEM((2, 32, hid), F32),
            pltpu.VMEM((3, 8, LANES), F32),
            pltpu.VMEM((24, lat), F32),
            pltpu.VMEM((16, lat), F32),
            pltpu.VMEM((small_rows, LANES), F32),
            pltpu.VMEM((small_rows, LANES), F32),
            pltpu.VMEM((CHIPS, small_rows // 2, LANES), F32),
            pltpu.VMEM((small_rows // 2, LANES), F32),
            pltpu.VMEM((steps, small_rows // 2, LANES), F32),
            pltpu.VMEM((small_rows, LANES), F32),
            dma((10,)), dma((chunks,)), dma((2 * chunks + 1,)),
            dma((chunks,)), dma((chunks,)), dma((chunks,)), dma((chunks,)),
            dma((2,)), dma((2,)), dma((chunks,)), dma((chunks,)), dma((chunks,)), dma((chunks,)),
            dma((4, CHIPS)), dma((4, CHIPS)), dma((4,)), dma((3, CHIPS)), dma((heads, 2)),
            dma((2,)), dma((2,)), dma((CHIPS,)), dma((CHIPS,)), dma((steps,)), dma((steps,)),
            dma((CHIPS, 3)), dma((CHIPS, 3)), dma((CHIPS, 3)), dma((CHIPS, 3)),
            pltpu.SemaphoreType.REGULAR, pltpu.SemaphoreType.REGULAR,
        ],
        compiler_params=pltpu.CompilerParams(
            collective_id=0, has_side_effects=True, vmem_limit_bytes=16350 * 2**12
        ),
        name="step",
    )(
        latent_in, actions[0].T, task_ids[None], valid[None], bins, fraction,
        action_mask.T, table, latent_cot[0],
        w_in[0], w_mid[0], w_dyn_out[0], w_q_out[0].transpose(0, 2, 1),
        b_in[0], g_in[0], beta_in[0], b_mid[0], g_mid[0], beta_mid[0],
        b_dyn_out, g_dyn_out, beta_dyn_out, b_q_out[0],
    )
    across = [[q * PEERS + r for q in range(groups)] for r in range(PEERS)]
    if groups > 1:
        small = lax.psum(small, "dp", axis_index_groups=across)

    def shape(*dims):
        return jax.ShapeDtypeStruct(dims, F32)

    lat_out, grad_out, part_in, part_mid, part_dyn, part_q, b_dyn, g_dyn, s_dyn, q_bias, grad_table, rms, *vecs = (
        pl.pallas_call(
            functools.partial(finish_kernel, (lat, in_width, hid, heads, bin_count, tasks, emb)),
            out_shape=[
                jax.ShapeDtypeStruct((rows, lat), B16),
                shape(rows, lat),
                shape(heads + 1, in_width, LANES),
                shape(heads + 1, hid, LANES),
                shape(LANES, lat),
                shape(heads, bin_count, 1, LANES),
                shape(1, lat), shape(1, lat), shape(1, lat),
                shape(heads, 1, bin_count),
                shape(tasks, emb),
                shape(1, 2),
            ] + [shape(heads + 1, 1, LANES)] * 6,
            in_specs=[hbm] * 5,
            out_specs=[hbm] * 4 + [vmem] * 14,
            scratch_shapes=[
                pltpu.VMEM((heads, 2, block, LANES), B16),
                pltpu.VMEM((block0, LANES), B16),
                pltpu.VMEM((small_rows, LANES), F32),
                pltpu.VMEM((heads + 1, in_width, LANES), F32),
                pltpu.VMEM((heads + 1, hid, LANES), F32),
                pltpu.VMEM((rows, lat), B16),
                pltpu.VMEM((rows, lat), F32),
                dma((heads + 4,)),
                dma((2 * heads + 4,)),
            ],
            compiler_params=pltpu.CompilerParams(vmem_limit_bytes=60 * 2**20),
            name="finish",
        )(recv_q, recv_0, small, lat_out, grad_out)
    )

    def owned(piece, dim):
        if groups == 1:
            return piece
        piece = lax.psum_scatter(piece, "dp", scatter_dimension=dim, axis_index_groups=across, tiled=True)
        moves = [(q * PEERS + r, r * groups + q) for q in range(groups) for r in range(PEERS)]
        return lax.ppermute(piece, "dp", moves)

    part_in, part_mid, part_q = owned(part_in, 2), owned(part_mid, 2), owned(part_q, 3)
    part_dyn = owned(part_dyn, 0)
    vecs = [owned(v, 2).transpose(1, 0, 2) for v in vecs]
    return (
        lat_out[None],
        grad_out[None],
        part_in[None],
        *vecs[:3],
        part_mid[None],
        *vecs[3:],
        part_dyn[None],
        b_dyn,
        g_dyn,
        s_dyn,
        part_q.transpose(2, 0, 3, 1),
        q_bias.transpose(1, 0, 2),
        grad_table,
        rms,
    )


def solution(mesh):
    placed = (
        P("dp", None),
        P("section", "dp", None),
        P("dp"),
        P("dp"),
        P(),
        P("section", "dp"),
        P("section", "dp"),
        P("section", "dp", None),
        P("section", None, None, None),
        P("section", None, None),
        P("section", None, None),
        P("section", None, None),
        P("section", None, None, None),
        P("section", None, None),
        P("section", None, None),
        P("section", None, None),
        P("section", None, None),
        P("section", None),
        P("section", None),
        P("section", None),
        P("section", None, None, None),
        P("section", None, None),
        P(),
    )
    return jax.shard_map(
        on_device,
        mesh=mesh,
        in_specs=placed,
        out_specs=(
            P("section", "dp", None),
            P("section", "dp", None),
            P("section", None, None, "dp"),
            P("section", None, "dp"),
            P("section", None, "dp"),
            P("section", None, "dp"),
            P("section", None, None, "dp"),
            P("section", None, "dp"),
            P("section", None, "dp"),
            P("section", None, "dp"),
            P("section", "dp", None),
            P("section", None),
            P("section", None),
            P("section", None),
            P("section", None, "dp", None),
            P("section", None, None),
            P(),
            P("section", None),
        ),
        check_vma=False,
    )
```

```python
import functools

import jax
import jax.numpy as jnp
from jax import lax
from jax.experimental import pallas as pl
from jax.experimental.pallas import tpu as pltpu
from jax.sharding import PartitionSpec as P

GROUP = 8
EPS = 1e-05
F32 = jnp.float32
B16 = jnp.bfloat16
MESH = pl.DeviceIdType.MESH

LANES = 128
CHIPS = 4
PEERS = 2 * CHIPS
CHUNK = 128
QROWS = 256
SUB = 256
VECS = 16

NN = (((1,), (0,)), ((), ()))
NT = (((1,), (1,)), ((), ()))
TN = (((0,), (0,)), ((), ()))


def dot(a, b, dims=NN):
    return lax.dot_general(a, b, dims, preferred_element_type=F32)


def split_dot(a, b, dims=NN):
    high = a.astype(B16)
    low = (a - high.astype(F32)).astype(B16)
    return dot(high, b, dims) + dot(low, b, dims)


def split_dot_right(a, b, dims):
    high = b.astype(B16)
    low = (b - high.astype(F32)).astype(B16)
    return dot(a, high, dims) + dot(a, low, dims)


def norm_mish(x, gain, shift):
    center = x - jnp.mean(x, -1, keepdims=True)
    spread = jnp.mean(center * center, -1, keepdims=True)
    scale = lax.rsqrt(spread + EPS)
    n = center * scale
    u = n * gain + shift
    w = jnp.exp(jnp.minimum(u, 30.0))
    top = w * (w + 2.0)
    over = pltpu.reciprocal(top + 2.0, approx=True)
    act = u * (top * over)
    slope = (top + 4.0 * (u * (top - w)) * over) * (over * gain)
    return act, n, slope, scale


def padded(count):
    return (count + 15) // 16 * 16


def tiles(size, step=256):
    return [(lo, min(lo + step, size)) for lo in range(0, size, step)]


def eight_rows(x):
    return x.reshape(x.shape[0] // 8, 8, x.shape[1]).sum(0)


def each_sub(count, body):
    sub = min(SUB, count)
    for j in range(0, count, sub):
        body(j, sub)


def layer_forward(pre, count, bias, gain, shift, act_ref, act_at, n_ref, slope_ref, scale_ref, lane, at):
    def body(j, sub):
        x = pre[pl.ds(j, sub), :]
        if bias is not None:
            x = x + bias
        act, n, slope, scale = norm_mish(x, gain, shift)
        act_ref[pl.ds(act_at + j, sub), :] = act.astype(B16)
        here = pl.ds(at + j, sub)
        n_ref[here, :] = n.astype(n_ref.dtype)
        slope_ref[here, :] = slope.astype(slope_ref.dtype)
        scale_ref[here, lane : lane + 1] = scale

    each_sub(count, body)


def layer_backward(pre, count, n_ref, slope_ref, scale_ref, lane, at, out_ref, out_at, sums, first):
    def body(j, sub):
        here = pl.ds(at + j, sub)
        n = n_ref[here, :].astype(F32)
        dn = pre[pl.ds(j, sub), :] * slope_ref[here, :].astype(F32)
        by_n = dn * n
        mean_dn = jnp.mean(dn, -1, keepdims=True)
        mean_by_n = jnp.mean(by_n, -1, keepdims=True)
        out = (dn - mean_dn - n * mean_by_n) * scale_ref[here, lane : lane + 1]
        out_ref[pl.ds(out_at + j, sub), :] = out.astype(B16)
        sums[first : first + 8, :] += eight_rows(by_n)
        sums[first + 8 : first + 16, :] += eight_rows(dn)

    each_sub(count, body)


def step_kernel(dims, *refs):
    rows, lat, act_width, in_width, hid, heads, bins, tasks, emb, steps = dims
    side_width = in_width - lat
    at_mid = in_width + VECS
    at_out = at_mid + hid
    block = at_out + padded(bins)
    block0 = at_out + lat
    both = 2 * rows
    ones_at = in_width // LANES * LANES
    pieces = ((0, at_mid), (at_mid, at_out), (at_out, block0))
    (
        lat_in, acts, task, valid, bin_at, part_of, amask, table, cot_in, w_in, w_mid, w_dyn, w_q,
        b_in, g_in, s_in, b_mid, g_mid, s_mid, b_dyn, g_dyn, s_dyn, b_q,
        lat_out, grad_out, recv_q, recv_0, small_out,
        x, m, wi, wm, wq, wq_raw, wi0, wm0, wd, vec, bq, diag,
        lines, acting, vec_lines, ig, act1, act2, spg, fpg, qg, n1, d1, n2, d2, q_scales, pre,
        act1_0, act2_0, spg_0, fpg_0, n1_0, d1_0, n2_0, d2_0, scales,
        dyn_n, new_lat, lat_low, cot, arrived, pair_grad, pair_send,
        gb, half_q, half_0, sums, q_sums, dyn_sums, stat, small, small_mate, small_chips, small_half, small_steps, small_done,
        w_sem, in_sem, out_sem, lat_s, lat_r, px_s, px_r, side_s, side_r, pg_s, pg_r, gr_s, gr_r,
        half_s, half_r, own_s, rb_s, rb_r, sm_s, sm_r, ch_s, ch_r, tb_s, tb_r, up_s, up_r, dn_s, dn_r, up_ok, dn_ok,
    ) = refs
    section = lax.axis_index("section")
    d = lax.axis_index("dp")
    place = lax.rem(d, PEERS)
    base = d - place
    chip = place // 2
    core = lax.rem(place, 2)
    edge = (chip == 0) | (chip == CHIPS - 1)
    lower = chip < CHIPS // 2
    side_of = chip // 2
    last = steps - 1
    mate = base + chip * 2 + (1 - core)
    pair = base + (chip + 1 - 2 * lax.rem(chip, 2)) * 2 + core
    following = jnp.minimum(section + 1, last)
    before = jnp.maximum(section - 1, 0)
    chunks = rows // CHUNK
    jobs = jnp.where(edge, 2, 3)
    held = (section >= steps - 2) & edge
    farthest = CHIPS - 1 - chip
    first_head = jnp.where(edge, 1, 3)

    def remote(src, dst, send, recv, to):
        return pltpu.make_async_remote_copy(
            src_ref=src, dst_ref=dst, send_sem=send, recv_sem=recv, device_id=to, device_id_type=MESH
        )

    def chunk_at(i):
        return pl.multiple_of(i * CHUNK, CHUNK)

    loads = [
        pltpu.make_async_copy(w_in.at[0], wi0.at[0:in_width], w_sem.at[0]),
        pltpu.make_async_copy(w_mid.at[0], wm0, w_sem.at[1]),
        pltpu.make_async_copy(w_dyn, wd, w_sem.at[2]),
    ]

    def job_loads(job):
        slot = lax.rem(job, 2)
        h = first_head + job
        return [
            pltpu.make_async_copy(w_in.at[h], wi.at[slot, 0:in_width], w_sem.at[3 + 3 * slot]),
            pltpu.make_async_copy(w_mid.at[h], wm.at[slot], w_sem.at[4 + 3 * slot]),
            pltpu.make_async_copy(w_q.at[h - 1], wq_raw.at[slot], w_sem.at[5 + 3 * slot]),
        ]

    load_cot = pltpu.make_async_copy(cot_in, cot, w_sem.at[9])

    def load_lat(i):
        here = pl.ds(chunk_at(i), CHUNK)
        return pltpu.make_async_copy(lat_in.at[here], x.at[here, 0:lat], in_sem.at[i])

    barrier = pltpu.get_barrier_semaphore()
    for other in range(1, PEERS):
        to = base + lax.rem(place + other, PEERS)
        pl.semaphore_signal(barrier, inc=1, device_id=(section, to), device_id_type=MESH)
    for other in range(1, steps):
        to = lax.rem(section + other, steps)
        pl.semaphore_signal(barrier, inc=1, device_id=(to, d), device_id_type=MESH)

    loads[0].start()

    @pl.when(section == 0)
    def _():
        for i in range(chunks):
            load_lat(i).start()

    for copy in loads[1:] + job_loads(jnp.int32(0)) + job_loads(jnp.int32(1)):
        copy.start()
    load_cot.start()

    head_lines = [task[...].astype(F32), valid[...].astype(F32), bin_at[...].astype(F32), part_of[...]]
    lines[0] = jnp.concatenate(head_lines + [jnp.zeros((4, rows), F32)], 0)
    acting[0] = acts[...]

    def one_hot(lo, count):
        task_lane = lax.broadcasted_iota(jnp.int32, (count, tasks), 1).astype(F32)
        return (m[lo : lo + count, 0:1] == task_lane).astype(F32).astype(B16)

    def prepare(which):
        lo = which * rows
        m[lo : lo + rows, 0:8] = lines[which].T
        hot = one_hot(lo, rows)
        mask = dot(amask[...].astype(F32).astype(B16), hot, NT)
        used = (acting[which].astype(F32) * mask).T
        x[lo : lo + rows, lat:in_width] = jnp.concatenate(
            [used.astype(B16), dot(hot, table[...]).astype(B16)], 1
        )

    lane = lax.broadcasted_iota(jnp.int32, (both, LANES), 1)
    x[:, ones_at : ones_at + LANES] = (lane == in_width - ones_at).astype(F32).astype(B16)
    prepare(0)
    for t, source in enumerate((b_in, g_in, s_in, b_mid, g_mid, s_mid)):
        vec[t, 0 : heads + 1, :] = source[...].astype(F32)
    shift = GROUP.bit_length() - 1
    diag[...] = (
        lax.shift_right_logical(lax.broadcasted_iota(jnp.int32, diag.shape, 0), shift)
        == lax.shift_right_logical(lax.broadcasted_iota(jnp.int32, diag.shape, 1), shift)
    ).astype(F32).astype(B16)

    def group_sums(values):
        width = diag.shape[0]
        return jnp.concatenate(
            [split_dot(values[:, lo : lo + width], diag[...]) for lo in range(0, lat, width)], 1
        )

    def bias_rows(h):
        line = lax.broadcasted_iota(jnp.int32, (VECS, hid), 0)
        return jnp.where(line == 0, vec[0, pl.ds(h, 1), :], 0.0).astype(B16)

    wi0[in_width:at_mid, :] = bias_rows(0)
    stat[...] = jnp.zeros(stat.shape, F32)

    def clear():
        bq[...] = jnp.full(bq.shape, -1e30, F32)
        bq[0:heads, 0:bins] = b_q[...].astype(F32)
        wq[...] = jnp.zeros(wq.shape, B16)
        sums[...] = jnp.zeros(sums.shape, F32)
        ig[...] = jnp.zeros(ig.shape, F32)
        q_sums[...] = jnp.zeros(q_sums.shape, F32)
        dyn_sums[...] = jnp.zeros(dyn_sums.shape, F32)
        small[...] = jnp.zeros(small.shape, F32)

    pl.semaphore_wait(barrier, PEERS - 1 + steps - 1)

    side_copies = [
        remote(lines.at[0], lines.at[1], side_s.at[0], side_r.at[0], (section, pair)),
        remote(acting.at[0], acting.at[1], side_s.at[1], side_r.at[1], (section, pair)),
    ]
    for copy in side_copies:
        copy.start()

    def settle():
        clear()
        for copy in side_copies:
            copy.wait_recv()
        prepare(1)

    @pl.when(section == last)
    def _():
        arrived[...] = jnp.zeros(arrived.shape, B16)

    @pl.when(section > 0)
    def _():
        settle()

    for copy in loads:
        copy.wait()

    def vec_of(t, h):
        return vec[t, pl.ds(h, 1), :]

    def lat_copy(i):
        here = pl.ds(chunk_at(i), CHUNK)
        return remote(
            lat_low.at[here], x.at[here, 0:lat], lat_s.at[i], lat_r.at[i], (following, d)
        )

    def pair_copy(i):
        here = chunk_at(i)
        return remote(
            x.at[pl.ds(here, CHUNK), 0:lat], x.at[pl.ds(rows + here, CHUNK), 0:lat],
            px_s.at[i], px_r.at[i], (section, pair),
        )

    def lat_store(i):
        here = pl.ds(chunk_at(i), CHUNK)
        return pltpu.make_async_copy(lat_low.at[here], lat_out.at[here], out_sem.at[i])

    def forward_chunk(i, carry):
        at = chunk_at(i)
        here = pl.ds(at, CHUNK)

        @pl.when(section > 0)
        def _():
            lat_copy(i).wait_recv()

        @pl.when(section == 0)
        def _():
            load_lat(i).wait()

        pair_copy(i).start()
        pre[0:CHUNK, :] = dot(x[here, 0:at_mid], wi0[...])
        layer_forward(
            pre, CHUNK, None, vec[1, 0:1, :], vec[2, 0:1, :], act1_0, at, n1_0, d1_0, scales, 0, at
        )
        pre[0:CHUNK, :] = dot(act1_0[here, :], wm0[...])
        layer_forward(
            pre, CHUNK, vec[3, 0:1, :], vec[4, 0:1, :], vec[5, 0:1, :], act2_0, at, n2_0, d2_0, scales, 1, at
        )
        out = dot(act2_0[here, :], wd[...]) + b_dyn[...].astype(F32)
        center = out - jnp.mean(out, -1, keepdims=True)
        scale = lax.rsqrt(jnp.mean(center * center, -1, keepdims=True) + EPS)
        normal = center * scale
        dyn_n[here, :] = normal.astype(B16)
        scales[here, 2:3] = scale
        power = jnp.exp(normal * g_dyn[...].astype(F32) + s_dyn[...].astype(F32))
        fresh = power * pltpu.reciprocal(group_sums(power), approx=True)
        new_lat[here, :] = fresh
        low = fresh.astype(B16)
        lat_low[here, :] = low

        @pl.when(section < last)
        def _():
            lat_copy(i).start()

        lat_store(i).start()
        wide = low.astype(F32)
        stat[0:8, :] += eight_rows(m[here, 1:2] * (wide * wide))
        return carry

    lax.fori_loop(0, chunks, forward_chunk, 0)

    @pl.when(section == 0)
    def _():
        settle()

    def pg_copy(i):
        here = pl.ds(chunk_at(i), CHUNK)
        return remote(
            pair_send.at[here], pair_grad.at[here], pg_s.at[i], pg_r.at[i], (section, pair)
        )

    def q_chunk(job, at):
        here = pl.ds(at, QROWS)
        h = first_head + job
        slot = lax.rem(job, 2)
        pre[...] = dot(x[here, 0:at_mid], wi[slot])
        layer_forward(
            pre, QROWS, None, vec_of(1, h), vec_of(2, h), act1, at, n1, d1, q_scales, 0, 0
        )
        pre[...] = dot(act1[here, :], wm[slot])
        layer_forward(
            pre, QROWS, vec_of(3, h), vec_of(4, h), vec_of(5, h), act2, at, n2, d2, q_scales, 1, 0
        )
        logits = dot(act2[here, :], wq[slot], NT) + bq[pl.ds(h - 1, 1), :]
        power = jnp.exp(logits - jnp.max(logits, -1, keepdims=True))
        chance = power / jnp.sum(power, -1, keepdims=True)
        lane = lax.broadcasted_iota(jnp.int32, (QROWS, LANES), 1).astype(F32)
        low_bin = m[here, 2:3]
        part = m[here, 3:4]
        target = jnp.where(lane == low_bin, 1.0 - part, 0.0) + jnp.where(lane == low_bin + 1.0, part, 0.0)
        grad = (m[here, 1:2] * (chance - target)).astype(B16)
        qg[here, :] = grad
        q_sums[job] += eight_rows(grad.astype(F32))
        pre[...] = dot(grad, wq[slot])
        layer_backward(pre, QROWS, n2, d2, q_scales, 1, 0, spg, at, sums.at[0], 16)
        pre[...] = dot(spg[here, :], wm[slot], NT)
        layer_backward(pre, QROWS, n1, d1, q_scales, 0, 0, fpg, at, sums.at[0], 0)
        for lo, hi in tiles(in_width):
            ig[here, lo:hi] += dot(fpg[here, :], wi[slot, lo:hi, :], NT)

    q_chunks = both // QROWS
    own_chunks = rows // QROWS

    def q_job(job):
        for copy in job_loads(job):
            copy.wait()
        slot = lax.rem(job, 2)
        wq[slot, 0:bins, :] = wq_raw[slot]
        wi[slot, in_width:at_mid, :] = bias_rows(first_head + job)
        sums[0] = jnp.zeros(sums.shape[1:], F32)

        def body(i, carry):
            which = lax.rem(i + jnp.where(job == 0, 0, own_chunks), q_chunks)
            at = pl.multiple_of(which * QROWS, QROWS)

            @pl.when((job == 0) & (which == own_chunks))
            def _():
                def pair_here(j, carry):
                    pair_copy(j).wait_recv()
                    return carry

                lax.fori_loop(0, chunks, pair_here, 0)

            q_chunk(job, at)

            @pl.when((job == jobs - 1) & (which >= own_chunks))
            def _():
                for k in range(QROWS // CHUNK):
                    j = (which - own_chunks) * (QROWS // CHUNK) + k
                    to = chunk_at(j)
                    pair_send[pl.ds(to, CHUNK), :] = ig[pl.ds(rows + to, CHUNK), 0:lat].astype(B16)
                    pg_copy(j).start()

            return carry

        lax.fori_loop(0, q_chunks, body, 0)

        @pl.when(job + 2 < jobs)
        def _():
            for copy in job_loads(job + 2):
                copy.start()

    def half_copy(job, z, q):
        if q:
            src, dst = gb.at[1 - core, z, 0:block], half_q.at[job, z]
        else:
            src, dst = gb.at[1 - core, z], half_0.at[z]
        return remote(src, dst, half_s.at[job, z], half_r.at[job, z], (section, mate))

    def owner_copy(job, z):
        head = first_head + job - 1
        return remote(
            half_q.at[job, z], recv_q.at[head, side_of], rb_s.at[job, z], rb_r.at[head, side_of],
            (section, base + 2 * z + core),
        )

    def keep_copy(job):
        return pltpu.make_async_copy(
            half_q.at[job, chip], recv_q.at[first_head + job - 1, side_of], own_s.at[job]
        )

    def add_rows(dst, src, size):
        step = size // 4 // 16 * 16
        for part in range(4):
            span = slice(part * step, size if part == 3 else (part + 1) * step)
            dst[span, :] = (dst[span, :].astype(F32) + src[span, :].astype(F32)).astype(B16)

    def at_chip(z):
        return (section, base + 2 * z + core)

    def stripe(z):
        return pl.ds(pl.multiple_of(z * LANES, LANES), LANES)

    def up_piece(z, p):
        size = pieces[p][1] - pieces[p][0]
        return (act1.at[0:size, stripe(z)], act1.at[0:size, stripe(CHIPS + z)], act2.at[0:size, stripe(z)])[p]

    def down_piece(z, p):
        size = pieces[p][1] - pieces[p][0]
        return (spg.at[0:size, stripe(z)], spg.at[0:size, stripe(CHIPS + z)], act2.at[0:size, stripe(CHIPS + z)])[p]

    def up_copy(z, p):
        return remote(
            half_0.at[z, pieces[p][0] : pieces[p][1]], up_piece(z, p), up_s.at[z, p], up_r.at[z, p],
            at_chip(jnp.minimum(chip + 1, CHIPS - 1)),
        )

    def down_copy(z, p):
        return remote(
            half_0.at[z, pieces[p][0] : pieces[p][1]], down_piece(z, p), dn_s.at[z, p], dn_r.at[z, p],
            at_chip(jnp.maximum(chip - 1, 0)),
        )

    def add_piece(piece, z, p):
        lo, hi = pieces[p]
        half_0[z, lo:hi, :] = (half_0[z, lo:hi, :].astype(F32) + piece(z, p)[...].astype(F32)).astype(B16)

    def weight_grads(job, q):
        if q:
            count, a1, a2, sp, fp, own_sums = both, act1, act2, spg, fpg, 0
        else:
            count, a1, a2, sp, fp, own_sums = rows, act1_0, act2_0, spg_0, fpg_0, 1
        size = block if q else block0
        h = first_head + job if q else 0
        line_at = lax.broadcasted_iota(jnp.int32, (VECS, hid), 0)
        vectors = jnp.zeros((VECS, hid), F32)
        for t, (first, gain) in enumerate(((0, 1), (8, 1), (None, None), (16, 4), (24, 4))):
            if gain is not None:
                line = jnp.sum(sums[own_sums, first : first + 8, :], 0, keepdims=True) / vec_of(gain, h)
                vectors = jnp.where(line_at == t + 1, line, vectors)
        vec_lines[...] = vectors
        row_at = lax.broadcasted_iota(jnp.int32, (VECS, 2 * LANES), 0)

        def order(i):
            far_first = jnp.where(lower, CHIPS - 1 - i, i)
            pair_first = lax.rem(jnp.where(lower, CHIPS - i, i + CHIPS - 1), CHIPS)
            if not q:
                return far_first
            return jnp.where(edge | ((section == last) & (job == jobs - 1)), far_first, pair_first)

        def make(z):
            cols = pl.ds(pl.multiple_of(z * 2 * LANES, 2 * LANES), 2 * LANES)
            for left, right, first, size_of in ((x, fp, 0, at_mid), (a1, sp, at_mid, hid)):
                for lo, hi in tiles(size_of):
                    grad = dot(left[0:count, lo:hi], right[0:count, cols], TN)
                    if left is x and hi == at_mid:
                        plain = grad[0 : in_width - lo]
                        bias_mid = dot(x[0:count, ones_at : ones_at + LANES], sp[0:count, cols], TN)
                        bias_mid = bias_mid[in_width - ones_at : in_width - ones_at + 1]
                        lines_here = grad[in_width - lo :] + vec_lines[:, cols]
                        grad = jnp.concatenate([plain, jnp.where(row_at == 3, bias_mid, lines_here)], 0)
                    for p in range(2):
                        gb[p, z, first + lo : first + hi, :] = grad[:, p * LANES : (p + 1) * LANES].astype(B16)
            if q:
                g_out = dot(qg[0:count, :], a2[0:count, cols], TN)
                for p in range(2):
                    gb[p, z, at_out:block, :] = g_out[0 : block - at_out, p * LANES : (p + 1) * LANES].astype(B16)
            else:
                g_out = dot(a2[0:count, cols], arrived[0:count, :], TN)
                for p in range(2):
                    for t in range(lat // LANES):
                        gb[p, z, at_out + t * LANES : at_out + (t + 1) * LANES, :] = g_out[
                            p * LANES : (p + 1) * LANES, t * LANES : (t + 1) * LANES
                        ].astype(B16)
            half_copy(job, z, q).start()

        def finish(z):
            half_copy(job, z, q).wait_recv()
            if q:
                add_rows(half_q.at[job, z], gb.at[core, z], size)

                @pl.when((z != chip) & ~((job == jobs - 1) & held & (z == farthest)))
                def _():
                    owner_copy(job, z).start()

                @pl.when(z == chip)
                def _():
                    keep_copy(job).start()
            else:
                add_rows(half_0.at[z], gb.at[core, z], size)

                @pl.when((chip == 0) & (z != chip))
                def _():
                    for p in range(3):
                        up_copy(z, p).start()

                @pl.when((chip == CHIPS - 1) & (z != chip))
                def _():
                    for p in range(3):
                        down_copy(z, p).start()

        def body(i, carry):
            @pl.when(i < CHIPS)
            def _():
                make(order(i))

            if not q:
                @pl.when(i == 1)
                def _():
                    small_over_chips()

            @pl.when(i > 0)
            def _():
                finish(order(i - 1))

            return carry

        lax.fori_loop(0, CHIPS + 1, body, 0)

        def sent(z, carry):
            half_copy(job, z, q).wait_send()
            return carry

        lax.fori_loop(0, CHIPS, sent, 0)

    def back_copy(i):
        here = pl.ds(chunk_at(i), CHUNK)
        return remote(lat_low.at[here], arrived.at[here], gr_s.at[i], gr_r.at[i], (before, d))

    def grad_store(i):
        here = pl.ds(chunk_at(i), CHUNK)
        return pltpu.make_async_copy(ig.at[here, 0:lat], grad_out.at[here], out_sem.at[chunks + i])

    def lat_sent(i, carry):
        lat_store(i).wait()

        @pl.when(section < last)
        def _():
            lat_copy(i).wait_send()

        return carry

    def backward_chunk(i, carry):
        at = chunk_at(i)
        here = pl.ds(at, CHUNK)

        @pl.when(section < last)
        def _():
            back_copy(i).wait_recv()

        out_grad = cot[here, :].astype(F32) + arrived[here, :].astype(F32)
        fresh = new_lat[here, :]
        normal = dyn_n[here, :].astype(F32)
        norm_grad = fresh * (out_grad - group_sums(out_grad * fresh))
        by_n = norm_grad * normal
        gain = g_dyn[...].astype(F32)
        dm = norm_grad * gain
        mean_dm = jnp.mean(dm, -1, keepdims=True)
        mean_by_n = jnp.mean(by_n * gain, -1, keepdims=True)
        low = ((dm - mean_dm - normal * mean_by_n) * scales[here, 2:3]).astype(B16)
        arrived[here, :] = low
        dyn_sums[0:8, :] += eight_rows(low.astype(F32))
        dyn_sums[8:16, :] += eight_rows(by_n)
        dyn_sums[16:24, :] += eight_rows(norm_grad)
        pre[0:CHUNK, :] = dot(low, wd[...], NT)
        layer_backward(pre, CHUNK, n2_0, d2_0, scales, 1, at, spg_0, at, sums.at[1], 16)
        pre[0:CHUNK, :] = dot(spg_0[here, :], wm0[...], NT)
        layer_backward(pre, CHUNK, n1_0, d1_0, scales, 0, at, fpg_0, at, sums.at[1], 0)
        back_in = dot(fpg_0[here, :], wi0[0:in_width, :], NT)
        pg_copy(i).wait_recv()

        @pl.when((i == chunks - 1) & held)
        def _():
            owner_copy(jobs - 1, farthest).start()

        total = back_in[:, 0:lat] + ig[here, 0:lat] + pair_grad[here, :].astype(F32)
        lat_low[here, :] = total.astype(B16)

        @pl.when(section > 0)
        def _():
            back_copy(i).start()

        ig[here, 0:lat] = total
        grad_store(i).start()
        stat[8:16, :] += eight_rows(m[here, 1:2] * (total * total))
        ig[here, lat:in_width] += back_in[:, lat:in_width]
        return carry

    half_rows = small.shape[0] // 2
    my_rows = pl.ds(pl.multiple_of(core * half_rows, half_rows), half_rows)

    def to_mate(src, dst, k):
        return remote(src, dst, sm_s.at[k], sm_r.at[k], (section, mate))

    def small_to_mate():
        return to_mate(small, small_mate, 0)

    def small_to_chip(other):
        to = lax.rem(chip + other, CHIPS)
        return remote(
            small.at[my_rows], small_chips.at[chip], ch_s.at[other], ch_r.at[chip], (section, base + 2 * to + core)
        )

    def small_from_chip(other):
        to = lax.rem(chip + other, CHIPS)
        return remote(
            small.at[my_rows], small_chips.at[to], ch_s.at[other], ch_r.at[to], (section, base + 2 * to + core)
        )

    def small_to_section(other):
        to = lax.rem(section + other, steps)
        return remote(small_half, small_steps.at[section], tb_s.at[other], tb_r.at[section], (to, d))

    def small_from_section(other):
        source = lax.rem(section + other, steps)
        return remote(small_half, small_steps.at[source], tb_s.at[other], tb_r.at[source], (source, d))

    def small_back():
        return to_mate(small_done.at[my_rows], small_done.at[my_rows], 1)

    def small_over_chips():
        small_to_mate().wait_recv()
        small_to_mate().wait_send()
        small[...] += small_mate[...]
        small_chips[chip] = small[my_rows, :]
        for other in range(1, CHIPS):
            small_to_chip(other).start()

    def small_over_sections():
        for other in range(1, CHIPS):
            small_from_chip(other).wait_recv()
        total = small_chips[0]
        for source in range(1, CHIPS):
            total = total + small_chips[source]
        small_half[...] = total
        small_steps[section] = total
        for other in range(1, steps):
            small_to_section(other).start()

    def small_last():
        for other in range(1, steps):
            small_from_section(other).wait_recv()
        whole = small_steps[0]
        for source in range(1, steps):
            whole = whole + small_steps[source]
        row = lax.broadcasted_iota(jnp.int32, whole.shape, 0) + core * half_rows
        small_done[my_rows, :] = jnp.where(row < tasks, whole, small_half[...])
        small_back().start()
        for other in range(1, CHIPS):
            small_to_chip(other).wait_send()
        for other in range(1, steps):
            small_to_section(other).wait_send()
        small_back().wait_recv()
        small_back().wait_send()

    def send_small():
        table_part = jnp.zeros((tasks, side_width), F32)
        for lo in (0, rows):
            table_part += split_dot_right(one_hot(lo, rows), ig[lo : lo + rows, lat:in_width], TN)
        small[0:tasks, 0:emb] = table_part[:, side_width - emb :]
        for t in range(3):
            line = jnp.sum(dyn_sums[8 * t : 8 * t + 8, :], 0, keepdims=True)
            for part in range(lat // LANES):
                row = tasks + t * (lat // LANES) + part
                small[row : row + 1, :] = line[:, part * LANES : (part + 1) * LANES]
        q_lines = [jnp.sum(q_sums[job], 0, keepdims=True) for job in range(3)]
        for h in range(heads):
            line = jnp.zeros((1, LANES), F32)
            for job in range(3):
                line += jnp.where(first_head + job == h + 1, q_lines[job], 0.0)
            row = tasks + 3 * (lat // LANES) + h
            small[row : row + 1, :] = line
        row = tasks + 3 * (lat // LANES) + heads
        lane = lax.broadcasted_iota(jnp.int32, (1, LANES), 1)
        count = jnp.sum(m[0:rows, 1:2], 0, keepdims=True)
        lat_square = jnp.sum(jnp.sum(stat[0:8, :], 0, keepdims=True), 1, keepdims=True)
        grad_square = jnp.sum(jnp.sum(stat[8:16, :], 0, keepdims=True), 1, keepdims=True)
        small[row : row + 1, :] = jnp.where(
            lane == 0, count, jnp.where(lane == 1, lat_square, jnp.where(lane == 2, grad_square, 0.0))
        )
        small_to_mate().start()

    waits = (section == last) & ~edge

    def turns(turn, carry):
        @pl.when(turn < jobs)
        def _():
            q_job(turn)

        @pl.when(turn == jobs)
        def _():
            load_cot.wait()
            lax.fori_loop(0, chunks, lat_sent, 0)
            lax.fori_loop(0, chunks, backward_chunk, 0)
            send_small()

        @pl.when((turn < jobs - 1) | ((turn == jobs - 1) & ~waits) | ((turn == jobs) & waits))
        def _():
            weight_grads(jnp.minimum(turn, jobs - 1), True)

            @pl.when((turn >= jobs - 1) & (chip > 0))
            def _():
                pl.semaphore_signal(up_ok, inc=1, device_id=at_chip(jnp.maximum(chip - 1, 0)), device_id_type=MESH)

            @pl.when((turn >= jobs - 1) & (chip < CHIPS - 1))
            def _():
                pl.semaphore_signal(
                    dn_ok, inc=1, device_id=at_chip(jnp.minimum(chip + 1, CHIPS - 1)), device_id_type=MESH
                )

        return carry

    lax.fori_loop(0, jobs + 1, turns, 0)

    @pl.when(chip < CHIPS - 1)
    def _():
        pl.semaphore_wait(up_ok, 1)

    @pl.when(chip > 0)
    def _():
        pl.semaphore_wait(dn_ok, 1)

    weight_grads(jnp.int32(3), False)

    def hops(turn, carry):
        @pl.when(((turn == 0) == lower) & ~edge)
        def _():
            for t in range(CHIPS - 1, 1, -1):
                @pl.when(t > chip)
                def _():
                    for p in range(3):
                        up_copy(t, p).wait_recv()
                        add_piece(up_piece, t, p)
                        up_copy(t, p).start()

        @pl.when(((turn == 0) != lower) & ~edge)
        def _():
            for t in range(CHIPS - 2):
                @pl.when(t < chip)
                def _():
                    for p in range(3):
                        down_copy(t, p).wait_recv()
                        add_piece(down_piece, t, p)
                        down_copy(t, p).start()

        @pl.when(turn == 0)
        def _():
            small_over_sections()

        return carry

    lax.fori_loop(0, 2, hops, 0)

    small_last()
    done = pltpu.make_async_copy(small_done, small_out, out_sem.at[2 * chunks])
    done.start()

    for copy in side_copies:
        copy.wait_send()

    def sends(i, carry):
        pair_copy(i).wait_send()
        pg_copy(i).wait_send()
        grad_store(i).wait()

        @pl.when(section > 0)
        def _():
            back_copy(i).wait_send()

        return carry

    lax.fori_loop(0, chunks, sends, 0)

    def job_done(job, carry):
        def body(other, carry):
            owner_copy(job, lax.rem(chip + other, CHIPS)).wait_send()
            return carry

        lax.fori_loop(1, CHIPS, body, 0)
        keep_copy(job).wait()
        return carry

    lax.fori_loop(0, jobs, job_done, 0)
    for head in range(heads):
        for half in range(2):
            source = (0, CHIPS - 1)[half] if head < 2 else (1, CHIPS - 2)[half]

            @pl.when(chip != source)
            def _():
                remote(
                    half_q.at[0, 0], recv_q.at[head, half], rb_s.at[0, 0], rb_r.at[head, half], at_chip(source)
                ).wait_recv()

    @pl.when(chip > 0)
    def _():
        for p in range(3):
            up_copy(chip, p).wait_recv()
            add_piece(up_piece, chip, p)

    @pl.when(chip < CHIPS - 1)
    def _():
        for p in range(3):
            down_copy(chip, p).wait_recv()
            add_piece(down_piece, chip, p)

    keep_0 = pltpu.make_async_copy(half_0.at[chip], recv_0, own_s.at[3])
    keep_0.start()
    for t in range(CHIPS):
        @pl.when(t > chip)
        def _():
            for p in range(3):
                up_copy(t, p).wait_send()

        @pl.when(t < chip)
        def _():
            for p in range(3):
                down_copy(t, p).wait_send()

    done.wait()
    keep_0.wait()


def finish_kernel(dims, *refs):
    lat, in_width, hid, heads, bins, tasks, emb = dims
    at_mid = in_width + VECS
    at_out = at_mid + hid
    recv_q, recv_0, small_in, lat_in, grad_in = refs[:5]
    lat_out, grad_out, w_in, w_mid, w_dyn, w_q, b_dyn, g_dyn, s_dyn, b_q, table, rms = refs[5:17]
    vecs = refs[17:23]
    part_q, part_0, small, sum_in, sum_mid, lat_held, grad_held, in_sem, out_sem = refs[23:]
    loads = [pltpu.make_async_copy(recv_0, part_0, in_sem.at[0])]
    loads += [pltpu.make_async_copy(recv_q.at[h], part_q.at[h], in_sem.at[1 + h]) for h in range(heads)]
    load_small = pltpu.make_async_copy(small_in, small, in_sem.at[1 + heads])
    through = [
        pltpu.make_async_copy(lat_in, lat_held, in_sem.at[2 + heads]),
        pltpu.make_async_copy(grad_in, grad_held, in_sem.at[3 + heads]),
    ]
    copies = [
        pltpu.make_async_copy(lat_held, lat_out, out_sem.at[0]),
        pltpu.make_async_copy(grad_held, grad_out, out_sem.at[1]),
    ]
    order = list(range(1, heads + 1)) + [0]
    for copy in [loads[h] for h in order] + through + [load_small]:
        copy.start()

    def total(h, lo, hi):
        if h == 0:
            return part_0[lo:hi, :].astype(F32)
        return part_q[h - 1, 0, lo:hi, :].astype(F32) + part_q[h - 1, 1, lo:hi, :].astype(F32)

    for h in order:
        loads[h].wait()
        sum_mid[h] = total(h, at_mid, at_out)
        sum_in[h] = total(h, 0, in_width)
        copies.append(pltpu.make_async_copy(sum_in.at[h], w_in.at[h], out_sem.at[2 + 2 * h]))
        copies.append(pltpu.make_async_copy(sum_mid.at[h], w_mid.at[h], out_sem.at[3 + 2 * h]))
        for copy in copies[-2:]:
            copy.start()
        lines = total(h, in_width, at_mid)
        for t in range(6):
            vecs[t][h] = lines[t : t + 1, :]
        if h:
            w_q[h - 1] = total(h, at_out, at_out + padded(bins))[0:bins, :].reshape(bins, 1, LANES)
    for arriving, leaving in zip(through, copies):
        arriving.wait()
        leaving.start()
    for t in range(lat // LANES):
        w_dyn[:, t * LANES : (t + 1) * LANES] = total(0, at_out + t * LANES, at_out + (t + 1) * LANES)
    load_small.wait()
    table[...] = small[0:tasks, 0:emb]
    for t, out in enumerate((b_dyn, g_dyn, s_dyn)):
        for part in range(lat // LANES):
            row = tasks + t * (lat // LANES) + part
            out[0:1, part * LANES : (part + 1) * LANES] = small[row : row + 1, :]
    at_q = tasks + 3 * (lat // LANES)
    for h in range(heads):
        b_q[h] = small[at_q + h : at_q + h + 1, 0:bins]
    stat = small[at_q + heads : at_q + heads + 1, :]
    count = stat[:, 0:1]
    squares = jnp.concatenate([stat[:, 1:2] / count, stat[:, 2:3] / (count * lat)], 1)
    rms[...] = jnp.sqrt(squares)
    for copy in copies:
        copy.wait()


def on_device(
    latent_in, actions, task_ids, valid, action_mask, bins, fraction, latent_cot,
    w_in, b_in, g_in, beta_in, w_mid, b_mid, g_mid, beta_mid,
    w_dyn_out, b_dyn_out, g_dyn_out, beta_dyn_out, w_q_out, b_q_out, table,
):
    steps = lax.axis_size("section")
    spread = lax.axis_size("dp")
    groups = spread // PEERS
    rows, lat = latent_in.shape
    act_width = actions.shape[2]
    in_width, hid = w_in.shape[2:]
    heads = w_q_out.shape[1]
    bin_count = w_q_out.shape[-1]
    tasks, emb = table.shape
    block = in_width + VECS + hid + padded(bin_count)
    block0 = in_width + VECS + hid + lat
    chunks = rows // CHUNK
    small_rows = padded(tasks + 3 * (lat // LANES) + heads + 1)
    dims = (rows, lat, act_width, in_width, hid, heads, bin_count, tasks, emb, steps)
    anywhere = pl.BlockSpec(memory_space=pl.ANY)
    vmem = pl.BlockSpec(memory_space=pltpu.VMEM)
    hbm = pl.BlockSpec(memory_space=pltpu.HBM)
    dma = pltpu.SemaphoreType.DMA
    both = 2 * rows
    wide = pltpu.VMEM((rows, hid), B16)
    thin = pltpu.VMEM((rows, LANES), F32)
    low = pltpu.VMEM((rows, lat), B16)
    part_low = pltpu.VMEM((QROWS, hid), B16)
    q_wide = pltpu.VMEM((both, hid), B16)
    lat_out, grad_out, recv_q, recv_0, small = pl.pallas_call(
        functools.partial(step_kernel, dims),
        out_shape=[
            jax.ShapeDtypeStruct((rows, lat), B16),
            jax.ShapeDtypeStruct((rows, lat), F32),
            jax.ShapeDtypeStruct((heads, 2, block, LANES), B16),
            jax.ShapeDtypeStruct((block0, LANES), B16),
            jax.ShapeDtypeStruct((small_rows, LANES), F32),
        ],
        in_specs=[anywhere] + [vmem] * 7 + [anywhere] * 5 + [vmem] * 10,
        out_specs=[anywhere] * 5,
        scratch_shapes=[
            pltpu.VMEM((both, 6 * LANES), B16),
            pltpu.VMEM((both, LANES), F32),
            pltpu.VMEM((2, in_width + VECS, hid), B16),
            pltpu.VMEM((2, hid, hid), B16),
            pltpu.VMEM((2, LANES, hid), B16),
            pltpu.VMEM((2, bin_count, hid), B16),
            pltpu.VMEM((in_width + VECS, hid), B16),
            pltpu.VMEM((hid, hid), B16),
            pltpu.VMEM((hid, lat), B16),
            pltpu.VMEM((6, 8, hid), F32),
            pltpu.VMEM((8, LANES), F32),
            pltpu.VMEM((2 * LANES, 2 * LANES), B16),
            pltpu.VMEM((2, 8, rows), F32),
            pltpu.VMEM((2, act_width, rows), B16),
            pltpu.VMEM((VECS, hid), F32),
            pltpu.VMEM((both, in_width), F32),
            q_wide, q_wide, q_wide, q_wide,
            pltpu.VMEM((both, LANES), B16),
            part_low, part_low, part_low, part_low,
            pltpu.VMEM((QROWS, LANES), F32),
            pltpu.VMEM((QROWS, hid), F32),
            wide, wide, wide, wide, wide, wide, wide, wide, thin,
            low,
            pltpu.VMEM((rows, lat), F32),
            low, low, low, low, low,
            pltpu.VMEM((2, CHIPS, block0, LANES), B16),
            pltpu.VMEM((3, CHIPS, block, LANES), B16),
            pltpu.VMEM((CHIPS, block0, LANES), B16),
            pltpu.VMEM((2, 32, hid), F32),
            pltpu.VMEM((3, 8, LANES), F32),
            pltpu.VMEM((24, lat), F32),
            pltpu.VMEM((16, lat), F32),
            pltpu.VMEM((small_rows, LANES), F32),
            pltpu.VMEM((small_rows, LANES), F32),
            pltpu.VMEM((CHIPS, small_rows // 2, LANES), F32),
            pltpu.VMEM((small_rows // 2, LANES), F32),
            pltpu.VMEM((steps, small_rows // 2, LANES), F32),
            pltpu.VMEM((small_rows, LANES), F32),
            dma((10,)), dma((chunks,)), dma((2 * chunks + 1,)),
            dma((chunks,)), dma((chunks,)), dma((chunks,)), dma((chunks,)),
            dma((2,)), dma((2,)), dma((chunks,)), dma((chunks,)), dma((chunks,)), dma((chunks,)),
            dma((4, CHIPS)), dma((4, CHIPS)), dma((4,)), dma((3, CHIPS)), dma((heads, 2)),
            dma((2,)), dma((2,)), dma((CHIPS,)), dma((CHIPS,)), dma((steps,)), dma((steps,)),
            dma((CHIPS, 3)), dma((CHIPS, 3)), dma((CHIPS, 3)), dma((CHIPS, 3)),
            pltpu.SemaphoreType.REGULAR, pltpu.SemaphoreType.REGULAR,
        ],
        compiler_params=pltpu.CompilerParams(
            collective_id=0, has_side_effects=True, vmem_limit_bytes=16350 * 2**12
        ),
        name="step",
    )(
        latent_in, actions[0].T, task_ids[None], valid[None], bins, fraction,
        action_mask.T, table, latent_cot[0],
        w_in[0], w_mid[0], w_dyn_out[0], w_q_out[0].transpose(0, 2, 1),
        b_in[0], g_in[0], beta_in[0], b_mid[0], g_mid[0], beta_mid[0],
        b_dyn_out, g_dyn_out, beta_dyn_out, b_q_out[0],
    )
    across = [[q * PEERS + r for q in range(groups)] for r in range(PEERS)]
    if groups > 1:
        small = lax.psum(small, "dp", axis_index_groups=across)

    def shape(*dims):
        return jax.ShapeDtypeStruct(dims, F32)

    lat_out, grad_out, part_in, part_mid, part_dyn, part_q, b_dyn, g_dyn, s_dyn, q_bias, grad_table, rms, *vecs = (
        pl.pallas_call(
            functools.partial(finish_kernel, (lat, in_width, hid, heads, bin_count, tasks, emb)),
            out_shape=[
                jax.ShapeDtypeStruct((rows, lat), B16),
                shape(rows, lat),
                shape(heads + 1, in_width, LANES),
                shape(heads + 1, hid, LANES),
                shape(LANES, lat),
                shape(heads, bin_count, 1, LANES),
                shape(1, lat), shape(1, lat), shape(1, lat),
                shape(heads, 1, bin_count),
                shape(tasks, emb),
                shape(1, 2),
            ] + [shape(heads + 1, 1, LANES)] * 6,
            in_specs=[hbm] * 5,
            out_specs=[hbm] * 4 + [vmem] * 14,
            scratch_shapes=[
                pltpu.VMEM((heads, 2, block, LANES), B16),
                pltpu.VMEM((block0, LANES), B16),
                pltpu.VMEM((small_rows, LANES), F32),
                pltpu.VMEM((heads + 1, in_width, LANES), F32),
                pltpu.VMEM((heads + 1, hid, LANES), F32),
                pltpu.VMEM((rows, lat), B16),
                pltpu.VMEM((rows, lat), F32),
                dma((heads + 4,)),
                dma((2 * heads + 4,)),
            ],
            compiler_params=pltpu.CompilerParams(vmem_limit_bytes=60 * 2**20),
            name="finish",
        )(recv_q, recv_0, small, lat_out, grad_out)
    )

    def owned(piece, dim):
        if groups == 1:
            return piece
        piece = lax.psum_scatter(piece, "dp", scatter_dimension=dim, axis_index_groups=across, tiled=True)
        moves = [(q * PEERS + r, r * groups + q) for q in range(groups) for r in range(PEERS)]
        return lax.ppermute(piece, "dp", moves)

    part_in, part_mid, part_q = owned(part_in, 2), owned(part_mid, 2), owned(part_q, 3)
    part_dyn = owned(part_dyn, 0)
    vecs = [owned(v, 2).transpose(1, 0, 2) for v in vecs]
    return (
        lat_out[None],
        grad_out[None],
        part_in[None],
        *vecs[:3],
        part_mid[None],
        *vecs[3:],
        part_dyn[None],
        b_dyn,
        g_dyn,
        s_dyn,
        part_q.transpose(2, 0, 3, 1),
        q_bias.transpose(1, 0, 2),
        grad_table,
        rms,
    )


def solution(mesh):
    placed = (
        P("dp", None),
        P("section", "dp", None),
        P("dp"),
        P("dp"),
        P(),
        P("section", "dp"),
        P("section", "dp"),
        P("section", "dp", None),
        P("section", None, None, None),
        P("section", None, None),
        P("section", None, None),
        P("section", None, None),
        P("section", None, None, None),
        P("section", None, None),
        P("section", None, None),
        P("section", None, None),
        P("section", None, None),
        P("section", None),
        P("section", None),
        P("section", None),
        P("section", None, None, None),
        P("section", None, None),
        P(),
    )
    return jax.shard_map(
        on_device,
        mesh=mesh,
        in_specs=placed,
        out_specs=(
            P("section", "dp", None),
            P("section", "dp", None),
            P("section", None, None, "dp"),
            P("section", None, "dp"),
            P("section", None, "dp"),
            P("section", None, "dp"),
            P("section", None, None, "dp"),
            P("section", None, "dp"),
            P("section", None, "dp"),
            P("section", None, "dp"),
            P("section", "dp", None),
            P("section", None),
            P("section", None),
            P("section", None),
            P("section", None, "dp", None),
            P("section", None, None),
            P(),
            P("section", None),
        ),
        check_vma=False,
    )
```
